256 devices in a mesh: head: 4 (over y_hi, core), seq: 32 (over z, x), mp: 2 (over y_lo).
Axes of the slice: x: 4, y: 4 (y_hi: 2, y_lo: 2; y = y_hi * 2 + y_lo), z: 8, core: 2. Of those that a mesh axis runs over, the one named last changes fastest.
Arguments:
- hidden_states: bfloat16 [12288, 2048], P('seq', ('head', 'mp'))
- norm_gain: bfloat16 [4, 2048], P('head'), may hold values from 0.25 to 1.75
- qkv_weight: bfloat16 [4, 2048, 3, 1024], P('head', 'seq', None, 'mp')
- out_weight: bfloat16 [4, 2048, 1024], P('head', 'seq', 'mp'), may hold values from -0.1875 to 0.1875
- cotangent: bfloat16 [4, 12288, 2048], P('head', 'seq'), may hold values from -1.5 to 1.5
- segment_ids: int32 [12288], replicated, may hold values from 0 to 63, as said below
Outputs:
- trunk_grad: bfloat16 [12288, 2048], P('seq', ('head', 'mp'))
- qkv_grad: bfloat16 [4, 2048, 3, 1024], P('head', 'seq', None, 'mp')
- out_grad: bfloat16 [4, 2048, 1024], P('head', 'seq', 'mp')
The draws below stay inside these ranges and needn't reach their ends.
Inputs may be any that keep to these rules, and one draw needn't show every extreme that they name: `segment_ids`: numbers never fall along the window; each document holds 1 to 384 positions and some document holds exactly 384.
All inputs are finite; a program needn't handle non-finite values.
Results may differ from the reference program's by a relative error of at most 0.022.
Values may be sent and summed in bfloat16 or wider, within the bound.
A program may use at most 128 MiB of HBM per device.

```python
import jax
import jax.numpy as jnp
from jax import lax

D = 2048
HEADS = 16
HD = 64
TOK_DEV = 384
INNER = 1024
TOKENS = 12288
MTP = 4


def draw_hidden_states(key, part):
    key = jax.random.fold_in(key, 11)
    base_key = jax.random.fold_in(key, 0)
    values = jnp.clip(jax.random.normal(base_key, (TOKENS, D), jnp.float32), -6.0, 6.0)
    return values.astype(jnp.bfloat16)


def draw_qkv_weight(key, part):
    key = jax.random.fold_in(key, 23)
    base_key = jax.random.fold_in(key, 0)
    base = jnp.clip(jax.random.normal(base_key, (MTP, D, 3, INNER), jnp.float32), -4.0, 4.0) * D ** (-0.5)
    values = base
    return values.astype(jnp.bfloat16)


def draw_segment_ids(key, part):
    key = jax.random.fold_in(key, 37)
    offset_key, place_key = jax.random.split(key, 2)
    blocks = TOKENS // TOK_DEV
    half = TOK_DEV // 2
    offsets = jax.random.randint(offset_key, (blocks,), 1, half, jnp.int32)
    chosen = jax.random.randint(place_key, (), 1, blocks, jnp.int32)
    block_index = jnp.arange(blocks, dtype=jnp.int32)
    offsets = jnp.where(block_index == chosen - 1, 0, jnp.where(block_index == chosen, half, offsets))
    starts = block_index * TOK_DEV + offsets
    first_cut = jnp.where(block_index == 0, TOKENS + 1, starts)
    second_cut = starts + half
    cuts = jnp.concatenate([first_cut, second_cut])
    positions = jnp.arange(TOKENS, dtype=jnp.int32)
    counts = jnp.sum((positions[:, None] >= cuts[None, :]).astype(jnp.int32), axis=1)
    return counts.astype(jnp.int32)


def block_scale(key, extent, shards, low, largest):
    def one(position, blocks):
        draws = jax.random.uniform(jax.random.fold_in(jax.random.fold_in(key, 6), position), (blocks,), jnp.float32, low / len(shards), largest / len(shards))
        return jnp.repeat(jnp.exp(draws), extent[position] // blocks).reshape((-1,) + (1,) * (len(extent) - position - 1))

    level = one(*shards[0])
    for cut in shards[1:]:
        level = level * one(*cut)
    return level


def gaussian(stream_key, shape, spread, reach, cuts=(), kind=jnp.bfloat16):
    result = spread * jax.random.normal(stream_key, shape, jnp.float32)
    if cuts:
        result = result * block_scale(stream_key, shape, cuts, -0.22, 0.18)
    return jnp.clip(result, -reach, reach).astype(kind)


def setup_inputs(seed: int = 0) -> dict:
    key_list = jax.random.split(jax.random.key(seed), 7)
    return {
        "hidden_states": draw_hidden_states(jax.random.fold_in(key_list[6], 71), 0),
        "norm_gain": jnp.clip(1.0 + 0.15 * jax.random.normal(key_list[1], (MTP, D), jnp.float32), 0.25, 1.75).astype(jnp.bfloat16),
        "qkv_weight": draw_qkv_weight(jax.random.fold_in(key_list[6], 71), 0),
        "out_weight": gaussian(key_list[3], (MTP, D, INNER), INNER ** -0.5, 0.1875, ((0, 4), (1, 32), (2, 2))),
        "cotangent": gaussian(key_list[4], (MTP, TOKENS, D), 0.25, 1.5, ((0, 4), (1, 32))),
        "segment_ids": draw_segment_ids(jax.random.fold_in(key_list[6], 71), 0),
    }


epsilon = 1e-05
masked_score = -1e+30

def block_mask(own_seg, earlier_seg):
    row_count = own_seg.shape[0]
    positions = jnp.arange(row_count)
    causal = positions[None, :] <= positions[:, None]
    own_ok = causal & (own_seg[None, :] == own_seg[:, None])
    prior_ok = earlier_seg[None, :] == own_seg[:, None]
    return jnp.concatenate([prior_ok, own_ok], axis=1)

def attend(queries, key_rows, value_rows, allowed, attn_grad):
    score_scale = HD ** (-0.5)
    queries_f = queries.astype(jnp.float32)
    keys_f = key_rows.astype(jnp.float32)
    values_f = value_rows.astype(jnp.float32)
    grad_f = attn_grad.astype(jnp.float32)
    scores = jnp.einsum('qhd,khd->hqk', queries_f, keys_f) * score_scale
    scores = jnp.where(allowed[None], scores, masked_score)
    row_max = lax.optimization_barrier(jnp.max(scores, axis=-1, keepdims=True))
    expo = jnp.exp(scores - row_max)
    probs = expo / lax.optimization_barrier(jnp.sum(expo, axis=-1, keepdims=True))
    prob_rows = probs.astype(jnp.bfloat16).astype(jnp.float32)
    attn_out = jnp.einsum('hqk,khd->qhd', prob_rows, values_f).astype(jnp.bfloat16)
    prob_grad = jnp.einsum('qhd,khd->hqk', grad_f, values_f)
    row_delta = lax.optimization_barrier(jnp.sum(probs * prob_grad, axis=-1, keepdims=True))
    score_grad = (probs * (prob_grad - row_delta) * score_scale).astype(jnp.bfloat16).astype(jnp.float32)
    query_grad = jnp.einsum('hqk,khd->qhd', score_grad, keys_f).astype(jnp.bfloat16)
    key_grads = jnp.einsum('hqk,qhd->khd', score_grad, queries_f)
    value_grads = jnp.einsum('hqk,qhd->khd', prob_rows, grad_f)
    return (attn_out, query_grad, key_grads, value_grads)

def block_pass(pieces):
    queries, prior_keys, prior_values, private_lookup_vectors, own_values, prior_seg, own_seg, attn_grad = pieces
    key_rows = jnp.concatenate([prior_keys, private_lookup_vectors], axis=0)
    value_rows = jnp.concatenate([prior_values, own_values], axis=0)
    allowed = block_mask(own_seg, prior_seg)
    return attend(queries, key_rows, value_rows, allowed, attn_grad)

def reference(hidden_states, norm_gain, qkv_weight, out_weight, cotangent, segment_ids):
    states = hidden_states.astype(jnp.float32)
    inverse = lax.rsqrt(lax.optimization_barrier(jnp.mean(states * states, axis=-1, keepdims=True)) + epsilon)
    unit_rows = states * inverse
    blocks = TOKENS // TOK_DEV
    filler = jnp.full((TOK_DEV,), -1, jnp.int32)
    own_segs = segment_ids.astype(jnp.int32).reshape(blocks, TOK_DEV)
    prior_segs = jnp.concatenate([filler, segment_ids.astype(jnp.int32)[:-TOK_DEV]]).reshape(blocks, TOK_DEV)
    total = jnp.zeros((TOKENS, D), jnp.float32)
    qkv_grads = []
    out_grads = []

    def split_heads(array):
        return array.reshape(blocks, TOK_DEV, HEADS, HD)
    for group in range(MTP):
        norm_scale = norm_gain[group].astype(jnp.float32)
        rescaled_hidden = (unit_rows * norm_scale).astype(jnp.bfloat16)
        triple_mapping_matrix = qkv_weight[group].astype(jnp.float32)
        weight_out = out_weight[group].astype(jnp.float32)
        mapped_triple = jnp.einsum('gl,lru->gru', rescaled_hidden.astype(jnp.float32), triple_mapping_matrix).astype(jnp.bfloat16)
        upstream = cotangent[group]
        attn_grad = jnp.einsum('td,de->te', upstream.astype(jnp.float32), weight_out).astype(jnp.bfloat16)
        zero_block = jnp.zeros((TOK_DEV, INNER), jnp.bfloat16)
        key_all = mapped_triple[:, 1]
        value_all = mapped_triple[:, 2]
        prior_keys = jnp.concatenate([zero_block, key_all[:-TOK_DEV]], axis=0)
        prior_values = jnp.concatenate([zero_block, value_all[:-TOK_DEV]], axis=0)
        attn_out, query_grad, key_grads, value_grads = lax.map(block_pass, (split_heads(mapped_triple[:, 0]), split_heads(prior_keys), split_heads(prior_values), split_heads(key_all), split_heads(value_all), prior_segs, own_segs, split_heads(attn_grad)))
        zero_grad = jnp.zeros((1, TOK_DEV, HEADS, HD), jnp.float32)
        key_total = key_grads[:, TOK_DEV:] + jnp.concatenate([key_grads[1:, :TOK_DEV], zero_grad], axis=0)
        value_total = value_grads[:, TOK_DEV:] + jnp.concatenate([value_grads[1:, :TOK_DEV], zero_grad], axis=0)
        triple_matrix_sensitivity = jnp.stack([query_grad.reshape(TOKENS, INNER), key_total.reshape(TOKENS, INNER).astype(jnp.bfloat16), value_total.reshape(TOKENS, INNER).astype(jnp.bfloat16)], axis=1)
        attn_flat = attn_out.reshape(TOKENS, INNER)

        def accumulate(carry, pieces):
            normed_block, grad_block, upstream_block, attn_block = pieces
            qkv_term = jnp.einsum('tc,tse->cse', normed_block.astype(jnp.float32), grad_block.astype(jnp.float32))
            out_term = jnp.einsum('tc,te->ce', upstream_block.astype(jnp.float32), attn_block.astype(jnp.float32))
            qkv_term = lax.optimization_barrier(qkv_term.astype(jnp.bfloat16)).astype(jnp.float32)
            out_term = lax.optimization_barrier(out_term.astype(jnp.bfloat16)).astype(jnp.float32)
            return ((carry[0] + qkv_term, carry[1] + out_term), None)
        start_carry = (jnp.zeros((D, 3, INNER), jnp.float32), jnp.zeros((D, INNER), jnp.float32))
        (qkv_sum, out_sum), unused = lax.scan(accumulate, start_carry, (rescaled_hidden.reshape(blocks, TOK_DEV, D), triple_matrix_sensitivity.reshape(blocks, TOK_DEV, 3, INNER), upstream.reshape(blocks, TOK_DEV, D), attn_flat.reshape(blocks, TOK_DEV, INNER)))
        qkv_grads.append(qkv_sum.astype(jnp.bfloat16))
        out_grads.append(out_sum.astype(jnp.bfloat16))
        rescaled_hidden_sensitivity = jnp.einsum('byq,xyq->bx', triple_matrix_sensitivity.astype(jnp.float32), triple_mapping_matrix)
        scaled = rescaled_hidden_sensitivity * norm_scale
        state_grad = inverse * (scaled - unit_rows * lax.optimization_barrier(jnp.mean(scaled * unit_rows, axis=-1, keepdims=True)))
        total = total + state_grad + upstream.astype(jnp.float32)
    return (total.astype(jnp.bfloat16), jnp.stack(qkv_grads), jnp.stack(out_grads))
```

```python
import functools

import jax
import jax.numpy as jnp
from jax import lax
from jax.experimental import pallas as pl
from jax.experimental.pallas import tpu as pltpu
from jax.sharding import PartitionSpec as P

HD = 64
EPS = 1e-05
MASKED = -1e30
MESH = pl.DeviceIdType.MESH
VMEM_LIMIT = 56 * 1024 * 1024
BF = jnp.bfloat16
F32 = jnp.float32


def places():
    head, seq, mp = (lax.axis_index(name) for name in ("head", "seq", "mp"))
    z, x = seq // 4, seq % 4
    odd = x % 2
    info = {
        "head": head,
        "mp": mp,
        "z": z,
        "x": x,
        "odd": odd,
        "pair": x // 2,
        "quarter": ((x + 1) // 2) % 2,
        "core": head % 2,
        "hi": head // 2,
        "e1": (head, seq + 1 - 2 * odd, mp),
        "e2": (head, z * 4 + 3 - x, mp),
        "zp": (head, ((z + 1) % 8) * 4 + x, mp),
        "zm": (head, ((z + 7) % 8) * 4 + x, mp),
        "near": (head, seq, 1 - mp),
        "far": ((head + 2) % 4, seq, 1 - mp),
        "twin": (head + 1 - 2 * (head % 2), seq, mp),
        "halo": (head, (seq + 31 + 2 * odd) % 32, mp),
    }
    return info


def greet(info):
    barrier = pltpu.get_barrier_semaphore()
    names = ("e1", "e2", "zp", "zm", "near", "far", "twin", "halo")
    for name in names:
        pl.semaphore_signal(barrier, inc=1, device_id=info[name], device_id_type=MESH)
    pl.semaphore_wait(barrier, len(names))


class Wires:
    def __init__(self, send, recv):
        self.send, self.recv, self.count = send, recv, 0
        self.started = []

    def slot(self):
        self.count += 1
        return self.count - 1

    def put(self, slot, src, dst, device):
        copy = pltpu.make_async_remote_copy(
            src_ref=src,
            dst_ref=dst,
            send_sem=self.send.at[slot],
            recv_sem=self.recv.at[slot],
            device_id=device,
            device_id_type=MESH,
        )
        copy.start()
        self.started.append((slot, src))

    def got(self, slot, dst):
        pltpu.make_async_copy(dst, dst, self.recv.at[slot]).wait()

    def finish(self):
        for slot, src in self.started:
            pltpu.make_async_copy(src, src, self.send.at[slot]).wait()


GATHER_SLOTS = 80


def gather_kernel(hid, ws, cot, h_out, w_out, c_out, send, recv, local):
    info = places()
    z, x, odd, p, q = (info[name] for name in ("z", "x", "odd", "pair", "quarter"))
    mp, core, hi = info["mp"], info["core"], info["hi"]
    wires = Wires(send, recv)

    own_w = pltpu.make_async_copy(ws.at[q], w_out.at[:, z, x], local.at[0])
    own_w.start()
    own_c = pltpu.make_async_copy(cot, c_out.at[odd], local.at[1])
    piece = (info["head"] * 2 + mp) * 256
    b = 1 + odd
    blocks = (b, 3 - b, 0)

    def cols(block, head_hi, head_core, part):
        start = pl.multiple_of(((head_hi * 2 + head_core) * 2 + part) * 256, 256)
        return h_out.at[block, :, pl.ds(start, 256)]

    own_h = pltpu.make_async_copy(hid, cols(b, hi, core, mp), local.at[2])
    own_h.start()
    own_c.start()

    greet(info)

    w_e1 = [wires.slot() for _ in range(2)]
    for half in range(2):
        arrs = pl.ds(2 * half, 2)
        wires.put(w_e1[half], ws.at[1 - q, arrs], w_out.at[arrs, z, x], info["e1"])
    h_e1, h_halo = wires.slot(), wires.slot()
    h_near = [wires.slot() for _ in range(3)]
    h_far = [wires.slot() for _ in range(3)]
    h_opp = [wires.slot() for _ in range(3)]
    h_twin = [[wires.slot() for _ in range(4)] for _ in range(3)]
    mine = cols(b, hi, core, mp)
    wires.put(h_e1, hid, mine, info["e1"])
    halo_own = cols(0, hi, core, mp)

    @pl.when(odd == 1)
    def _():
        pltpu.make_async_remote_copy(
            src_ref=hid,
            dst_ref=halo_own,
            send_sem=send.at[h_halo],
            recv_sem=recv.at[h_halo],
            device_id=info["halo"],
            device_id_type=MESH,
        ).start()

    def spread(r, src):
        dst = cols(blocks[r], hi, core, mp)
        wires.put(h_near[r], src, dst, info["near"])
        wires.put(h_far[r], src, dst, info["far"])
        wires.put(h_twin[r][0], src, dst, info["twin"])

    def from_near(r):
        got = cols(blocks[r], hi, core, 1 - mp)
        wires.got(h_near[r], got)
        wires.put(h_opp[r], got, got, info["far"])
        wires.put(h_twin[r][1], got, got, info["twin"])

    def from_far(r):
        got = cols(blocks[r], 1 - hi, core, 1 - mp)
        wires.got(h_far[r], got)
        wires.put(h_twin[r][2], got, got, info["twin"])

    def from_opp(r):
        got = cols(blocks[r], 1 - hi, core, mp)
        wires.got(h_opp[r], got)
        wires.put(h_twin[r][3], got, got, info["twin"])

    def from_twin(r):
        other = 1 - core
        wires.got(h_twin[r][0], cols(blocks[r], hi, other, mp))
        wires.got(h_twin[r][1], cols(blocks[r], hi, other, 1 - mp))
        wires.got(h_twin[r][2], cols(blocks[r], 1 - hi, other, 1 - mp))
        wires.got(h_twin[r][3], cols(blocks[r], 1 - hi, other, mp))

    spread(0, hid)

    def own_pair(first, count, layer):
        return w_out.at[pl.ds(first, count), layer, pl.ds(2 * p, 2)]

    def other_pair(first, count, layer):
        return w_out.at[pl.ds(first, count), layer, pl.ds(2 - 2 * p, 2)]

    a_own = [[wires.slot() for _ in range(4)] for _ in range(2)]
    a_oth = [[wires.slot() for _ in range(4)] for _ in range(2)]
    b_own = [[wires.slot() for _ in range(4)] for _ in range(2)]
    a_e2 = wires.slot()
    b_e2 = [wires.slot()] + [wires.slot() for _ in range(8)]
    ways = ("zp", "zm")

    def span(way, hop, first):
        return (first, 2) if hop < 4 else (first + way, 1)

    def layer_from(way, hop):
        return (z + 8 - hop) % 8 if way == 0 else (z + hop) % 8

    def pass_on(slots, part, first, way, hop):
        lo, count = span(way, hop + 1, first)
        ref = part(lo, count, layer_from(way, hop))
        wires.put(slots[way][hop], ref, ref, info[ways[way]])

    def take(slots, part, first, way, hop):
        lo, count = span(way, hop, first)
        ref = part(lo, count, layer_from(way, hop))
        wires.got(slots[way][hop - 1], ref)
        return ref

    own_w.wait()
    wires.got(w_e1[0], w_out.at[pl.ds(0, 2), z, x + 1 - 2 * odd])
    for way in range(2):
        pass_on(a_own, own_pair, 0, way, 0)
    ref = own_pair(0, 2, z)
    wires.put(a_e2, ref, ref, info["e2"])
    wires.got(w_e1[1], w_out.at[pl.ds(2, 2), z, x + 1 - 2 * odd])
    for way in range(2):
        pass_on(b_own, own_pair, 2, way, 0)
    ref = own_pair(2, 2, z)
    wires.put(b_e2[0], ref, ref, info["e2"])

    rows = 48
    c_e1 = [wires.slot() for _ in range(4)]
    c_near = [wires.slot() for _ in range(4)]

    def c_rows(block, part, k):
        return c_out.at[block, pl.ds(pl.multiple_of(part * 192 + k * rows, rows), rows)]

    for k in range(4):
        src = cot.at[pl.ds(pl.multiple_of(mp * 192 + k * rows, rows), rows)]
        wires.put(c_e1[k], src, c_rows(odd, mp, k), info["e1"])

    def c_step(k):
        ref = c_rows(1 - odd, mp, k)
        wires.got(c_e1[k], ref)
        wires.put(c_near[k], ref, ref, info["near"])

    wires.got(h_e1, cols(3 - b, hi, core, mp))
    spread(1, cols(3 - b, hi, core, mp))

    wires.got(a_e2, other_pair(0, 2, z))
    for way in range(2):
        pass_on(a_oth, other_pair, 0, way, 0)
    from_near(0)
    wires.got(h_halo, halo_own)

    @pl.when(odd == 0)
    def _():
        pltpu.make_async_remote_copy(
            src_ref=halo_own,
            dst_ref=halo_own,
            send_sem=send.at[h_halo],
            recv_sem=recv.at[h_halo],
            device_id=info["e1"],
            device_id_type=MESH,
        ).start()

    wires.started.append((h_halo, hid))
    spread(2, halo_own)

    count = 1
    for hop in range(1, 5):
        for way in range(2):
            take(a_own, own_pair, 0, way, hop)
            if hop < 4:
                pass_on(a_own, own_pair, 0, way, hop)
        for way in range(2):
            ref = take(b_own, own_pair, 2, way, hop)
            if hop < 4:
                pass_on(b_own, own_pair, 2, way, hop)
            wires.put(b_e2[count], ref, ref, info["e2"])
            count += 1
        if hop < 4:
            from_far(hop - 1)
            from_near(hop) if hop < 3 else None
        c_step(hop - 1)
        for way in range(2):
            take(a_oth, other_pair, 0, way, hop)
            if hop < 4:
                pass_on(a_oth, other_pair, 0, way, hop)
        if hop < 4:
            from_opp(hop - 1)

    wires.got(b_e2[0], other_pair(2, 2, z))
    count = 1
    for hop in range(1, 5):
        for way in range(2):
            lo, width = span(way, hop, 2)
            wires.got(b_e2[count], other_pair(lo, width, layer_from(way, hop)))
            count += 1
    for r in range(3):
        from_twin(r)
    for k in range(4):
        wires.got(c_near[k], c_rows(1 - odd, 1 - mp, k))
    own_h.wait()
    own_c.wait()
    wires.finish()


def gather(hid, ws, cot):
    anywhere = pl.BlockSpec(memory_space=pl.ANY)
    return pl.pallas_call(
        gather_kernel,
        out_shape=(
            jax.ShapeDtypeStruct((3, 384, 2048), BF),
            jax.ShapeDtypeStruct((4, 8, 4, 64, 256), BF),
            jax.ShapeDtypeStruct((2, 384, 2048), BF),
        ),
        in_specs=[anywhere] * 3,
        out_specs=(anywhere,) * 3,
        scratch_shapes=[
            pltpu.SemaphoreType.DMA((GATHER_SLOTS,)),
            pltpu.SemaphoreType.DMA((GATHER_SLOTS,)),
            pltpu.SemaphoreType.DMA((3,)),
        ],
        compiler_params=pltpu.CompilerParams(
            collective_id=0, has_side_effects=True, vmem_limit_bytes=VMEM_LIMIT
        ),
        name="gather",
    )(hid, ws, cot)


REDUCE_SLOTS = 64


def add(*terms):
    total = terms[0].astype(F32)
    for term in terms[1:]:
        total = total + term.astype(F32)
    return total.astype(BF)


def reduce_kernel(
    grads, trunk, w_res, t_res,
    a_got, a_out, b_e2got, b_got, b_out, a_fin, a_e2got, w_pair,
    t_twin, t_sum, t_far, t_mid, t_near, t_fin, t_e1, t_halo, t_pass,
    send, recv, local,
):
    info = places()
    z, x, odd, p, q = (info[name] for name in ("z", "x", "odd", "pair", "quarter"))
    mp, core, hi = info["mp"], info["core"], info["hi"]
    wires = Wires(send, recv)
    ways = ("zp", "zm")
    a_slot = [[wires.slot() for _ in range(4)] for _ in range(2)]
    b_slot = [[wires.slot() for _ in range(4)] for _ in range(2)]
    b_e2 = [wires.slot() for _ in range(8)]
    a_e2 = wires.slot()
    w_e1 = [wires.slot() for _ in range(2)]
    s_twin = [[wires.slot() for _ in range(2)] for _ in range(3)]
    s_far = [wires.slot() for _ in range(3)]
    s_near = [wires.slot() for _ in range(3)]
    s_e1 = wires.slot()
    s_half = wires.slot()
    s_halo = wires.slot()
    blocks = (0, 2 - odd, 1 + odd)
    half = 512

    greet(info)

    def to_layer(way, left):
        return (z + left) % 8 if way == 0 else (z + 8 - left) % 8

    for way in range(2):
        wires.put(
            a_slot[way][0],
            grads.at[pl.ds(way, 1), to_layer(way, 4)],
            a_got.at[way, 0, pl.ds(way, 1)],
            info[ways[way]],
        )
    order = [(0, 4), (0, 3), (1, 3), (0, 2), (1, 2), (0, 1), (1, 1), (0, 0)]
    for k, (way, left) in enumerate(order):
        wires.put(
            b_e2[k],
            grads.at[pl.ds(2, 2), to_layer(way, left), pl.ds(2 - 2 * p, 2)],
            b_e2got.at[k],
            info["e2"],
        )

    def columns(side, head_core):
        return pl.ds(pl.multiple_of(side * 1024 + head_core * half, half), half)

    for r in range(3):
        for side in range(2):
            wires.put(
                s_twin[r][side],
                trunk.at[blocks[r], :, columns(side, 1 - core)],
                t_twin.at[r, side],
                info["twin"],
            )

    def fold_twin(r):
        for side in (0, 1):
            wires.got(s_twin[r][side], t_twin.at[r, side])
            t_sum[r, side] = add(
                trunk[blocks[r], :, columns(side, core)], t_twin[r, side]
            )
        wires.put(s_far[r], t_sum.at[r, 1 - hi], t_far.at[r], info["far"])

    def fold_far(r):
        wires.got(s_far[r], t_far.at[r])
        for part in range(2):
            lanes = pl.ds(part * 256, 256)
            t_mid[r, part] = add(t_sum[r, hi, :, lanes], t_far[r, :, lanes])
        wires.put(s_near[r], t_mid.at[r, 1 - mp], t_near.at[r], info["near"])

    def fold_near(r):
        wires.got(s_near[r], t_near.at[r])
        t_fin[r] = add(t_mid[r, mp], t_near[r])

    def b_start(way, left, k):
        layer = to_layer(way, left)
        return add(grads[pl.ds(2, 2), layer, pl.ds(2 * p, 2)], b_e2got[k])

    def a_step(way, step):
        arrived = a_got.at[way, step - 1]
        layer = to_layer(way, 4 - step)
        if step == 1:
            wires.got(a_slot[way][0], a_got.at[way, 0, pl.ds(way, 1)])
            a_out[way, step, way] = add(grads[way, layer], a_got[way, 0, way])
            a_out[way, step, 1 - way] = grads[1 - way, layer]
        else:
            wires.got(a_slot[way][step - 1], arrived)
            a_out[way, step] = add(grads[pl.ds(0, 2), layer], a_got[way, step - 1])
        wires.put(a_slot[way][step], a_out.at[way, step], a_got.at[way, step], info[ways[way]])

    def b_step(way, step):
        k = {1: 1 + way, 2: 3 + way, 3: 5 + way}[step]
        wires.got(b_e2[k], b_e2got.at[k])
        mine = b_start(way, 4 - step, k)
        if step == 1:
            wires.got(b_slot[way][0], b_got.at[way, 0, pl.ds(way, 1)])
            b_out[way, step, way] = add(mine[way], b_got[way, 0, way])
            b_out[way, step, 1 - way] = mine[1 - way]
        else:
            wires.got(b_slot[way][step - 1], b_got.at[way, step - 1])
            b_out[way, step] = add(mine, b_got[way, step - 1])
        wires.put(b_slot[way][step], b_out.at[way, step], b_got.at[way, step], info[ways[way]])

    fold_twin(0)
    wires.got(b_e2[0], b_e2got.at[0])
    b_out[0, 0] = b_start(0, 4, 0)
    for way in range(2):
        wires.put(
            b_slot[way][0],
            b_out.at[0, 0, pl.ds(way, 1)],
            b_got.at[way, 0, pl.ds(way, 1)],
            info[ways[way]],
        )
    fold_twin(1)
    fold_twin(2)
    for way in range(2):
        a_step(way, 1)
    for way in range(2):
        b_step(way, 1)
    fold_far(0)
    for way in range(2):
        a_step(way, 2)
    for way in range(2):
        b_step(way, 2)
    fold_near(0)

    @pl.when(odd == 1)
    def _():
        pltpu.make_async_remote_copy(
            src_ref=t_fin.at[0],
            dst_ref=t_halo,
            send_sem=send.at[s_half],
            recv_sem=recv.at[s_half],
            device_id=info["e1"],
            device_id_type=MESH,
        ).start()

    for way in range(2):
        a_step(way, 3)
    for way in range(2):
        b_step(way, 3)
    fold_far(1)

    @pl.when(odd == 0)
    def _():
        wires.got(s_half, t_halo)
        t_pass[...] = add(t_fin[0], t_halo[...])
        pltpu.make_async_remote_copy(
            src_ref=t_pass,
            dst_ref=t_halo,
            send_sem=send.at[s_halo],
            recv_sem=recv.at[s_halo],
            device_id=info["halo"],
            device_id_type=MESH,
        ).start()

    for way in range(2):
        wires.got(a_slot[way][3], a_got.at[way, 3])
    a_fin[...] = add(grads[pl.ds(0, 2), z], a_got[0, 3], a_got[1, 3])
    wires.put(a_e2, a_fin.at[:, pl.ds(2 - 2 * p, 2)], a_e2got, info["e2"])
    fold_near(1)
    wires.put(s_e1, t_fin.at[1], t_e1, info["e1"])
    wires.got(b_e2[7], b_e2got.at[7])
    for way in range(2):
        wires.got(b_slot[way][3], b_got.at[way, 3])
    w_pair[pl.ds(2, 2)] = add(
        grads[pl.ds(2, 2), z, pl.ds(2 * p, 2)], b_e2got[7], b_got[0, 3], b_got[1, 3]
    )
    wires.put(
        w_e1[1], w_pair.at[pl.ds(2, 2), 1 - odd], w_res.at[q, pl.ds(2, 2)], info["e1"]
    )
    wires.got(a_e2, a_e2got)
    w_pair[pl.ds(0, 2)] = add(a_fin[:, pl.ds(2 * p, 2)], a_e2got[...])
    wires.put(
        w_e1[0], w_pair.at[pl.ds(0, 2), 1 - odd], w_res.at[q, pl.ds(0, 2)], info["e1"]
    )
    w_res[q] = w_pair[:, odd]
    fold_far(2)
    fold_near(2)
    wires.got(s_e1, t_e1)

    @pl.when(odd == 0)
    def _():
        t_res[...] = add(t_fin[2], t_e1[...])
        pltpu.make_async_copy(t_pass, t_pass, send.at[s_halo]).wait()

    @pl.when(odd == 1)
    def _():
        wires.got(s_halo, t_halo)
        t_res[...] = add(t_fin[2], t_e1[...], t_halo[...])
        pltpu.make_async_copy(t_halo, t_halo, send.at[s_half]).wait()

    for part in range(2):
        wires.got(w_e1[part], w_res.at[1 - q, pl.ds(2 * part, 2)])
    wires.finish()


def reduce(grads, trunk):
    in_vmem = pl.BlockSpec(memory_space=pltpu.VMEM)
    return pl.pallas_call(
        reduce_kernel,
        out_shape=(
            jax.ShapeDtypeStruct((2, 4, 64, 256), BF),
            jax.ShapeDtypeStruct((384, 256), BF),
        ),
        in_specs=[in_vmem] * 2,
        out_specs=(in_vmem,) * 2,
        scratch_shapes=[
            pltpu.VMEM((2, 4, 2, 4, 64, 256), BF),
            pltpu.VMEM((2, 4, 2, 4, 64, 256), BF),
            pltpu.VMEM((8, 2, 2, 64, 256), BF),
            pltpu.VMEM((2, 4, 2, 2, 64, 256), BF),
            pltpu.VMEM((2, 4, 2, 2, 64, 256), BF),
            pltpu.VMEM((2, 4, 64, 256), BF),
            pltpu.VMEM((2, 2, 64, 256), BF),
            pltpu.VMEM((4, 2, 64, 256), BF),
            pltpu.VMEM((3, 2, 384, 512), BF),
            pltpu.VMEM((3, 2, 384, 512), BF),
            pltpu.VMEM((3, 384, 512), BF),
            pltpu.VMEM((3, 2, 384, 256), BF),
            pltpu.VMEM((3, 384, 256), BF),
            pltpu.VMEM((3, 384, 256), BF),
            pltpu.VMEM((384, 256), BF),
            pltpu.VMEM((384, 256), BF),
            pltpu.VMEM((384, 256), BF),
            pltpu.SemaphoreType.DMA((REDUCE_SLOTS,)),
            pltpu.SemaphoreType.DMA((REDUCE_SLOTS,)),
            pltpu.SemaphoreType.DMA((1,)),
        ],
        compiler_params=pltpu.CompilerParams(
            collective_id=1, has_side_effects=True, vmem_limit_bytes=VMEM_LIMIT
        ),
        name="reduce",
    )(grads, trunk)


NT = (((1,), (1,)), ((), ()))
TN = (((0,), (0,)), ((), ()))


def attend_kernel(q_ref, k_ref, v_ref, g_ref, segk_ref, segq_ref, o_ref, dq_ref, dk_ref, dv_ref, dk_acc, dv_acc):
    scale = HD**-0.5
    dk_acc[...] = jnp.zeros_like(dk_acc)
    dv_acc[...] = jnp.zeros_like(dv_acc)
    lane_head = lax.broadcasted_iota(jnp.int32, (128, 256), 1) // HD

    def by_head(rows):
        return jnp.concatenate(
            [jnp.where(lane_head == h, rows, jnp.zeros_like(rows)) for h in range(4)], axis=0
        )

    def fold(wide):
        return jnp.concatenate(
            [wide[h * HD : (h + 1) * HD, h * 128 : (h + 1) * 128] for h in range(4)], axis=0
        ).T

    key_at = lax.broadcasted_iota(jnp.int32, (512, 128), 0)
    query_at = lax.broadcasted_iota(jnp.int32, (512, 128), 1) + 384
    causal = key_at <= query_at

    def tile(t, carry):
        start = pl.multiple_of(t * 128, 128)
        here, window = pl.ds(start, 128), pl.ds(start, 512)
        queries, grads = by_head(q_ref[here, :]), by_head(g_ref[here, :])
        keys, values = k_ref[window, :], v_ref[window, :]
        allowed = causal & (segk_ref[window, :] == segq_ref[t])
        allowed = jnp.concatenate([allowed] * 4, axis=1)
        scores = lax.dot_general(keys, queries, NT, preferred_element_type=F32) * scale
        scores = jnp.where(allowed, scores, MASKED)
        expo = jnp.exp(scores - jnp.max(scores, axis=0, keepdims=True))
        probs = expo * (1.0 / jnp.sum(expo, axis=0, keepdims=True))
        prob_rows = probs.astype(BF)
        prob_grad = lax.dot_general(values, grads, NT, preferred_element_type=F32)
        delta = jnp.sum(probs * prob_grad, axis=0, keepdims=True)
        score_grad = (probs * (prob_grad - delta) * scale).astype(BF)
        dv_acc[window, :] += jnp.dot(prob_rows, grads, preferred_element_type=F32)
        dk_acc[window, :] += jnp.dot(score_grad, queries, preferred_element_type=F32)
        o_ref[here, :] = fold(
            lax.dot_general(values, prob_rows, TN, preferred_element_type=F32)
        ).astype(BF)
        dq_ref[here, :] = fold(
            lax.dot_general(keys, score_grad, TN, preferred_element_type=F32)
        ).astype(BF)
        return carry

    lax.fori_loop(0, 6, tile, 0)
    dk_ref[...] = dk_acc[...].astype(BF)
    dv_ref[...] = dv_acc[...].astype(BF)


def attend(queries, keys, values, attn_grad, seg_keys, seg_queries):
    shapes = [(768, 256), (768, 256), (1152, 256), (1152, 256)]
    return pl.pallas_call(
        attend_kernel,
        out_shape=tuple(jax.ShapeDtypeStruct(shape, BF) for shape in shapes),
        scratch_shapes=[pltpu.VMEM((1152, 256), F32)] * 2,
        compiler_params=pltpu.CompilerParams(vmem_limit_bytes=VMEM_LIMIT),
        name="attend",
    )(queries, keys, values, attn_grad, seg_keys, seg_queries)


def per_device(hidden_states, norm_gain, qkv_weight, out_weight, cotangent, segment_ids):
    seq, mp = lax.axis_index("seq"), lax.axis_index("mp")
    odd = seq % 2
    shard = jnp.concatenate(
        [jnp.transpose(qkv_weight[0], (1, 0, 2)), out_weight], axis=0
    )
    shard = jnp.transpose(shard.reshape(4, 64, 2, 256), (2, 0, 1, 3))
    hidden, weights, upstream = gather(hidden_states, shard, cotangent[0])
    hidden = hidden.reshape(1152, 2048)
    weights = weights.reshape(4, 2048, 256)
    upstream = upstream.reshape(768, 2048)

    states = hidden.astype(F32)
    inverse = lax.rsqrt(jnp.mean(states * states, axis=-1, keepdims=True) + EPS)
    unit_rows = states * inverse
    gain = norm_gain[0].astype(F32)
    normed = (unit_rows * gain).astype(BF)

    def project(rows, weight):
        return jnp.dot(rows, weight, preferred_element_type=F32).astype(BF)

    queries = project(normed[384:], weights[0])
    keys = project(normed, weights[1])
    values = project(normed, weights[2])
    attn_grad = project(upstream, weights[3])

    first = (seq - odd) * 384 - 384
    seg = lax.dynamic_slice_in_dim(segment_ids, first + 384, 768)
    earlier = lax.dynamic_slice_in_dim(segment_ids, jnp.maximum(first, 0), 384)
    earlier = jnp.where(first >= 0, earlier, -1)
    seg_keys = jnp.concatenate([earlier, seg])[:, None]
    attn_out, dq, dk, dv = attend(
        queries, keys, values, attn_grad, seg_keys, seg.reshape(6, 1, 128)
    )

    def weight_grad(rows, grad):
        return lax.dot_general(rows, grad, TN, preferred_element_type=F32).astype(BF)

    grads = jnp.stack(
        [
            weight_grad(normed[384:], dq),
            weight_grad(normed, dk),
            weight_grad(normed, dv),
            weight_grad(upstream, attn_out),
        ]
    )

    def back(grad, weight):
        return lax.dot_general(grad, weight, NT, preferred_element_type=F32)

    scaled = (
        back(jnp.pad(dq, ((384, 0), (0, 0))), weights[0])
        + back(dk, weights[1])
        + back(dv, weights[2])
    ) * gain
    state_grad = inverse * (
        scaled - unit_rows * jnp.mean(scaled * unit_rows, axis=-1, keepdims=True)
    )
    block = jnp.arange(1152) // 384
    keep = (block == 1 + odd) & (mp == 0)
    residual = jnp.pad(upstream, ((384, 0), (0, 0))).astype(F32)
    trunk = (state_grad + jnp.where(keep[:, None], residual, 0.0)).astype(BF)

    w_res, t_res = reduce(grads.reshape(4, 8, 4, 64, 256), trunk.reshape(3, 384, 2048))
    merged = jnp.transpose(w_res, (1, 2, 0, 3)).reshape(4, 64, 512)
    return (t_res, jnp.transpose(merged[:3], (1, 0, 2))[None], merged[3][None])


def solution(mesh):
    placed = (
        P("seq", ("head", "mp")),
        P("head", None),
        P("head", "seq", None, "mp"),
        P("head", "seq", "mp"),
        P("head", "seq", None),
        P(),
    )
    return jax.shard_map(
        per_device,
        mesh=mesh,
        in_specs=placed,
        out_specs=(P("seq", ("head", "mp")), P("head", "seq", None, "mp"), P("head", "seq", "mp")),
        check_vma=False,
    )
```

```python
import functools

import jax
import jax.numpy as jnp
from jax import lax
from jax.experimental import pallas as pl
from jax.experimental.pallas import tpu as pltpu
from jax.sharding import PartitionSpec as P

HD = 64
EPS = 1e-05
MASKED = -1e30
MESH = pl.DeviceIdType.MESH
VMEM_LIMIT = 56 * 1024 * 1024
BF = jnp.bfloat16
F32 = jnp.float32


def places():
    head, seq, mp = (lax.axis_index(name) for name in ("head", "seq", "mp"))
    z, x = seq // 4, seq % 4
    odd = x % 2
    info = {
        "head": head,
        "mp": mp,
        "z": z,
        "x": x,
        "odd": odd,
        "pair": x // 2,
        "quarter": ((x + 1) // 2) % 2,
        "core": head % 2,
        "hi": head // 2,
        "e1": (head, seq + 1 - 2 * odd, mp),
        "e2": (head, z * 4 + 3 - x, mp),
        "zp": (head, ((z + 1) % 8) * 4 + x, mp),
        "zm": (head, ((z + 7) % 8) * 4 + x, mp),
        "near": (head, seq, 1 - mp),
        "far": ((head + 2) % 4, seq, 1 - mp),
        "twin": (head + 1 - 2 * (head % 2), seq, mp),
        "halo": (head, (seq + 31 + 2 * odd) % 32, mp),
    }
    return info


def greet(info):
    barrier = pltpu.get_barrier_semaphore()
    names = ("e1", "e2", "zp", "zm", "near", "far", "twin", "halo")
    for name in names:
        pl.semaphore_signal(barrier, inc=1, device_id=info[name], device_id_type=MESH)
    pl.semaphore_wait(barrier, len(names))


class Wires:
    def __init__(self, send, recv):
        self.send, self.recv, self.count = send, recv, 0
        self.started = []

    def slot(self):
        self.count += 1
        return self.count - 1

    def put(self, slot, src, dst, device):
        copy = pltpu.make_async_remote_copy(
            src_ref=src,
            dst_ref=dst,
            send_sem=self.send.at[slot],
            recv_sem=self.recv.at[slot],
            device_id=device,
            device_id_type=MESH,
        )
        copy.start()
        self.started.append((slot, src))

    def got(self, slot, dst):
        pltpu.make_async_copy(dst, dst, self.recv.at[slot]).wait()

    def finish(self):
        for slot, src in self.started:
            pltpu.make_async_copy(src, src, self.send.at[slot]).wait()


NT = (((1,), (1,)), ((), ()))
TN = (((0,), (0,)), ((), ()))


LAYERS = 8
COT_PARTS = 6
COT_ROWS = 192 // COT_PARTS
GATHER_SLOTS = 100


def front_kernel(
    hid, ws, cot, gain,
    q_out, k_out, v_out, g_out, inv_out, h_out, n_out, w_out, c_out,
    hv, nv, wv, cv, acc, send, recv, local,
):
    info = places()
    z, x, odd, p, q = (info[name] for name in ("z", "x", "odd", "pair", "quarter"))
    mp, core, hi = info["mp"], info["core"], info["hi"]
    wires = Wires(send, recv)
    ways = ("zp", "zm")
    mate = x + 1 - 2 * odd
    b = 1 + odd
    blocks = (b, 3 - b, 0)
    kept = []

    def keep(src, dst):
        copy = pltpu.make_async_copy(src, dst, local.at[3 + len(kept)])
        copy.start()
        kept.append(copy)

    def cols(block, head_hi, head_core, part):
        start = pl.multiple_of(((head_hi * 2 + head_core) * 2 + part) * 256, 256)
        return hv.at[block, :, pl.ds(start, 256)]

    own_w = pltpu.make_async_copy(ws.at[q], wv.at[:, z, x], local.at[0])
    own_w.start()
    own_h = pltpu.make_async_copy(hid, cols(b, hi, core, mp), local.at[1])
    own_h.start()
    own_c = pltpu.make_async_copy(cot, cv.at[odd], local.at[2])
    own_c.start()

    greet(info)

    w_e1 = [wires.slot() for _ in range(2)]
    h_e1, h_halo = wires.slot(), wires.slot()
    h_near = [wires.slot() for _ in range(3)]
    h_far = [wires.slot() for _ in range(3)]
    h_opp = [wires.slot() for _ in range(3)]
    h_twin = [[wires.slot() for _ in range(4)] for _ in range(3)]
    a_first = [[wires.slot() for _ in range(2)] for _ in range(2)]
    b_first = [[wires.slot() for _ in range(2)] for _ in range(2)]
    a_own = [[None] + [wires.slot() for _ in range(3)] for _ in range(2)]
    b_own = [[None] + [wires.slot() for _ in range(3)] for _ in range(2)]
    a_oth = [[wires.slot() for _ in range(4)] for _ in range(2)]
    a_e2 = [wires.slot() for _ in range(2)]
    b_e2 = [[wires.slot(), wires.slot()]] + [wires.slot() for _ in range(8)]
    c_e1 = [wires.slot() for _ in range(COT_PARTS)]
    c_near = [wires.slot() for _ in range(COT_PARTS)]

    def one(first, count, layer, place):
        return wv.at[pl.ds(first, count), layer, pl.ds(place, 1)]

    def own_pair(first, count, layer):
        return wv.at[pl.ds(first, count), layer, pl.ds(2 * p, 2)]

    def other_pair(first, count, layer):
        return wv.at[pl.ds(first, count), layer, pl.ds(2 - 2 * p, 2)]

    def span(way, hop, first):
        return (first, 2) if hop < 4 else (first + way, 1)

    def layer_from(way, hop):
        return (z + 8 - hop) % 8 if way == 0 else (z + hop) % 8

    def pass_on(slots, part, first, way, hop):
        lo, count = span(way, hop + 1, first)
        ref = part(lo, count, layer_from(way, hop))
        wires.put(slots[way][hop], ref, ref, info[ways[way]])

    def take(slots, part, first, way, hop):
        lo, count = span(way, hop, first)
        ref = part(lo, count, layer_from(way, hop))
        wires.got(slots[way][hop - 1], ref)
        return ref

    for half in (1, 0):
        arrs = pl.ds(2 * half, 2)
        wires.put(w_e1[half], ws.at[1 - q, arrs], wv.at[arrs, z, x], info["e1"])
    mine = cols(b, hi, core, mp)
    halo_own = cols(0, hi, core, mp)
    for first, slots in ((2, b_first), (0, a_first)):
        src = ws.at[q, pl.ds(first, 2)]
        for way in range(2):
            wires.put(slots[way][0], src, wv.at[pl.ds(first, 2), z, x], info[ways[way]])
    for first, slots in ((2, b_e2[0]), (0, a_e2)):
        src = ws.at[q, pl.ds(first, 2)]
        wires.put(slots[0], src, wv.at[pl.ds(first, 2), z, x], info["e2"])

    def spread(r, src):
        dst = cols(blocks[r], hi, core, mp)
        wires.put(h_near[r], src, dst, info["near"])
        wires.put(h_far[r], src, dst, info["far"])
        wires.put(h_twin[r][0], src, dst, info["twin"])

    wires.put(h_e1, hid, mine, info["e1"])

    @pl.when(odd == 1)
    def _():
        pltpu.make_async_remote_copy(
            src_ref=hid,
            dst_ref=halo_own,
            send_sem=send.at[h_halo],
            recv_sem=recv.at[h_halo],
            device_id=info["halo"],
            device_id_type=MESH,
        ).start()

    spread(0, hid)

    def second(half, slots, x_slots):
        first = 2 * half
        ref = one(first, 2, z, mate)
        wires.got(w_e1[half], ref)
        for way in range(2):
            wires.put(slots[way][1], ref, ref, info[ways[way]])
        wires.put(x_slots[1], ref, ref, info["e2"])

    def from_near(r):
        got = cols(blocks[r], hi, core, 1 - mp)
        wires.got(h_near[r], got)
        wires.put(h_opp[r], got, got, info["far"])
        wires.put(h_twin[r][1], got, got, info["twin"])

    def from_far(r):
        got = cols(blocks[r], 1 - hi, core, 1 - mp)
        wires.got(h_far[r], got)
        wires.put(h_twin[r][2], got, got, info["twin"])

    def from_opp(r):
        got = cols(blocks[r], 1 - hi, core, mp)
        wires.got(h_opp[r], got)
        wires.put(h_twin[r][3], got, got, info["twin"])

    def from_twin(r):
        other = 1 - core
        wires.got(h_twin[r][0], cols(blocks[r], hi, other, mp))
        wires.got(h_twin[r][1], cols(blocks[r], hi, other, 1 - mp))
        wires.got(h_twin[r][2], cols(blocks[r], 1 - hi, other, 1 - mp))
        wires.got(h_twin[r][3], cols(blocks[r], 1 - hi, other, mp))
        if r == 0:
            own_h.wait()
        block = blocks[r]

        def rows_step(i, carry):
            rows = pl.ds(pl.multiple_of(i * 32, 32), 32)
            states = hv[block, rows, :].astype(F32)
            inverse = lax.rsqrt(jnp.mean(states * states, axis=1, keepdims=True) + EPS)
            nv[block, rows, :] = (states * inverse * gain[...]).astype(BF)
            inv_out[block, rows, :] = jnp.broadcast_to(inverse, (32, 128))
            return carry

        lax.fori_loop(0, 12, rows_step, 0)
        keep(hv.at[block], h_out.at[block])
        keep(nv.at[block], n_out.at[block])

    def halo_on():
        wires.got(h_halo, halo_own)

        @pl.when(odd == 0)
        def _():
            pltpu.make_async_remote_copy(
                src_ref=halo_own,
                dst_ref=halo_own,
                send_sem=send.at[h_halo],
                recv_sem=recv.at[h_halo],
                device_id=info["e1"],
                device_id_type=MESH,
            ).start()

        wires.started.append((h_halo, hid))

    def c_rows(block, part, k):
        start = pl.multiple_of(part * 192 + k * COT_ROWS, COT_ROWS)
        return cv.at[block, pl.ds(start, COT_ROWS)]

    def c_send():
        for k in range(COT_PARTS):
            start = pl.multiple_of(mp * 192 + k * COT_ROWS, COT_ROWS)
            wires.put(c_e1[k], cot.at[pl.ds(start, COT_ROWS)], c_rows(odd, mp, k), info["e1"])

    def c_on(k):
        ref = c_rows(1 - odd, mp, k)
        wires.got(c_e1[k], ref)
        wires.put(c_near[k], ref, ref, info["near"])

    def c_got(k):
        wires.got(c_near[k], c_rows(1 - odd, 1 - mp, k))

    def first_hop(slots, first, way):
        layer = layer_from(way, 1)
        wires.got(slots[way][0], one(first, 2, layer, x))
        wires.got(slots[way][1], one(first, 2, layer, mate))

    def a_hop(hop, way):
        if hop == 1:
            first_hop(a_first, 0, way)
        else:
            take(a_own, own_pair, 0, way, hop)
        if hop < 4:
            pass_on(a_own, own_pair, 0, way, hop)

    def b_hop(hop, way):
        if hop == 1:
            first_hop(b_first, 2, way)
        else:
            take(b_own, own_pair, 2, way, hop)
        if hop < 4:
            pass_on(b_own, own_pair, 2, way, hop)
        lo, count = span(way, hop, 2)
        ref = own_pair(lo, count, layer_from(way, hop))
        wires.put(b_e2[2 * hop - 1 + way], ref, ref, info["e2"])

    def x_hop(hop, way):
        if hop == 0:
            wires.got(a_e2[0], one(0, 2, z, 3 - x))
            wires.got(a_e2[1], one(0, 2, z, 3 - mate))
            for way in range(2):
                pass_on(a_oth, other_pair, 0, way, 0)
        else:
            take(a_oth, other_pair, 0, way, hop)
            if hop < 4:
                pass_on(a_oth, other_pair, 0, way, hop)

    def e2_got(hop, way):
        if hop == 0:
            wires.got(b_e2[0][0], one(2, 2, z, 3 - x))
            wires.got(b_e2[0][1], one(2, 2, z, 3 - mate))
        else:
            lo, count = span(way, hop, 2)
            wires.got(b_e2[2 * hop - 1 + way], other_pair(lo, count, layer_from(way, hop)))

    def project(hop, count):
        def step(i, carry):
            way, block = i // 3, i % 3
            layer = (z + hop + way * (8 - 2 * hop)) % 8
            lanes = pl.ds(pl.multiple_of(layer * 256, 256), 256)
            rows = nv[block, :, lanes]
            for s in range(3):
                weight = wv[s, layer].reshape(256, 256)
                term = jnp.dot(rows, weight, preferred_element_type=F32)
                if hop == 0:
                    acc[s, block] = term
                else:
                    acc[s, block] += term
            return carry

        lax.fori_loop(0, 3 * count, step, 0)
        for layer in {0: (z,), 4: (layer_from(0, 4),)}.get(
            hop, (layer_from(0, hop), layer_from(1, hop))
        ):
            keep(wv.at[:, layer], w_out.at[:, layer])

    second(1, b_first, b_e2[0])
    from_near(0)
    from_far(0)
    b_hop(1, 0)
    second(0, a_first, a_e2)
    b_hop(1, 1)
    halo_on()
    c_send()
    e2_got(0, 0)
    a_hop(1, 1)
    b_hop(2, 0)
    spread(2, halo_own)
    wires.got(h_e1, cols(3 - b, hi, core, mp))
    spread(1, cols(3 - b, hi, core, mp))
    from_opp(0)
    a_hop(1, 0)
    e2_got(1, 0)
    b_hop(2, 1)
    x_hop(0, 0)
    from_twin(0)
    b_hop(3, 0)
    a_hop(2, 1)
    c_on(0)
    e2_got(1, 1)
    a_hop(2, 0)
    from_near(2)
    from_far(2)
    from_near(1)
    c_on(1)
    from_far(1)
    e2_got(2, 0)
    x_hop(1, 0)
    x_hop(1, 1)
    b_hop(3, 1)
    b_hop(4, 0)
    e2_got(2, 1)
    c_on(2)
    a_hop(3, 1)
    a_hop(3, 0)
    c_got(0)
    e2_got(3, 0)
    from_opp(2)
    x_hop(2, 0)
    c_on(3)
    b_hop(4, 1)
    x_hop(2, 1)
    from_opp(1)
    e2_got(3, 1)
    own_w.wait()
    from_twin(2)
    a_hop(4, 0)
    c_on(4)
    c_got(1)
    from_twin(1)
    a_hop(4, 1)
    c_on(5)
    x_hop(3, 0)
    x_hop(3, 1)
    project(0, 1)
    project(1, 2)
    e2_got(4, 0)
    e2_got(4, 1)
    c_got(2)
    project(2, 2)
    x_hop(4, 0)
    x_hop(4, 1)
    project(3, 2)
    project(4, 1)
    c_got(3)
    c_got(4)
    c_got(5)
    own_c.wait()
    keep(cv, c_out)

    def finish_block(block, carry):
        for s, out in ((0, q_out), (1, k_out), (2, v_out)):
            out[block] = acc[s, block].astype(BF)
        return carry

    lax.fori_loop(0, 3, finish_block, 0)

    def grad_block(block, carry):
        g_out[block] = jnp.dot(
            cv[block], wv[3].reshape(2048, 256), preferred_element_type=F32
        ).astype(BF)
        return carry

    lax.fori_loop(0, 2, grad_block, 0)
    wires.finish()
    for copy in kept:
        copy.wait()


def front(hid, ws, cot, gain):
    anywhere = pl.BlockSpec(memory_space=pl.ANY)
    in_vmem = pl.BlockSpec(memory_space=pltpu.VMEM)
    return pl.pallas_call(
        front_kernel,
        out_shape=(
            jax.ShapeDtypeStruct((3, 384, 256), BF),
            jax.ShapeDtypeStruct((3, 384, 256), BF),
            jax.ShapeDtypeStruct((3, 384, 256), BF),
            jax.ShapeDtypeStruct((2, 384, 256), BF),
            jax.ShapeDtypeStruct((3, 384, 128), F32),
            jax.ShapeDtypeStruct((3, 384, 2048), BF),
            jax.ShapeDtypeStruct((3, 384, 2048), BF),
            jax.ShapeDtypeStruct((4, 8, 4, 64, 256), BF),
            jax.ShapeDtypeStruct((2, 384, 2048), BF),
        ),
        in_specs=[anywhere] * 3 + [in_vmem],
        out_specs=(in_vmem,) * 5 + (anywhere,) * 4,
        scratch_shapes=[
            pltpu.VMEM((3, 384, 2048), BF),
            pltpu.VMEM((3, 384, 2048), BF),
            pltpu.VMEM((4, 8, 4, 64, 256), BF),
            pltpu.VMEM((2, 384, 2048), BF),
            pltpu.VMEM((3, 3, 384, 256), F32),
            pltpu.SemaphoreType.DMA((GATHER_SLOTS,)),
            pltpu.SemaphoreType.DMA((GATHER_SLOTS,)),
            pltpu.SemaphoreType.DMA((24,)),
        ],
        compiler_params=pltpu.CompilerParams(
            collective_id=0, has_side_effects=True, vmem_limit_bytes=VMEM_LIMIT
        ),
        name="front",
    )(hid, ws, cot, gain)


REDUCE_SLOTS = 70


def add(*terms):
    total = terms[0].astype(F32)
    for term in terms[1:]:
        total = total + term.astype(F32)
    return total.astype(BF)


def back_kernel(
    dqkv, attn, inv, gain, h_in, n_in, w_in, c_in,
    w_res, t_res,
    hv, nv, wv, cv, grads, trunk, scaled,
    a_got, a_out, b_e2got, b_got, b_out, a_fin, a_e2got, w_pair,
    t_twin, t_sum, t_far1, t_far2, t_near1, t_near2, t_mid1, t_mid2, t_fin, t_e1, t_halo, t_pass,
    send, recv, local,
):
    info = places()
    z, x, odd, p, q = (info[name] for name in ("z", "x", "odd", "pair", "quarter"))
    mp, core, hi = info["mp"], info["core"], info["hi"]
    wires = Wires(send, recv)
    ways = ("zp", "zm")
    loads = [
        pltpu.make_async_copy(src, dst, local.at[i])
        for i, (src, dst) in enumerate(((n_in, nv), (c_in, cv), (w_in, wv), (h_in, hv)))
    ]
    for load in loads:
        load.start()
    a_slot = [[wires.slot() for _ in range(4)] for _ in range(2)]
    b_slot = [[wires.slot() for _ in range(4)] for _ in range(2)]
    b_e2 = [wires.slot() for _ in range(8)]
    a_e2 = wires.slot()
    w_e1 = [wires.slot() for _ in range(2)]
    s_twin = [[wires.slot() for _ in range(2)] for _ in range(3)]
    s_far1, s_far2, s_near1, s_near2, s_near3 = (
        [wires.slot() for _ in range(3)] for _ in range(5)
    )
    s_e1 = wires.slot()
    s_half = wires.slot()
    s_halo = wires.slot()
    blocks = (0, 2 - odd, 1 + odd)
    top, low = pl.ds(0, 192), pl.ds(192, 192)

    greet(info)

    def to_layer(way, left):
        return (z + left) % 8 if way == 0 else (z + 8 - left) % 8

    def weight_grads(left, count):
        def step(way, carry):
            layer = (z + left + way * (8 - 2 * left)) % 8
            lanes = pl.ds(pl.multiple_of(layer * 256, 256), 256)
            rows = nv[:, lanes]
            triple = lax.dot_general(rows, dqkv[...], TN, preferred_element_type=F32)
            for s in range(3):
                grads[s, layer] = triple[:, s * 256 : (s + 1) * 256].astype(BF).reshape(4, 64, 256)
            last = lax.dot_general(cv[:, lanes], attn[...], TN, preferred_element_type=F32)
            grads[3, layer] = last.astype(BF).reshape(4, 64, 256)
            return carry

        lax.fori_loop(0, count, step, 0)

    def cross(k, way, left):
        wires.put(
            b_e2[k],
            grads.at[pl.ds(2, 2), to_layer(way, left), pl.ds(2 - 2 * p, 2)],
            b_e2got.at[k],
            info["e2"],
        )

    def state_grads(r):
        block = blocks[r]
        start = pl.multiple_of(block * 384, 384)
        factor = inv[block, :, 0:1]

        def first(c, carry):
            lanes = pl.ds(pl.multiple_of(c * 256, 256), 256)
            total = None
            for s in range(3):
                if r == 0 and s == 0:
                    continue
                term = lax.dot_general(
                    dqkv[pl.ds(start, 384), s * 256 : (s + 1) * 256],
                    wv[s, c].reshape(256, 256),
                    NT,
                    preferred_element_type=F32,
                )
                total = term if total is None else total + term
            total = total * gain[:, lanes]
            scaled[c] = total
            units = hv[block, :, lanes].astype(F32) * factor
            return carry + jnp.sum(total * units, axis=1, keepdims=True)

        mean = lax.fori_loop(0, 8, first, jnp.zeros((384, 1), F32)) * (1.0 / 2048)
        once = jnp.where(mp == 0, 1.0, 0.0)

        def second(c, carry):
            lanes = pl.ds(pl.multiple_of(c * 256, 256), 256)
            units = hv[block, :, lanes].astype(F32) * factor
            result = factor * (scaled[c] - units * mean)
            if r == 2:
                own = cv[pl.ds(pl.multiple_of(odd * 384, 384), 384), lanes]
                result = result + own.astype(F32) * once
            trunk[r, c] = result.astype(BF)
            return carry

        lax.fori_loop(0, 8, second, 0)
        for side in range(2):
            there = pl.ds((side * 2 + 1 - core) * 2, 2)
            wires.put(s_twin[r][side], trunk.at[r, there], t_twin.at[r, side], info["twin"])

    def fold_twin(r):
        for side in (0, 1):
            wires.got(s_twin[r][side], t_twin.at[r, side])
            t_sum[r, side] = add(trunk[r, pl.ds((side * 2 + core) * 2, 2)], t_twin[r, side])
        wires.put(s_far1[r], t_sum.at[r, 1 - hi, :, top], t_far1.at[r], info["far"])
        wires.put(s_near1[r], t_sum.at[r, hi, 1 - mp, low], t_near1.at[r, 0], info["near"])
        wires.put(s_near3[r], t_sum.at[r, 1 - hi, mp, low], t_near1.at[r, 1], info["near"])

    def fold_first(r):
        wires.got(s_far1[r], t_far1.at[r])
        t_mid1[r] = add(t_sum[r, hi, :, 0:192], t_far1[r])
        wires.put(s_near2[r], t_mid1.at[r, 1 - mp], t_near2.at[r], info["near"])
        wires.got(s_near3[r], t_near1.at[r, 1])
        t_mid2[r, 1] = add(t_sum[r, 1 - hi, 1 - mp, 192:384], t_near1[r, 1])
        wires.put(s_far2[r], t_mid2.at[r, 1], t_far2.at[r], info["far"])
        wires.got(s_near1[r], t_near1.at[r, 0])
        t_mid2[r, 0] = add(t_sum[r, hi, mp, 192:384], t_near1[r, 0])

    def fold_second(r):
        wires.got(s_near2[r], t_near2.at[r])
        t_fin[r, 0:192] = add(t_mid1[r, mp], t_near2[r])
        wires.got(s_far2[r], t_far2.at[r])
        t_fin[r, 192:384] = add(t_mid2[r, 0], t_far2[r])

    def a_step(way, step):
        layer = to_layer(way, 4 - step)
        if step == 1:
            wires.got(a_slot[way][0], a_got.at[way, 0, pl.ds(way, 1)])
            a_out[way, step, way] = add(grads[way, layer], a_got[way, 0, way])
            a_out[way, step, 1 - way] = grads[1 - way, layer]
        else:
            wires.got(a_slot[way][step - 1], a_got.at[way, step - 1])
            a_out[way, step] = add(grads[pl.ds(0, 2), layer], a_got[way, step - 1])
        wires.put(a_slot[way][step], a_out.at[way, step], a_got.at[way, step], info[ways[way]])

    def b_start(way, left, k):
        wires.got(b_e2[k], b_e2got.at[k])
        layer = to_layer(way, left)
        return add(grads[pl.ds(2, 2), layer, pl.ds(2 * p, 2)], b_e2got[k])

    def b_step(way, step):
        mine = b_start(way, 4 - step, 2 * step - 1 + way)
        if step == 1:
            wires.got(b_slot[way][0], b_got.at[way, 0, pl.ds(way, 1)])
            b_out[way, step, way] = add(mine[way], b_got[way, 0, way])
            b_out[way, step, 1 - way] = mine[1 - way]
        else:
            wires.got(b_slot[way][step - 1], b_got.at[way, step - 1])
            b_out[way, step] = add(mine, b_got[way, step - 1])
        wires.put(b_slot[way][step], b_out.at[way, step], b_got.at[way, step], info[ways[way]])

    loads[0].wait()
    loads[1].wait()
    weight_grads(4, 1)
    for way in range(2):
        wires.put(
            a_slot[way][0],
            grads.at[pl.ds(way, 1), to_layer(way, 4)],
            a_got.at[way, 0, pl.ds(way, 1)],
            info[ways[way]],
        )
    cross(0, 0, 4)
    weight_grads(3, 2)
    cross(1, 0, 3)
    cross(2, 1, 3)
    for way in range(2):
        a_step(way, 1)
    b_out[0, 0] = b_start(0, 4, 0)
    for way in range(2):
        wires.put(
            b_slot[way][0],
            b_out.at[0, 0, pl.ds(way, 1)],
            b_got.at[way, 0, pl.ds(way, 1)],
            info[ways[way]],
        )
    loads[2].wait()
    loads[3].wait()
    state_grads(0)
    weight_grads(2, 2)
    cross(3, 0, 2)
    cross(4, 1, 2)
    fold_twin(0)
    for way in range(2):
        b_step(way, 1)
    state_grads(1)
    for way in range(2):
        a_step(way, 2)
    weight_grads(1, 2)
    cross(5, 0, 1)
    cross(6, 1, 1)
    fold_twin(1)
    fold_first(0)
    state_grads(2)
    for way in range(2):
        b_step(way, 2)
    weight_grads(0, 1)
    cross(7, 0, 0)
    fold_twin(2)
    for way in range(2):
        a_step(way, 3)
    fold_second(0)

    @pl.when(odd == 1)
    def _():
        pltpu.make_async_remote_copy(
            src_ref=t_fin.at[0],
            dst_ref=t_halo,
            send_sem=send.at[s_half],
            recv_sem=recv.at[s_half],
            device_id=info["e1"],
            device_id_type=MESH,
        ).start()

    fold_first(1)
    for way in range(2):
        b_step(way, 3)

    @pl.when(odd == 0)
    def _():
        wires.got(s_half, t_halo)
        t_pass[...] = add(t_fin[0], t_halo[...])
        pltpu.make_async_remote_copy(
            src_ref=t_pass,
            dst_ref=t_halo,
            send_sem=send.at[s_halo],
            recv_sem=recv.at[s_halo],
            device_id=info["halo"],
            device_id_type=MESH,
        ).start()

    fold_second(1)
    wires.put(s_e1, t_fin.at[1], t_e1, info["e1"])
    fold_first(2)
    for way in range(2):
        wires.got(a_slot[way][3], a_got.at[way, 3])
    a_fin[...] = add(grads[pl.ds(0, 2), z], a_got[0, 3], a_got[1, 3])
    wires.put(a_e2, a_fin.at[:, pl.ds(2 - 2 * p, 2)], a_e2got, info["e2"])
    fold_second(2)
    last = b_start(0, 0, 7)
    for way in range(2):
        wires.got(b_slot[way][3], b_got.at[way, 3])
    w_pair[pl.ds(2, 2)] = add(last, b_got[0, 3], b_got[1, 3])
    wires.put(
        w_e1[1], w_pair.at[pl.ds(2, 2), 1 - odd], w_res.at[q, pl.ds(2, 2)], info["e1"]
    )
    wires.got(a_e2, a_e2got)
    w_pair[pl.ds(0, 2)] = add(a_fin[:, pl.ds(2 * p, 2)], a_e2got[...])
    wires.put(
        w_e1[0], w_pair.at[pl.ds(0, 2), 1 - odd], w_res.at[q, pl.ds(0, 2)], info["e1"]
    )
    w_res[q] = w_pair[:, odd]
    wires.got(s_e1, t_e1)

    @pl.when(odd == 0)
    def _():
        t_res[...] = add(t_fin[2], t_e1[...])
        pltpu.make_async_copy(t_pass, t_pass, send.at[s_halo]).wait()

    @pl.when(odd == 1)
    def _():
        wires.got(s_halo, t_halo)
        t_res[...] = add(t_fin[2], t_e1[...], t_halo[...])
        pltpu.make_async_copy(t_halo, t_halo, send.at[s_half]).wait()

    for part in range(2):
        wires.got(w_e1[part], w_res.at[1 - q, pl.ds(2 * part, 2)])
    wires.finish()


def back(dqkv, attn, inv, gain, hidden, normed, weights, upstream):
    anywhere = pl.BlockSpec(memory_space=pl.ANY)
    in_vmem = pl.BlockSpec(memory_space=pltpu.VMEM)
    shapes = [
        (3, 384, 2048), (1152, 2048), (4, 8, 4, 64, 256), (768, 2048), (4, 8, 4, 64, 256),
        (3, 8, 384, 256),
    ]
    more = [
        (2, 4, 2, 4, 64, 256), (2, 4, 2, 4, 64, 256), (8, 2, 2, 64, 256), (2, 4, 2, 2, 64, 256),
        (2, 4, 2, 2, 64, 256), (2, 4, 64, 256), (2, 2, 64, 256), (4, 2, 64, 256),
        (3, 2, 2, 384, 256), (3, 2, 2, 384, 256),
        (3, 2, 192, 256), (3, 192, 256), (3, 2, 192, 256), (3, 192, 256),
        (3, 2, 192, 256), (3, 2, 192, 256),
        (3, 384, 256), (384, 256), (384, 256), (384, 256),
    ]
    return pl.pallas_call(
        back_kernel,
        out_shape=(
            jax.ShapeDtypeStruct((2, 4, 64, 256), BF),
            jax.ShapeDtypeStruct((384, 256), BF),
        ),
        in_specs=[in_vmem] * 4 + [anywhere] * 4,
        out_specs=(in_vmem,) * 2,
        scratch_shapes=[pltpu.VMEM(shape, BF) for shape in shapes]
        + [pltpu.VMEM((8, 384, 256), F32)]
        + [pltpu.VMEM(shape, BF) for shape in more]
        + [
            pltpu.SemaphoreType.DMA((REDUCE_SLOTS,)),
            pltpu.SemaphoreType.DMA((REDUCE_SLOTS,)),
            pltpu.SemaphoreType.DMA((4,)),
        ],
        compiler_params=pltpu.CompilerParams(
            collective_id=1, has_side_effects=True, vmem_limit_bytes=VMEM_LIMIT
        ),
        name="back",
    )(dqkv, attn, inv, gain, hidden, normed, weights, upstream)


def attend_kernel(q_ref, k_ref, v_ref, g_ref, segk_ref, segq_ref, dqkv_ref, o_ref, dk_acc, dv_acc):
    scale = HD**-0.5
    dk_acc[...] = jnp.zeros_like(dk_acc)
    dv_acc[...] = jnp.zeros_like(dv_acc)
    dqkv_ref[0:384, 0:256] = jnp.zeros((384, 256), BF)
    lane_head = lax.broadcasted_iota(jnp.int32, (128, 256), 1) // HD

    def by_head(rows):
        return jnp.concatenate(
            [jnp.where(lane_head == h, rows, jnp.zeros_like(rows)) for h in range(4)], axis=0
        )

    def fold(wide):
        return jnp.concatenate(
            [wide[h * HD : (h + 1) * HD, h * 128 : (h + 1) * 128] for h in range(4)], axis=0
        ).T

    key_at = lax.broadcasted_iota(jnp.int32, (512, 128), 0)
    query_at = lax.broadcasted_iota(jnp.int32, (512, 128), 1) + 384
    causal = key_at <= query_at

    def tile(t, carry):
        start = pl.multiple_of(t * 128, 128)
        here, window = pl.ds(start, 128), pl.ds(start, 512)
        there = pl.ds(pl.multiple_of(start + 384, 128), 128)
        queries, grads = by_head(q_ref[there, :]), by_head(g_ref[here, :])
        keys, values = k_ref[window, :], v_ref[window, :]
        allowed = causal & (segk_ref[window, :] == segq_ref[t])
        allowed = jnp.concatenate([allowed] * 4, axis=1)
        scores = lax.dot_general(keys, queries, NT, preferred_element_type=F32) * scale
        scores = jnp.where(allowed, scores, MASKED)
        expo = jnp.exp(scores - jnp.max(scores, axis=0, keepdims=True))
        probs = expo * (1.0 / jnp.sum(expo, axis=0, keepdims=True))
        prob_rows = probs.astype(BF)
        prob_grad = lax.dot_general(values, grads, NT, preferred_element_type=F32)
        delta = jnp.sum(probs * prob_grad, axis=0, keepdims=True)
        score_grad = (probs * (prob_grad - delta) * scale).astype(BF)
        dv_acc[window, :] += jnp.dot(prob_rows, grads, preferred_element_type=F32)
        dk_acc[window, :] += jnp.dot(score_grad, queries, preferred_element_type=F32)
        o_ref[here, :] = fold(
            lax.dot_general(values, prob_rows, TN, preferred_element_type=F32)
        ).astype(BF)
        dqkv_ref[there, 0:256] = fold(
            lax.dot_general(keys, score_grad, TN, preferred_element_type=F32)
        ).astype(BF)
        return carry

    lax.fori_loop(0, 6, tile, 0)
    dqkv_ref[:, 256:512] = dk_acc[...].astype(BF)
    dqkv_ref[:, 512:768] = dv_acc[...].astype(BF)


def attend(queries, keys, values, attn_grad, seg_keys, seg_queries):
    return pl.pallas_call(
        attend_kernel,
        out_shape=(
            jax.ShapeDtypeStruct((1152, 768), BF),
            jax.ShapeDtypeStruct((768, 256), BF),
        ),
        scratch_shapes=[pltpu.VMEM((1152, 256), F32)] * 2,
        compiler_params=pltpu.CompilerParams(vmem_limit_bytes=VMEM_LIMIT),
        name="attend",
    )(queries, keys, values, attn_grad, seg_keys, seg_queries)


def per_device(hidden_states, norm_gain, qkv_weight, out_weight, cotangent, segment_ids):
    seq = lax.axis_index("seq")
    odd = seq % 2
    shard = jnp.concatenate(
        [jnp.transpose(qkv_weight[0], (1, 0, 2)), out_weight], axis=0
    )
    shard = jnp.transpose(shard.reshape(4, 64, 2, 256), (2, 0, 1, 3))
    gain = norm_gain.astype(F32)
    queries, keys, values, attn_grad, inverse, hidden, normed, weights, upstream = front(
        hidden_states, shard, cotangent[0], gain
    )

    first = (seq - odd) * 384 - 384
    seg = lax.dynamic_slice_in_dim(segment_ids, first + 384, 768)
    earlier = lax.dynamic_slice_in_dim(segment_ids, jnp.maximum(first, 0), 384)
    earlier = jnp.where(first >= 0, earlier, -1)
    seg_keys = jnp.concatenate([earlier, seg])[:, None]
    dqkv, attn_out = attend(
        queries.reshape(1152, 256),
        keys.reshape(1152, 256),
        values.reshape(1152, 256),
        attn_grad.reshape(768, 256),
        seg_keys,
        seg.reshape(6, 1, 128),
    )
    w_res, t_res = back(
        dqkv,
        attn_out,
        inverse,
        gain,
        hidden,
        normed.reshape(1152, 2048),
        weights,
        upstream.reshape(768, 2048),
    )
    merged = jnp.transpose(w_res, (1, 2, 0, 3)).reshape(4, 64, 512)
    return (t_res, jnp.transpose(merged[:3], (1, 0, 2))[None], merged[3][None])


def solution(mesh):
    placed = (
        P("seq", ("head", "mp")),
        P("head", None),
        P("head", "seq", None, "mp"),
        P("head", "seq", "mp"),
        P("head", "seq", None),
        P(),
    )
    return jax.shard_map(
        per_device,
        mesh=mesh,
        in_specs=placed,
        out_specs=(P("seq", ("head", "mp")), P("head", "seq", None, "mp"), P("head", "seq", "mp")),
        check_vma=False,
    )
```

```python
import functools

import jax
import jax.numpy as jnp
from jax import lax
from jax.experimental import pallas as pl
from jax.experimental.pallas import tpu as pltpu
from jax.sharding import PartitionSpec as P

HD = 64
EPS = 1e-05
MASKED = -1e30
MESH = pl.DeviceIdType.MESH
VMEM_LIMIT = 60 * 1024 * 1024
BF = jnp.bfloat16
F32 = jnp.float32


def places():
    head, seq, mp = (lax.axis_index(name) for name in ("head", "seq", "mp"))
    z, x = seq // 4, seq % 4
    odd = x % 2
    info = {
        "head": head,
        "mp": mp,
        "z": z,
        "x": x,
        "odd": odd,
        "pair": x // 2,
        "quarter": ((x + 1) // 2) % 2,
        "core": head % 2,
        "hi": head // 2,
        "e1": (head, seq + 1 - 2 * odd, mp),
        "e2": (head, z * 4 + 3 - x, mp),
        "zp": (head, ((z + 1) % 8) * 4 + x, mp),
        "zm": (head, ((z + 7) % 8) * 4 + x, mp),
        "near": (head, seq, 1 - mp),
        "far": ((head + 2) % 4, seq, 1 - mp),
        "twin": (head + 1 - 2 * (head % 2), seq, mp),
        "halo": (head, (seq + 31 + 2 * odd) % 32, mp),
    }
    return info


def greet(info):
    barrier = pltpu.get_barrier_semaphore()
    names = ("e1", "e2", "zp", "zm", "near", "far", "twin", "halo")
    for name in names:
        pl.semaphore_signal(barrier, inc=1, device_id=info[name], device_id_type=MESH)
    pl.semaphore_wait(barrier, len(names))


class Wires:
    def __init__(self, send, recv):
        self.send, self.recv, self.count = send, recv, 0
        self.started = []

    def slot(self):
        self.count += 1
        return self.count - 1

    def put(self, slot, src, dst, device):
        copy = pltpu.make_async_remote_copy(
            src_ref=src,
            dst_ref=dst,
            send_sem=self.send.at[slot],
            recv_sem=self.recv.at[slot],
            device_id=device,
            device_id_type=MESH,
        )
        copy.start()
        self.started.append((slot, src))

    def got(self, slot, dst):
        pltpu.make_async_copy(dst, dst, self.recv.at[slot]).wait()

    def finish(self):
        for slot, src in self.started:
            pltpu.make_async_copy(src, src, self.send.at[slot]).wait()


NT = (((1,), (1,)), ((), ()))
TN = (((0,), (0,)), ((), ()))
COT_PARTS = 6
COT_ROWS = 192 // COT_PARTS
SLOTS = 216


def add(*terms):
    total = terms[0].astype(F32)
    for term in terms[1:]:
        total = total + term.astype(F32)
    return total.astype(BF)


def kernel(
    hid, qkv, wo, cot, gain, seg,
    t_res, qkv_res, wo_res,
    ws, hv, nv, wv, cv, inv, acc, q_s, k_s, v_s, g_s, segk, dqkv, attn, grads,
    a_got, b_e2got, b_got, a_fin, a_e2got, w_pair, w_res,
    t_twin, t_far1, t_far2, t_near1, t_near2, t_mid1, t_mid2, t_fin, t_e1, t_halo, t_pass,
    send, recv, local,
):
    info = places()
    z, x, odd, p, q = (info[name] for name in ("z", "x", "odd", "pair", "quarter"))
    mp, core, hi = info["mp"], info["core"], info["hi"]
    seq = z * 4 + x
    wires = Wires(send, recv)
    ways = ("zp", "zm")
    mate = x + 1 - 2 * odd
    b = 1 + odd
    order = (b, 3 - b, 0)

    def cols(block, head_hi, head_core, part):
        start = pl.multiple_of(((head_hi * 2 + head_core) * 2 + part) * 256, 256)
        return hv.at[block, :, pl.ds(start, 256)]

    own_h = pltpu.make_async_copy(hid, cols(b, hi, core, mp), local.at[0])
    own_h.start()
    own_rows = pl.ds(pl.multiple_of(odd * 384, 384), 384)
    own_c = pltpu.make_async_copy(cot.at[0], cv.at[own_rows], local.at[1])
    own_c.start()
    for half in range(2):
        lanes = slice(half * 256, half * 256 + 256)
        for s in range(3):
            ws[half, s] = qkv[0, s, :, lanes]
        ws[half, 3] = wo[0, :, lanes]
    wv[:, z, x] = ws[q]

    greet(info)

    def slots(count):
        return [wires.slot() for _ in range(count)]

    w_e1 = slots(2)
    h_e1, h_halo = slots(2)
    h_near, h_far, h_opp = slots(3), slots(3), slots(3)
    h_twin = [slots(4) for _ in range(3)]
    w_z = {kind: [[slots(4) for _ in range(2)] for _ in range(2)] for kind in "ab"}
    x_z = [slots(4) for _ in range(2)]
    a_e2in = slots(2)
    b_e2in = [[slots(2)] + [None] * 4, [slots(2)] + [None] * 4]
    for way in range(2):
        for hop in range(1, 5):
            b_e2in[way][hop] = slots(2)
    c_e1, c_near = slots(COT_PARTS), slots(COT_PARTS)
    base = {"a": 0, "b": 2}

    def one(first, count, layer, place):
        return wv.at[pl.ds(first, count), layer, pl.ds(place, 1)]

    def other_pair(first, count, layer):
        return wv.at[pl.ds(first, count), layer, pl.ds(2 - 2 * p, 2)]

    def span(way, hop, first):
        return (first, 2) if hop < 4 else (first + way, 1)

    def layer_from(way, hop):
        return (z + 8 - hop) % 8 if way == 0 else (z + hop) % 8

    mine = cols(b, hi, core, mp)
    halo_own = cols(0, hi, core, mp)
    wires.put(h_e1, hid, mine, info["e1"])
    for half in (1, 0):
        arrs = pl.ds(2 * half, 2)
        wires.put(
            w_e1[half], ws.at[1 - q, arrs], wv.at[arrs, z, x], info["e1"]
        )
    for kind in "ba":
        arrs = pl.ds(base[kind], 2)
        for way in range(2):
            wires.put(w_z[kind][0][way][0], ws.at[q, arrs], wv.at[arrs, z, x], info[ways[way]])
    wires.put(a_e2in[0], ws.at[q, pl.ds(0, 2)], wv.at[pl.ds(0, 2), z, x], info["e2"])
    wires.put(b_e2in[0][0][0], ws.at[q, pl.ds(2, 2)], wv.at[pl.ds(2, 2), z, x], info["e2"])

    @pl.when(odd == 1)
    def _():
        pltpu.make_async_remote_copy(
            src_ref=hid,
            dst_ref=halo_own,
            send_sem=send.at[h_halo],
            recv_sem=recv.at[h_halo],
            device_id=info["halo"],
            device_id_type=MESH,
        ).start()

    def spread(r):
        dst = cols(order[r], hi, core, mp)
        if r == 1:
            wires.got(h_e1, dst)
        src = hid if r == 0 else dst
        wires.put(h_near[r], src, dst, info["near"])
        wires.put(h_far[r], src, dst, info["far"])
        wires.put(h_twin[r][0], src, dst, info["twin"])

    spread(0)

    def halo_on():
        wires.got(h_halo, halo_own)

        @pl.when(odd == 0)
        def _():
            pltpu.make_async_remote_copy(
                src_ref=halo_own,
                dst_ref=halo_own,
                send_sem=send.at[h_halo],
                recv_sem=recv.at[h_halo],
                device_id=info["e1"],
                device_id_type=MESH,
            ).start()

        wires.started.append((h_halo, hid))

    def from_near(r):
        got = cols(order[r], hi, core, 1 - mp)
        wires.got(h_near[r], got)
        wires.put(h_opp[r], got, got, info["far"])
        wires.put(h_twin[r][1], got, got, info["twin"])

    def from_far(r):
        got = cols(order[r], 1 - hi, core, 1 - mp)
        wires.got(h_far[r], got)
        wires.put(h_twin[r][2], got, got, info["twin"])

    def from_opp(r):
        got = cols(order[r], 1 - hi, core, mp)
        wires.got(h_opp[r], got)
        wires.put(h_twin[r][3], got, got, info["twin"])

    def from_twin(r):
        other = 1 - core
        wires.got(h_twin[r][0], cols(order[r], hi, other, mp))
        wires.got(h_twin[r][1], cols(order[r], hi, other, 1 - mp))
        wires.got(h_twin[r][2], cols(order[r], 1 - hi, other, 1 - mp))
        wires.got(h_twin[r][3], cols(order[r], 1 - hi, other, mp))
        if r == 0:
            own_h.wait()
        block = order[r]

        def rows_step(i, carry):
            rows = pl.ds(pl.multiple_of(i * 32, 32), 32)
            states = hv[block, rows, :].astype(F32)
            inverse = lax.rsqrt(jnp.mean(states * states, axis=1, keepdims=True) + EPS)
            there = pl.ds(pl.multiple_of(block * 384 + i * 32, 32), 32)
            nv[there, :] = (states * inverse * gain[...].astype(F32)).astype(BF)
            inv[block, rows, :] = jnp.broadcast_to(inverse, (32, 128))
            return carry

        lax.fori_loop(0, 12, rows_step, 0)

    def c_rows(block, part, k):
        start = pl.multiple_of(block * 384 + part * 192 + k * COT_ROWS, COT_ROWS)
        return cv.at[pl.ds(start, COT_ROWS)]

    def c_send(k):
        start = pl.multiple_of(mp * 192 + k * COT_ROWS, COT_ROWS)
        wires.put(c_e1[k], cot.at[0, pl.ds(start, COT_ROWS)], c_rows(odd, mp, k), info["e1"])

    def c_on(k):
        ref = c_rows(1 - odd, mp, k)
        wires.got(c_e1[k], ref)
        wires.put(c_near[k], ref, ref, info["near"])

    def c_got(k):
        wires.got(c_near[k], c_rows(1 - odd, 1 - mp, k))

    def second(half):
        kind, first = "ab"[half], 2 * half
        ref = one(first, 2, z, mate)
        wires.got(w_e1[half], wv.at[pl.ds(first, 2), z, mate])
        for way in range(2):
            wires.put(w_z[kind][1][way][0], ref, ref, info[ways[way]])
        wires.put(a_e2in[1] if half == 0 else b_e2in[0][0][1], ref, ref, info["e2"])

    def w_hop(kind, hop, way, member):
        place = (x, mate)[member]
        lo, count = span(way, hop, base[kind])
        layer = layer_from(way, hop)
        ref = one(lo, count, layer, place)
        wires.got(w_z[kind][member][way][hop - 1], ref)
        if hop < 4:
            lo, count = span(way, hop + 1, base[kind])
            on = one(lo, count, layer, place)
            wires.put(w_z[kind][member][way][hop], on, on, info[ways[way]])
        if kind == "b":
            wires.put(b_e2in[way][hop][member], ref, ref, info["e2"])

    def a_hop(hop, way, member):
        w_hop("a", hop, way, member)

    def b_hop(hop, way, member):
        w_hop("b", hop, way, member)

    def x_hop(hop, way):
        if hop == 0:
            wires.got(a_e2in[0], one(0, 2, z, 3 - x))
            wires.got(a_e2in[1], one(0, 2, z, 3 - mate))
            ref = other_pair(0, 2, z)
            for each in range(2):
                wires.put(x_z[each][0], ref, ref, info[ways[each]])
            return
        lo, count = span(way, hop, 0)
        layer = layer_from(way, hop)
        wires.got(x_z[way][hop - 1], other_pair(lo, count, layer))
        if hop < 4:
            lo, count = span(way, hop + 1, 0)
            on = other_pair(lo, count, layer)
            wires.put(x_z[way][hop], on, on, info[ways[way]])

    def e2_got(hop, way):
        lo, count = span(way, hop, 2)
        layer = layer_from(way, hop)
        wires.got(b_e2in[way][hop][0], one(lo, count, layer, 3 - x))
        wires.got(b_e2in[way][hop][1], one(lo, count, layer, 3 - mate))

    def project(hop, r):
        here = pl.ds(pl.multiple_of(order[r] * 384, 384), 384)

        def step(way, carry):
            layer = (z + hop + way * (8 - 2 * hop)) % 8
            lanes = pl.ds(pl.multiple_of(layer * 256, 256), 256)
            rows = nv[here, lanes]
            for s in range(1 if r == 2 else 0, 3):
                weight = wv[s, layer].reshape(256, 256)
                term = jnp.dot(rows, weight, preferred_element_type=F32)
                if hop == 0:
                    acc[s, here] = term
                else:
                    acc[s, here] += term
            return carry

        lax.fori_loop(0, 1 if hop in (0, 4) else 2, step, 0)

    def grad_block(block):
        rows = pl.ds(pl.multiple_of(block * 384, 384), 384)
        g_s[rows] = jnp.dot(
            cv[rows], wv[3].reshape(2048, 256), preferred_element_type=F32
        ).astype(BF)

    first_row = (seq - odd) * 3 - 3

    def seg_step(i, carry):
        row = first_row + i
        values = seg[pl.ds(jnp.maximum(row, 0), 1), :].astype(F32)
        values = jnp.where(row < 0, -1.0, values)
        segk[pl.ds(pl.multiple_of(i * 128, 128), 128), :] = jnp.broadcast_to(values, (128, 128)).T
        return carry

    lax.fori_loop(0, 9, seg_step, 0)

    b_hop(1, 0, 0)
    b_hop(1, 1, 0)
    a_hop(1, 0, 0)
    a_hop(1, 1, 0)
    from_near(0)
    b_hop(2, 0, 0)
    b_hop(2, 1, 0)
    from_far(0)
    spread(1)
    a_hop(2, 0, 0)
    a_hop(2, 1, 0)
    second(1)
    b_hop(3, 0, 0)
    b_hop(3, 1, 0)
    a_hop(3, 0, 0)
    a_hop(3, 1, 0)
    from_opp(0)
    second(0)
    b_hop(1, 0, 1)
    b_hop(1, 1, 1)
    from_near(1)
    halo_on()
    spread(2)
    c_send(0)
    c_send(1)
    c_send(2)
    c_send(3)
    a_hop(4, 0, 0)
    a_hop(4, 1, 0)
    a_hop(1, 0, 1)
    a_hop(1, 1, 1)
    b_hop(4, 0, 0)
    b_hop(4, 1, 0)
    c_send(4)
    c_send(5)
    from_far(1)
    e2_got(0, 0)
    b_hop(2, 0, 1)
    b_hop(2, 1, 1)
    from_twin(0)
    a_hop(2, 0, 1)
    a_hop(2, 1, 1)
    from_opp(1)
    x_hop(0, 0)
    project(0, 0)
    e2_got(1, 0)
    c_on(0)
    b_hop(3, 1, 1)
    from_near(2)
    a_hop(3, 0, 1)
    a_hop(3, 1, 1)
    b_hop(3, 0, 1)
    e2_got(1, 1)
    from_far(2)
    c_on(1)
    from_twin(1)
    e2_got(2, 0)
    c_got(0)
    project(0, 1)
    x_hop(1, 0)
    x_hop(1, 1)
    project(1, 1)
    e2_got(2, 1)
    a_hop(4, 0, 1)
    b_hop(4, 1, 1)
    c_on(2)
    project(1, 0)
    b_hop(4, 0, 1)
    a_hop(4, 1, 1)
    e2_got(3, 1)
    from_opp(2)
    c_got(1)
    e2_got(3, 0)
    c_on(3)
    e2_got(4, 1)
    x_hop(2, 0)
    x_hop(2, 1)
    project(2, 0)
    e2_got(4, 0)
    project(2, 1)
    c_got(2)
    c_on(4)
    from_twin(2)
    project(0, 2)
    project(1, 2)
    c_got(3)
    x_hop(3, 0)
    x_hop(3, 1)
    c_on(5)
    project(3, 2)
    project(2, 2)
    project(3, 1)
    project(3, 0)
    c_got(4)
    x_hop(4, 0)
    x_hop(4, 1)
    project(4, 1)
    project(4, 2)
    project(4, 0)
    c_got(5)
    own_c.wait()
    grad_block(odd)
    grad_block(1 - odd)
    wires.finish()
    wires.started = []

    def extract(i, carry):
        rows = pl.ds(pl.multiple_of(i * 128, 128), 128)
        q_s[rows] = (acc[0, rows] * HD**-0.5).astype(BF)
        k_s[rows] = acc[1, rows].astype(BF)
        v_s[rows] = acc[2, rows].astype(BF)
        acc[1, rows] = jnp.zeros((128, 256), F32)
        acc[2, rows] = jnp.zeros((128, 256), F32)
        return carry

    lax.fori_loop(0, 9, extract, 0)
    dqkv[0:384, 0:256] = jnp.zeros((384, 256), BF)
    lane_head = lax.broadcasted_iota(jnp.int32, (128, 256), 1) // HD

    def by_head(rows):
        return jnp.concatenate(
            [jnp.where(lane_head == h, rows, jnp.zeros_like(rows)) for h in range(4)], axis=0
        )

    def fold(wide):
        return jnp.concatenate(
            [wide[h * HD : (h + 1) * HD, h * 128 : (h + 1) * 128] for h in range(4)], axis=0
        ).T

    key_at = lax.broadcasted_iota(jnp.int32, (512, 128), 0)
    query_at = lax.broadcasted_iota(jnp.int32, (512, 128), 1) + 384
    causal = key_at <= query_at

    def tile(t, carry):
        start = pl.multiple_of(t * 128, 128)
        here, window = pl.ds(start, 128), pl.ds(start, 512)
        there = pl.ds(pl.multiple_of(start + 384, 128), 128)
        queries, out_grads = by_head(q_s[there, :]), by_head(g_s[here, :])
        keys, values = k_s[window, :], v_s[window, :]
        own_seg = seg[pl.ds(first_row + 3 + t, 1), :].astype(F32)
        allowed = causal & (segk[window, :] == own_seg)
        allowed = jnp.concatenate([allowed] * 4, axis=1)
        scores = lax.dot_general(keys, queries, NT, preferred_element_type=F32)
        scores = jnp.where(allowed, scores, MASKED)
        expo = jnp.exp(scores - jnp.max(scores, axis=0, keepdims=True))
        probs = expo * (1.0 / jnp.sum(expo, axis=0, keepdims=True))
        prob_rows = probs.astype(BF)
        prob_grad = lax.dot_general(values, out_grads, NT, preferred_element_type=F32)
        delta = jnp.sum(probs * prob_grad, axis=0, keepdims=True)
        score_grad = (probs * (prob_grad - delta)).astype(BF)
        acc[2, window] += jnp.dot(prob_rows, out_grads, preferred_element_type=F32)
        acc[1, window] += jnp.dot(score_grad, queries, preferred_element_type=F32)
        attn[here, :] = fold(
            lax.dot_general(values, prob_rows, TN, preferred_element_type=F32)
        ).astype(BF)
        dqkv[there, 0:256] = (
            fold(lax.dot_general(keys, score_grad, TN, preferred_element_type=F32)) * HD**-0.5
        ).astype(BF)
        return carry

    lax.fori_loop(0, 6, tile, 0)

    def pack(i, carry):
        rows = pl.ds(pl.multiple_of(i * 128, 128), 128)
        dqkv[rows, 256:512] = acc[1, rows].astype(BF)
        dqkv[rows, 512:768] = acc[2, rows].astype(BF)
        return carry

    lax.fori_loop(0, 9, pack, 0)

    a_slot, b_slot = ([slots(4) for _ in range(2)] for _ in range(2))
    b_e2 = slots(8)
    (a_e2,) = slots(1)
    r_e1 = slots(2)
    s_twin = [slots(2) for _ in range(3)]
    s_far1, s_far2, s_near1, s_near2, s_near3 = (slots(3) for _ in range(5))
    s_e1, s_half, s_halo = slots(3)
    blocks = (0, 2 - odd, 1 + odd)
    top, low = pl.ds(0, 192), pl.ds(192, 192)

    def to_layer(way, left):
        return (z + left) % 8 if way == 0 else (z + 8 - left) % 8

    def weight_grads(left, count):
        def step(way, carry):
            layer = (z + left + way * (8 - 2 * left)) % 8
            lanes = pl.ds(pl.multiple_of(layer * 256, 256), 256)
            triple = lax.dot_general(nv[:, lanes], dqkv[...], TN, preferred_element_type=F32)
            for s in range(3):
                grads[s, layer] = triple[:, s * 256 : (s + 1) * 256].astype(BF).reshape(4, 64, 256)
            last = lax.dot_general(cv[:, lanes], attn[...], TN, preferred_element_type=F32)
            grads[3, layer] = last.astype(BF).reshape(4, 64, 256)
            return carry

        lax.fori_loop(0, count, step, 0)

    def cross(k, way, left):
        wires.put(
            b_e2[k],
            grads.at[pl.ds(2, 2), to_layer(way, left), pl.ds(2 - 2 * p, 2)],
            b_e2got.at[k],
            info["e2"],
        )

    def w4():
        weight_grads(4, 1)
        for way in range(2):
            wires.put(
                a_slot[way][0],
                grads.at[pl.ds(way, 1), to_layer(way, 4)],
                a_got.at[way, 0, pl.ds(way, 1)],
                info[ways[way]],
            )
        cross(0, 0, 4)

    def w_part(left):
        weight_grads(left, 2 if left else 1)
        for way in range(2 if left else 1):
            cross(7 - 2 * left + way, way, left)

    def state_grads(r):
        block = blocks[r]
        start = pl.multiple_of(block * 384, 384)
        factor = inv[block, :, 0:1]

        def first(c, carry):
            lanes = pl.ds(pl.multiple_of(c * 256, 256), 256)
            total = None
            for s in range(1 if r == 0 else 0, 3):
                term = lax.dot_general(
                    dqkv[pl.ds(start, 384), s * 256 : (s + 1) * 256],
                    wv[s, c].reshape(256, 256),
                    NT,
                    preferred_element_type=F32,
                )
                total = term if total is None else total + term
            total = total * gain[:, lanes].astype(F32)
            acc[c // 3, pl.ds(pl.multiple_of((c % 3) * 384, 384), 384)] = total
            units = hv[block, :, lanes].astype(F32) * factor
            return carry + jnp.sum(total * units, axis=1, keepdims=True)

        mean = lax.fori_loop(0, 8, first, jnp.zeros((384, 1), F32)) * (1.0 / 2048)
        once = jnp.where(mp == 0, 1.0, 0.0)

        def final(c, carry):
            lanes = pl.ds(pl.multiple_of(c * 256, 256), 256)
            units = hv[block, :, lanes].astype(F32) * factor
            scaled = acc[c // 3, pl.ds(pl.multiple_of((c % 3) * 384, 384), 384)]
            result = factor * (scaled - units * mean)
            if r == 2:
                result = result + cv[own_rows, lanes].astype(F32) * once
            hv[block, :, lanes] = result.astype(BF)
            return carry

        lax.fori_loop(0, 8, final, 0)
        for side in range(2):
            lanes = pl.ds(pl.multiple_of(side * 1024 + (1 - core) * 512, 512), 512)
            wires.put(s_twin[r][side], hv.at[block, :, lanes], t_twin.at[r, side], info["twin"])

    def fold_twin(r):
        for side in (0, 1):
            lanes = pl.ds(pl.multiple_of(side * 1024 + core * 512, 512), 512)
            wires.got(s_twin[r][side], t_twin.at[r, side])
            t_twin[r, side] = add(t_twin[r, side], hv[blocks[r], :, lanes])
        wires.put(s_far1[r], t_twin.at[r, 1 - hi, top], t_far1.at[r], info["far"])
        there = pl.ds(pl.multiple_of((1 - mp) * 256, 256), 256)
        wires.put(s_near1[r], t_twin.at[r, hi, low, there], t_near1.at[r, 0], info["near"])
        there = pl.ds(pl.multiple_of(mp * 256, 256), 256)
        wires.put(s_near3[r], t_twin.at[r, 1 - hi, low, there], t_near1.at[r, 1], info["near"])

    def fold_far(r):
        wires.got(s_far1[r], t_far1.at[r])
        for part in range(2):
            lanes = slice(part * 256, part * 256 + 256)
            t_mid1[r, part] = add(t_twin[r, hi, 0:192, lanes], t_far1[r, :, lanes])
        wires.put(s_near2[r], t_mid1.at[r, 1 - mp], t_near2.at[r], info["near"])

    def fold_near(r):
        wires.got(s_near3[r], t_near1.at[r, 1])
        there = pl.ds(pl.multiple_of((1 - mp) * 256, 256), 256)
        t_mid2[r, 1] = add(t_twin[r, 1 - hi, 192:384, there], t_near1[r, 1])
        wires.put(s_far2[r], t_mid2.at[r, 1], t_far2.at[r], info["far"])
        wires.got(s_near1[r], t_near1.at[r, 0])
        there = pl.ds(pl.multiple_of(mp * 256, 256), 256)
        t_mid2[r, 0] = add(t_twin[r, hi, 192:384, there], t_near1[r, 0])

    def fold_second(r):
        wires.got(s_near2[r], t_near2.at[r])
        t_fin[r, 0:192] = add(t_mid1[r, mp], t_near2[r])
        wires.got(s_far2[r], t_far2.at[r])
        t_fin[r, 192:384] = add(t_mid2[r, 0], t_far2[r])
        if r == 0:
            @pl.when(odd == 1)
            def _():
                pltpu.make_async_remote_copy(
                    src_ref=t_fin.at[0],
                    dst_ref=t_halo,
                    send_sem=send.at[s_half],
                    recv_sem=recv.at[s_half],
                    device_id=info["e1"],
                    device_id_type=MESH,
                ).start()

        if r == 1:
            wires.put(s_e1, t_fin.at[1], t_e1, info["e1"])

    def halo_pass():
        @pl.when(odd == 0)
        def _():
            wires.got(s_half, t_halo)
            t_pass[...] = add(t_fin[0], t_halo[...])
            pltpu.make_async_remote_copy(
                src_ref=t_pass,
                dst_ref=t_halo,
                send_sem=send.at[s_halo],
                recv_sem=recv.at[s_halo],
                device_id=info["halo"],
                device_id_type=MESH,
            ).start()

    def a_step(way, step):
        layer = to_layer(way, 4 - step)
        if step == 1:
            wires.got(a_slot[way][0], a_got.at[way, 0, pl.ds(way, 1)])
            a_got[way, 0, way] = add(grads[way, layer], a_got[way, 0, way])
            a_got[way, 0, 1 - way] = grads[1 - way, layer]
        else:
            wires.got(a_slot[way][step - 1], a_got.at[way, step - 1])
            a_got[way, step - 1] = add(grads[pl.ds(0, 2), layer], a_got[way, step - 1])
        wires.put(a_slot[way][step], a_got.at[way, step - 1], a_got.at[way, step], info[ways[way]])

    def b_start(way, left, k):
        wires.got(b_e2[k], b_e2got.at[k])
        layer = to_layer(way, left)
        return add(grads[pl.ds(2, 2), layer, pl.ds(2 * p, 2)], b_e2got[k])

    def b_begin():
        b_e2got[0] = b_start(0, 4, 0)
        for way in range(2):
            wires.put(
                b_slot[way][0],
                b_e2got.at[0, pl.ds(way, 1)],
                b_got.at[way, 0, pl.ds(way, 1)],
                info[ways[way]],
            )

    def b_step(way, step):
        added = b_start(way, 4 - step, 2 * step - 1 + way)
        if step == 1:
            wires.got(b_slot[way][0], b_got.at[way, 0, pl.ds(way, 1)])
            b_got[way, 0, way] = add(added[way], b_got[way, 0, way])
            b_got[way, 0, 1 - way] = added[1 - way]
        else:
            wires.got(b_slot[way][step - 1], b_got.at[way, step - 1])
            b_got[way, step - 1] = add(added, b_got[way, step - 1])
        wires.put(b_slot[way][step], b_got.at[way, step - 1], b_got.at[way, step], info[ways[way]])

    def a_finish():
        for way in range(2):
            wires.got(a_slot[way][3], a_got.at[way, 3])
        a_fin[...] = add(grads[pl.ds(0, 2), z], a_got[0, 3], a_got[1, 3])
        wires.put(a_e2, a_fin.at[:, pl.ds(2 - 2 * p, 2)], a_e2got, info["e2"])

    def b_finish():
        last = b_start(0, 0, 7)
        for way in range(2):
            wires.got(b_slot[way][3], b_got.at[way, 3])
        w_pair[pl.ds(2, 2)] = add(last, b_got[0, 3], b_got[1, 3])
        wires.put(
            r_e1[1], w_pair.at[pl.ds(2, 2), 1 - odd], w_res.at[q, pl.ds(2, 2)], info["e1"]
        )
        w_res[q, pl.ds(2, 2)] = w_pair[pl.ds(2, 2), odd]

    def a_end():
        wires.got(a_e2, a_e2got)
        w_pair[pl.ds(0, 2)] = add(a_fin[:, pl.ds(2 * p, 2)], a_e2got[...])
        wires.put(
            r_e1[0], w_pair.at[pl.ds(0, 2), 1 - odd], w_res.at[q, pl.ds(0, 2)], info["e1"]
        )
        w_res[q, pl.ds(0, 2)] = w_pair[pl.ds(0, 2), odd]

    def w_end():
        for part in range(2):
            wires.got(r_e1[part], w_res.at[1 - q, pl.ds(2 * part, 2)])
        for half in range(2):
            lanes = slice(half * 256, half * 256 + 256)
            for s in range(3):
                qkv_res[0, s, :, lanes] = w_res[half, s]
            wo_res[0, :, lanes] = w_res[half, 3]

    def t_end():
        wires.got(s_e1, t_e1)

        @pl.when(odd == 0)
        def _():
            t_res[...] = add(t_fin[2], t_e1[...])
            pltpu.make_async_copy(t_pass, t_pass, send.at[s_halo]).wait()

        @pl.when(odd == 1)
        def _():
            wires.got(s_halo, t_halo)
            t_res[...] = add(t_fin[2], t_e1[...], t_halo[...])
            pltpu.make_async_copy(t_halo, t_halo, send.at[s_half]).wait()

    w4()
    w_part(3)
    state_grads(0)
    a_step(1, 1)
    a_step(0, 1)
    b_begin()
    w_part(2)
    fold_twin(0)
    w_part(1)
    state_grads(1)
    a_step(0, 2)
    a_step(1, 2)
    b_step(1, 1)
    b_step(0, 1)
    fold_near(0)
    fold_far(0)
    state_grads(2)
    fold_twin(1)
    fold_second(0)
    w_part(0)
    a_step(0, 3)
    a_step(1, 3)
    fold_twin(2)
    b_step(0, 2)
    b_step(1, 2)
    fold_near(1)
    halo_pass()
    fold_far(1)
    fold_near(2)
    fold_far(2)
    a_finish()
    fold_second(1)
    b_step(0, 3)
    b_step(1, 3)
    fold_second(2)
    a_end()
    b_finish()
    t_end()
    w_end()
    wires.finish()


def hand_over(a_ref, b_ref, c_ref, a_out, b_out, c_out):
    a_out[...] = a_ref[...]
    b_out[...] = b_ref[...]
    c_out[...] = c_ref[...]


def per_device(hidden_states, norm_gain, qkv_weight, out_weight, cotangent, segment_ids):
    anywhere = pl.BlockSpec(memory_space=pl.ANY)
    in_vmem = pl.BlockSpec(memory_space=pltpu.VMEM)
    first = [
        (2, 4, 64, 256), (3, 384, 2048), (1152, 2048), (4, 8, 4, 64, 256), (768, 2048),
    ]
    wide = [(3, 384, 128), (3, 1152, 256)]
    heads = [(1152, 256), (1152, 256), (1152, 256), (768, 256)]
    later = [
        (1152, 768), (768, 256), (4, 8, 4, 64, 256),
        (2, 4, 2, 4, 64, 256), (8, 2, 2, 64, 256), (2, 4, 2, 2, 64, 256),
        (2, 4, 64, 256), (2, 2, 64, 256), (4, 2, 64, 256), (2, 4, 64, 256),
        (3, 2, 384, 512), (3, 192, 512), (3, 192, 256), (3, 2, 192, 256), (3, 192, 256),
        (3, 2, 192, 256), (3, 2, 192, 256),
        (3, 384, 256), (384, 256), (384, 256), (384, 256),
    ]

    def vmem(shapes, dtype):
        return [pltpu.VMEM(shape, dtype) for shape in shapes]

    results = pl.pallas_call(
        kernel,
        out_shape=(
            jax.ShapeDtypeStruct((384, 256), BF),
            jax.ShapeDtypeStruct((1, 3, 64, 512), BF),
            jax.ShapeDtypeStruct((1, 64, 512), BF),
        ),
        in_specs=[anywhere, in_vmem, in_vmem, anywhere, in_vmem, in_vmem],
        out_specs=(in_vmem,) * 3,
        scratch_shapes=vmem(first, BF)
        + vmem(wide, F32)
        + vmem(heads, BF)
        + vmem([(1152, 128)], F32)
        + vmem(later, BF)
        + [
            pltpu.SemaphoreType.DMA((SLOTS,)),
            pltpu.SemaphoreType.DMA((SLOTS,)),
            pltpu.SemaphoreType.DMA((2,)),
        ],
        compiler_params=pltpu.CompilerParams(
            collective_id=0, has_side_effects=True, vmem_limit_bytes=VMEM_LIMIT
        ),
        name="whole",
    )(
        hidden_states,
        jnp.transpose(qkv_weight, (0, 2, 1, 3)),
        out_weight,
        cotangent,
        norm_gain,
        segment_ids.reshape(96, 128),
    )
    trunk_grad, qkv_grad, out_grad = pl.pallas_call(
        hand_over,
        out_shape=tuple(jax.ShapeDtypeStruct(result.shape, BF) for result in results),
        in_specs=[in_vmem] * 3,
        out_specs=(in_vmem,) * 3,
        name="hand_over",
    )(*results)
    return (trunk_grad, jnp.transpose(qkv_grad, (0, 2, 1, 3)), out_grad)


def solution(mesh):
    placed = (
        P("seq", ("head", "mp")),
        P("head", None),
        P("head", "seq", None, "mp"),
        P("head", "seq", "mp"),
        P("head", "seq", None),
        P(),
    )
    return jax.shard_map(
        per_device,
        mesh=mesh,
        in_specs=placed,
        out_specs=(P("seq", ("head", "mp")), P("head", "seq", None, "mp"), P("head", "seq", "mp")),
        check_vma=False,
    )
```

```python
import functools

import jax
import jax.numpy as jnp
from jax import lax
from jax.experimental import pallas as pl
from jax.experimental.pallas import tpu as pltpu
from jax.sharding import PartitionSpec as P

HD = 64
EPS = 1e-05
MASKED = -1e30
MESH = pl.DeviceIdType.MESH
VMEM_LIMIT = 60 * 1024 * 1024
BF = jnp.bfloat16
F32 = jnp.float32


def places():
    head, seq, mp = (lax.axis_index(name) for name in ("head", "seq", "mp"))
    z, x = seq // 4, seq % 4
    odd = x % 2
    info = {
        "head": head,
        "mp": mp,
        "z": z,
        "x": x,
        "odd": odd,
        "pair": x // 2,
        "quarter": ((x + 1) // 2) % 2,
        "core": head % 2,
        "hi": head // 2,
        "e1": (head, seq + 1 - 2 * odd, mp),
        "e2": (head, z * 4 + 3 - x, mp),
        "zp": (head, ((z + 1) % 8) * 4 + x, mp),
        "zm": (head, ((z + 7) % 8) * 4 + x, mp),
        "near": (head, seq, 1 - mp),
        "far": ((head + 2) % 4, seq, 1 - mp),
        "twin": (head + 1 - 2 * (head % 2), seq, mp),
        "halo": (head, (seq + 31 + 2 * odd) % 32, mp),
    }
    return info


def greet(info):
    barrier = pltpu.get_barrier_semaphore()
    names = ("e1", "e2", "zp", "zm", "near", "far", "twin", "halo")
    for name in names:
        pl.semaphore_signal(barrier, inc=1, device_id=info[name], device_id_type=MESH)
    pl.semaphore_wait(barrier, len(names))


class Wires:
    def __init__(self, send, recv):
        self.send, self.recv, self.count = send, recv, 0
        self.started = []

    def slot(self):
        self.count += 1
        return self.count - 1

    def put(self, slot, src, dst, device):
        copy = pltpu.make_async_remote_copy(
            src_ref=src,
            dst_ref=dst,
            send_sem=self.send.at[slot],
            recv_sem=self.recv.at[slot],
            device_id=device,
            device_id_type=MESH,
        )
        copy.start()
        self.started.append((slot, src))

    def got(self, slot, dst):
        pltpu.make_async_copy(dst, dst, self.recv.at[slot]).wait()

    def finish(self):
        for slot, src in self.started:
            pltpu.make_async_copy(src, src, self.send.at[slot]).wait()


NT = (((1,), (1,)), ((), ()))
TN = (((0,), (0,)), ((), ()))
COT_PARTS = 4
COT_ROWS = 192 // COT_PARTS
SLOTS = 160
Q, K, V, O = 2, 3, 0, 1


def add(*terms):
    total = terms[0].astype(F32)
    for term in terms[1:]:
        total = total + term.astype(F32)
    return total.astype(BF)


def kernel(
    hid, qkv, wo, cot, gain, seg,
    t_res, qkv_res, wo_res,
    ws, hv, nv, wv, cv, inv, acc, q_s, k_s, v_s, g_s, segk, means, probs, dqkv, attn, grads,
    a_got, b_e2got, b_got, a_fin, a_e2got, w_pair, w_res,
    t_twin, t_far1, t_far2, t_near1, t_near2, t_mid1, t_mid2, t_fin, t_e1, t_halo, t_pass,
    send, recv, local,
):
    info = places()
    z, x, odd, p, q = (info[name] for name in ("z", "x", "odd", "pair", "quarter"))
    mp, core, hi = info["mp"], info["core"], info["hi"]
    seq = z * 4 + x
    wires = Wires(send, recv)
    ways = ("zp", "zm")
    mate = x + 1 - 2 * odd
    b = 1 + odd
    order = (b, 3 - b, 0)

    def cols(block, head_hi, head_core, part):
        start = pl.multiple_of(((head_hi * 2 + head_core) * 2 + part) * 256, 256)
        return hv.at[block, :, pl.ds(start, 256)]

    own_h = pltpu.make_async_copy(hid, cols(b, hi, core, mp), local.at[0])
    own_h.start()
    own_rows = pl.ds(pl.multiple_of(odd * 384, 384), 384)
    own_c = pltpu.make_async_copy(cot.at[0], cv.at[own_rows], local.at[1])
    own_c.start()
    for half in range(2):
        lanes = slice(half * 256, half * 256 + 256)
        for s in range(3):
            ws[half, (Q, K, V)[s]] = qkv[0, s, :, lanes]
        ws[half, O] = wo[0, :, lanes]
    wv[:, z, x] = ws[q]

    greet(info)

    def slots(count):
        return [wires.slot() for _ in range(count)]

    (w_e1,) = slots(1)
    h_e1, h_halo = slots(2)
    h_near, h_far, h_opp = slots(3), slots(3), slots(3)
    h_twin = [slots(2) for _ in range(3)]
    w_z = [[slots(4) for _ in range(2)] for _ in range(2)]
    x_z = [slots(4) for _ in range(2)]
    first_e2 = slots(2)
    b_e2in = [slots(5) for _ in range(2)]
    c_e1, c_near = slots(COT_PARTS), slots(COT_PARTS)

    def one(first, count, layer, place):
        return wv.at[pl.ds(first, count), layer, pl.ds(place, 1)]

    def other_pair(first, count, layer):
        return wv.at[pl.ds(first, count), layer, pl.ds(2 - 2 * p, 2)]

    def own_pair(first, count, layer):
        return wv.at[pl.ds(first, count), layer, pl.ds(2 * p, 2)]

    def span(way, hop, count):
        return (0, count) if hop < 4 else (way * count // 2, count // 2)

    def layer_from(way, hop):
        return (z + 8 - hop) % 8 if way == 0 else (z + hop) % 8

    mine = cols(b, hi, core, mp)
    halo_own = cols(0, hi, core, mp)
    wires.put(w_e1, ws.at[1 - q], wv.at[:, z, x], info["e1"])
    wires.put(h_e1, hid, mine, info["e1"])
    own_rows_w = ws.at[q]
    own_place = wv.at[:, z, x]
    for way in range(2):
        wires.put(w_z[0][way][0], own_rows_w, own_place, info[ways[way]])
    wires.put(first_e2[0], own_rows_w, own_place, info["e2"])

    @pl.when(odd == 1)
    def _():
        pltpu.make_async_remote_copy(
            src_ref=hid,
            dst_ref=halo_own,
            send_sem=send.at[h_halo],
            recv_sem=recv.at[h_halo],
            device_id=info["halo"],
            device_id_type=MESH,
        ).start()

    def spread(r):
        dst = cols(order[r], hi, core, mp)
        if r == 1:
            wires.got(h_e1, dst)
        src = hid if r == 0 else dst
        wires.put(h_near[r], src, dst, info["near"])
        wires.put(h_far[r], src, dst, info["far"])

    spread(0)

    def half_cols(block, head_hi, head_core):
        start = pl.multiple_of((head_hi * 2 + head_core) * 512, 512)
        return hv.at[block, :, pl.ds(start, 512)]

    def halo_on():
        wires.got(h_halo, halo_own)

        @pl.when(odd == 0)
        def _():
            pltpu.make_async_remote_copy(
                src_ref=halo_own,
                dst_ref=halo_own,
                send_sem=send.at[h_halo],
                recv_sem=recv.at[h_halo],
                device_id=info["e1"],
                device_id_type=MESH,
            ).start()

        wires.started.append((h_halo, hid))

    def from_near(r):
        got = cols(order[r], hi, core, 1 - mp)
        wires.got(h_near[r], got)
        wires.put(h_opp[r], got, got, info["far"])
        if r == 0:
            own_h.wait()
        both = half_cols(order[r], hi, core)
        wires.put(h_twin[r][0], both, both, info["twin"])

    def from_far(r):
        wires.got(h_far[r], cols(order[r], 1 - hi, core, 1 - mp))
        wires.got(h_opp[r], cols(order[r], 1 - hi, core, mp))
        both = half_cols(order[r], 1 - hi, core)
        wires.put(h_twin[r][1], both, both, info["twin"])

    def from_twin(r):
        wires.got(h_twin[r][0], half_cols(order[r], hi, 1 - core))
        wires.got(h_twin[r][1], half_cols(order[r], 1 - hi, 1 - core))
        block = order[r]

        def rows_step(i, carry):
            rows = pl.ds(pl.multiple_of(i * 32, 32), 32)
            states = hv[block, rows, :].astype(F32)
            inverse = lax.rsqrt(jnp.mean(states * states, axis=1, keepdims=True) + EPS)
            there = pl.ds(pl.multiple_of(block * 384 + i * 32, 32), 32)
            nv[there, :] = (states * inverse * gain[...].astype(F32)).astype(BF)
            inv[block, rows, :] = jnp.broadcast_to(inverse, (32, 128))
            return carry

        lax.fori_loop(0, 12, rows_step, 0)

    def c_rows(block, part, k):
        start = pl.multiple_of(block * 384 + part * 192 + k * COT_ROWS, COT_ROWS)
        return cv.at[pl.ds(start, COT_ROWS)]

    def c_send(k):
        start = pl.multiple_of(mp * 192 + k * COT_ROWS, COT_ROWS)
        wires.put(c_e1[k], cot.at[0, pl.ds(start, COT_ROWS)], c_rows(odd, mp, k), info["e1"])

    def c_on(k):
        ref = c_rows(1 - odd, mp, k)
        wires.got(c_e1[k], ref)
        wires.put(c_near[k], ref, ref, info["near"])

    def c_got(k):
        wires.got(c_near[k], c_rows(1 - odd, 1 - mp, k))

    def second():
        ref = wv.at[:, z, mate]
        wires.got(w_e1, ref)
        wires.put(first_e2[1], ref, ref, info["e2"])
        for way in range(2):
            wires.put(w_z[1][way][0], ref, ref, info[ways[way]])

    def w_hop(hop, way, member):
        place = (x, mate)[member]
        layer = layer_from(way, hop)
        lo, count = span(way, hop, 4)
        wires.got(w_z[member][way][hop - 1], one(lo, count, layer, place))
        if hop < 4:
            lo, count = span(way, hop + 1, 4)
            on = one(lo, count, layer, place)
            wires.put(w_z[member][way][hop], on, on, info[ways[way]])
        if member == 1 and (hop < 4 or way == 1):
            ref = own_pair(2, 2, layer)
            wires.put(b_e2in[way][hop], ref, ref, info["e2"])

    def x_hop(hop, way):
        if hop == 0:
            wires.got(first_e2[0], wv.at[:, z, 3 - x])
            wires.got(first_e2[1], wv.at[:, z, 3 - mate])
            ref = other_pair(0, 2, z)
            for each in range(2):
                wires.put(x_z[each][0], ref, ref, info[ways[each]])
            return
        lo, count = span(way, hop, 2)
        layer = layer_from(way, hop)
        wires.got(x_z[way][hop - 1], other_pair(lo, count, layer))
        if hop < 4:
            lo, count = span(way, hop + 1, 2)
            on = other_pair(lo, count, layer)
            wires.put(x_z[way][hop], on, on, info[ways[way]])

    def e2_got(hop, way):
        wires.got(b_e2in[way][hop], other_pair(2, 2, layer_from(way, hop)))

    def project(hop, r):
        here = pl.ds(pl.multiple_of(order[r] * 384, 384), 384)

        def step(way, carry):
            layer = (z + hop + way * (8 - 2 * hop)) % 8
            lanes = pl.ds(pl.multiple_of(layer * 256, 256), 256)
            rows = nv[here, lanes]
            for s in range(1 if r == 2 else 0, 3):
                weight = wv[(Q, K, V)[s], layer].reshape(256, 256)
                term = jnp.dot(rows, weight, preferred_element_type=F32)
                if hop == 0:
                    acc[s, here] = term
                else:
                    acc[s, here] += term
            return carry

        lax.fori_loop(0, 1 if hop in (0, 4) else 2, step, 0)

    def grad_block(block):
        rows = pl.ds(pl.multiple_of(block * 384, 384), 384)
        g_s[rows] = jnp.dot(
            cv[rows], wv[O].reshape(2048, 256), preferred_element_type=F32
        ).astype(BF)

    first_row = (seq - odd) * 3 - 3

    def seg_step(i, carry):
        row = first_row + i
        values = seg[pl.ds(jnp.maximum(row, 0), 1), :].astype(F32)
        values = jnp.where(row < 0, -1.0, values)
        segk[pl.ds(pl.multiple_of(i * 128, 128), 128), :] = jnp.broadcast_to(values, (128, 128)).T
        return carry

    lax.fori_loop(0, 9, seg_step, 0)

    def extract():
        lax.fori_loop(0, 9, extract_step, 0)
        dqkv[0:384, 0:256] = jnp.zeros((384, 256), BF)
        q_s[0:384] = jnp.zeros((384, 256), BF)

    def extract_step(i, carry):
        rows = pl.ds(pl.multiple_of(i * 128, 128), 128)
        q_s[rows] = (acc[0, rows] * HD**-0.5).astype(BF)
        k_s[rows] = acc[1, rows].astype(BF)
        v_s[rows] = acc[2, rows].astype(BF)
        acc[1, rows] = jnp.zeros((128, 256), F32)
        acc[2, rows] = jnp.zeros((128, 256), F32)
        return carry

    lane_head = lax.broadcasted_iota(jnp.int32, (128, 256), 1) // HD

    def by_head(rows):
        return jnp.concatenate(
            [jnp.where(lane_head == h, rows, jnp.zeros_like(rows)) for h in range(4)], axis=0
        )

    def fold(wide):
        return jnp.concatenate(
            [wide[h * HD : (h + 1) * HD, h * 128 : (h + 1) * 128] for h in range(4)], axis=0
        ).T

    key_at = lax.broadcasted_iota(jnp.int32, (512, 128), 0)
    query_at = lax.broadcasted_iota(jnp.int32, (512, 128), 1) + 384
    causal = key_at <= query_at

    def tile_rows(t):
        start = pl.multiple_of(t * 128, 128)
        return (
            pl.ds(start, 128), pl.ds(start, 512), pl.ds(pl.multiple_of(start + 384, 128), 128)
        )

    def tile_front(t, carry):
        here, window, there = tile_rows(t)
        queries = by_head(q_s[there, :])
        keys, values = k_s[window, :], v_s[window, :]
        own_seg = seg[pl.ds(first_row + 3 + t, 1), :].astype(F32)
        allowed = causal & (segk[window, :] == own_seg)
        allowed = jnp.concatenate([allowed] * 4, axis=1)
        scores = lax.dot_general(keys, queries, NT, preferred_element_type=F32)
        scores = jnp.where(allowed, scores, MASKED)
        expo = jnp.exp(scores - jnp.max(scores, axis=0, keepdims=True))
        rows = expo * (1.0 / jnp.sum(expo, axis=0, keepdims=True))
        probs[t] = rows
        prob_rows = rows.astype(BF)
        attn[here, :] = fold(
            lax.dot_general(values, prob_rows, TN, preferred_element_type=F32)
        ).astype(BF)
        return carry

    def tiles_front(low_tile, high_tile):
        def pair(i, carry):
            tile_front(low_tile + 2 * i, 0)
            tile_front(low_tile + 2 * i + 1, 0)
            return carry

        lax.fori_loop(0, (high_tile - low_tile) // 2, pair, 0)

    def tiles_value():
        def value_step(t, carry):
            here, window, there = tile_rows(t)
            acc[2, window] += jnp.dot(
                probs[t].astype(BF), by_head(g_s[here, :]), preferred_element_type=F32
            )
            return carry

        lax.fori_loop(0, 6, value_step, 0)

        def pack_values(i, carry):
            rows = pl.ds(pl.multiple_of(i * 128, 128), 128)
            dqkv[rows, 512:768] = acc[2, rows].astype(BF)
            return carry

        lax.fori_loop(0, 9, pack_values, 0)

    def tile_step(t, carry):
        here, window, there = tile_rows(t)
        queries, out_grads = by_head(q_s[there, :]), by_head(g_s[here, :])
        keys, values = k_s[window, :], v_s[window, :]
        rows = probs[t]
        prob_grad = lax.dot_general(values, out_grads, NT, preferred_element_type=F32)
        delta = jnp.sum(rows * prob_grad, axis=0, keepdims=True)
        score_grad = (rows * (prob_grad - delta)).astype(BF)
        acc[1, window] += jnp.dot(score_grad, queries, preferred_element_type=F32)
        dqkv[there, 0:256] = (
            fold(lax.dot_general(keys, score_grad, TN, preferred_element_type=F32)) * HD**-0.5
        ).astype(BF)
        return carry

    def tiles_back(low_tile, high_tile):
        def pair(i, carry):
            tile_step(low_tile + 2 * i, 0)
            tile_step(low_tile + 2 * i + 1, 0)
            return carry

        pairs = (high_tile - low_tile) // 2
        lax.fori_loop(0, pairs, pair, 0)
        if high_tile - low_tile > 2 * pairs:
            lax.fori_loop(high_tile - 1, high_tile, tile_step, 0)

    def pack():
        def step(i, carry):
            rows = pl.ds(pl.multiple_of(i * 128, 128), 128)
            dqkv[rows, 256:512] = acc[1, rows].astype(BF)
            products = (
                dqkv[rows, 0:256].astype(F32) * q_s[rows].astype(F32) * HD**0.5
                + dqkv[rows, 256:512].astype(F32) * k_s[rows].astype(F32)
                + dqkv[rows, 512:768].astype(F32) * v_s[rows].astype(F32)
            )
            mean = jnp.sum(products, axis=1, keepdims=True) * (1.0 / 2048)
            means[rows] = jnp.broadcast_to(mean, (128, 128))
            return carry

        lax.fori_loop(0, 9, step, 0)

    w_hop(1, 0, 0)
    w_hop(1, 1, 0)
    from_near(0)
    second()
    w_hop(2, 1, 0)
    w_hop(2, 0, 0)
    spread(1)
    w_hop(1, 0, 1)
    x_hop(0, 0)
    w_hop(1, 1, 1)
    halo_on()
    from_near(1)
    c_send(1)
    e2_got(1, 0)
    w_hop(3, 0, 0)
    x_hop(1, 1)
    w_hop(3, 1, 0)
    spread(2)
    w_hop(2, 0, 1)
    from_far(0)
    c_send(0)
    c_send(3)
    e2_got(1, 1)
    c_send(2)
    x_hop(1, 0)
    w_hop(4, 0, 0)
    w_hop(2, 1, 1)
    from_twin(0)
    project(0, 0)
    x_hop(2, 1)
    from_far(1)
    e2_got(2, 0)
    c_on(1)
    w_hop(3, 0, 1)
    w_hop(4, 1, 0)
    from_near(2)
    project(1, 0)
    x_hop(2, 0)
    w_hop(3, 1, 1)
    e2_got(2, 1)
    project(2, 0)
    c_on(0)
    from_twin(1)
    e2_got(3, 0)
    w_hop(4, 0, 1)
    x_hop(3, 1)
    project(0, 1)
    project(1, 1)
    project(2, 1)
    w_hop(4, 1, 1)
    c_got(1)
    from_far(2)
    e2_got(3, 1)
    x_hop(3, 0)
    c_on(3)
    project(3, 0)
    project(3, 1)
    c_got(0)
    from_twin(2)
    x_hop(4, 1)
    e2_got(4, 1)
    x_hop(4, 0)
    project(4, 1)
    project(0, 2)
    c_on(2)
    project(4, 0)
    project(1, 2)
    project(3, 2)
    c_got(3)
    project(4, 2)
    project(2, 2)
    extract()
    own_c.wait()
    grad_block(odd)
    tiles_front(0, 2)
    tiles_front(2, 4)
    c_got(2)
    grad_block(1 - odd)
    tiles_front(4, 6)
    tiles_value()
    front_sends = wires.started
    wires.started = []

    a_slot, b_slot = ([slots(4) for _ in range(2)] for _ in range(2))
    b_e2 = slots(8)
    (a_e2,) = slots(1)
    r_e1 = slots(2)
    s_twin = [slots(2) for _ in range(3)]
    s_far1, s_far2, s_near1, s_near2, s_near3 = (slots(3) for _ in range(5))
    s_e1, s_half, s_halo = slots(3)
    blocks = (0, 2 - odd, 1 + odd)
    top, low = pl.ds(0, 192), pl.ds(192, 192)

    def to_layer(way, left):
        return (z + left) % 8 if way == 0 else (z + 8 - left) % 8

    def layers(left, body):
        def step(way, carry):
            layer = (z + left + way * (8 - 2 * left)) % 8
            body(layer, pl.ds(pl.multiple_of(layer * 256, 256), 256))
            return carry

        lax.fori_loop(0, 1 if left in (0, 4) else 2, step, 0)

    def store(s, layer, value):
        grads[s, layer] = value.astype(BF).reshape(4, 64, 256)

    def qk_grads(layer, lanes):
        pair = lax.dot_general(nv[:, lanes], dqkv[:, 0:512], TN, preferred_element_type=F32)
        store(Q, layer, pair[:, 0:256])
        store(K, layer, pair[:, 256:512])

    def vo_grads(layer, lanes):
        store(
            V,
            layer,
            lax.dot_general(nv[:, lanes], dqkv[:, 512:768], TN, preferred_element_type=F32),
        )
        store(O, layer, lax.dot_general(cv[:, lanes], attn[...], TN, preferred_element_type=F32))

    def cross(k, way, left):
        wires.put(
            b_e2[k],
            grads.at[pl.ds(2, 2), to_layer(way, left), pl.ds(2 - 2 * p, 2)],
            b_e2got.at[k],
            info["e2"],
        )

    def a_part(left):
        layers(left, vo_grads)
        if left == 4:
            for way in range(2):
                wires.put(
                    a_slot[way][0],
                    grads.at[pl.ds(way, 1), to_layer(way, 4)],
                    a_got.at[way, 0, pl.ds(way, 1)],
                    info[ways[way]],
                )

    def b_part(left):
        layers(left, qk_grads)
        if left == 4:
            cross(0, 0, 4)
            return
        for way in range(2 if left else 1):
            cross(7 - 2 * left + way, way, left)

    hidden_slots = {h_e1, h_halo, *h_near, *h_far, *h_opp}.union(*h_twin)

    def settle(sends):
        for slot, src in sends:
            pltpu.make_async_copy(src, src, send.at[slot]).wait()

    def hsettle():
        settle([each for each in front_sends if each[0] in hidden_slots])

    def wsettle():
        settle([each for each in front_sends if each[0] not in hidden_slots])

    def state_grads(r):
        block = blocks[r]
        start = pl.multiple_of(block * 384, 384)
        factor = inv[block, :, 0:1]

        mean = means[pl.ds(start, 384), 0:1]
        once = jnp.where(mp == 0, 1.0, 0.0)

        def final(c, carry):
            lanes = pl.ds(pl.multiple_of(c * 256, 256), 256)
            total = None
            for s in range(1 if r == 0 else 0, 3):
                term = lax.dot_general(
                    dqkv[pl.ds(start, 384), s * 256 : (s + 1) * 256],
                    wv[(Q, K, V)[s], c].reshape(256, 256),
                    NT,
                    preferred_element_type=F32,
                )
                total = term if total is None else total + term
            units = hv[block, :, lanes].astype(F32) * factor
            result = factor * (total * gain[:, lanes].astype(F32) - units * mean)
            if r == 2:
                result = result + cv[own_rows, lanes].astype(F32) * once
            hv[block, :, lanes] = result.astype(BF)
            return carry

        lax.fori_loop(0, 8, final, 0)
        for side in range(2):
            lanes = pl.ds(pl.multiple_of(side * 1024 + (1 - core) * 512, 512), 512)
            wires.put(s_twin[r][side], hv.at[block, :, lanes], t_twin.at[r, side], info["twin"])

    def fold_twin(r):
        for side in (0, 1):
            lanes = pl.ds(pl.multiple_of(side * 1024 + core * 512, 512), 512)
            wires.got(s_twin[r][side], t_twin.at[r, side])
            t_twin[r, side] = add(t_twin[r, side], hv[blocks[r], :, lanes])
        wires.put(s_far1[r], t_twin.at[r, 1 - hi, top], t_far1.at[r], info["far"])
        there = pl.ds(pl.multiple_of((1 - mp) * 256, 256), 256)
        wires.put(s_near1[r], t_twin.at[r, hi, low, there], t_near1.at[r, 0], info["near"])
        there = pl.ds(pl.multiple_of(mp * 256, 256), 256)
        wires.put(s_near3[r], t_twin.at[r, 1 - hi, low, there], t_near1.at[r, 1], info["near"])

    def fold_far(r):
        wires.got(s_far1[r], t_far1.at[r])
        for part in range(2):
            lanes = slice(part * 256, part * 256 + 256)
            t_mid1[r, part] = add(t_twin[r, hi, 0:192, lanes], t_far1[r, :, lanes])
        wires.put(s_near2[r], t_mid1.at[r, 1 - mp], t_near2.at[r], info["near"])

    def fold_near(r):
        wires.got(s_near3[r], t_near1.at[r, 1])
        there = pl.ds(pl.multiple_of((1 - mp) * 256, 256), 256)
        t_mid2[r, 1] = add(t_twin[r, 1 - hi, 192:384, there], t_near1[r, 1])
        wires.put(s_far2[r], t_mid2.at[r, 1], t_far2.at[r], info["far"])
        wires.got(s_near1[r], t_near1.at[r, 0])
        there = pl.ds(pl.multiple_of(mp * 256, 256), 256)
        t_mid2[r, 0] = add(t_twin[r, hi, 192:384, there], t_near1[r, 0])

    def fold_second(r):
        wires.got(s_near2[r], t_near2.at[r])
        t_fin[r, 0:192] = add(t_mid1[r, mp], t_near2[r])
        wires.got(s_far2[r], t_far2.at[r])
        t_fin[r, 192:384] = add(t_mid2[r, 0], t_far2[r])
        if r == 0:
            @pl.when(odd == 1)
            def _():
                pltpu.make_async_remote_copy(
                    src_ref=t_fin.at[0],
                    dst_ref=t_halo,
                    send_sem=send.at[s_half],
                    recv_sem=recv.at[s_half],
                    device_id=info["e1"],
                    device_id_type=MESH,
                ).start()

        if r == 1:
            wires.put(s_e1, t_fin.at[1], t_e1, info["e1"])

    def halo_pass():
        @pl.when(odd == 0)
        def _():
            wires.got(s_half, t_halo)
            t_pass[...] = add(t_fin[0], t_halo[...])
            pltpu.make_async_remote_copy(
                src_ref=t_pass,
                dst_ref=t_halo,
                send_sem=send.at[s_halo],
                recv_sem=recv.at[s_halo],
                device_id=info["halo"],
                device_id_type=MESH,
            ).start()

    def a_step(way, step):
        layer = to_layer(way, 4 - step)
        if step == 1:
            wires.got(a_slot[way][0], a_got.at[way, 0, pl.ds(way, 1)])
            a_got[way, 0, way] = add(grads[way, layer], a_got[way, 0, way])
            a_got[way, 0, 1 - way] = grads[1 - way, layer]
        else:
            wires.got(a_slot[way][step - 1], a_got.at[way, step - 1])
            a_got[way, step - 1] = add(grads[pl.ds(0, 2), layer], a_got[way, step - 1])
        wires.put(a_slot[way][step], a_got.at[way, step - 1], a_got.at[way, step], info[ways[way]])

    def b_start(way, left, k):
        wires.got(b_e2[k], b_e2got.at[k])
        layer = to_layer(way, left)
        return add(grads[pl.ds(2, 2), layer, pl.ds(2 * p, 2)], b_e2got[k])

    def b_begin():
        b_e2got[0] = b_start(0, 4, 0)
        for way in range(2):
            wires.put(
                b_slot[way][0],
                b_e2got.at[0, pl.ds(way, 1)],
                b_got.at[way, 0, pl.ds(way, 1)],
                info[ways[way]],
            )

    def b_step(way, step):
        added = b_start(way, 4 - step, 2 * step - 1 + way)
        if step == 1:
            wires.got(b_slot[way][0], b_got.at[way, 0, pl.ds(way, 1)])
            b_got[way, 0, way] = add(added[way], b_got[way, 0, way])
            b_got[way, 0, 1 - way] = added[1 - way]
        else:
            wires.got(b_slot[way][step - 1], b_got.at[way, step - 1])
            b_got[way, step - 1] = add(added, b_got[way, step - 1])
        wires.put(b_slot[way][step], b_got.at[way, step - 1], b_got.at[way, step], info[ways[way]])

    def a_finish():
        for way in range(2):
            wires.got(a_slot[way][3], a_got.at[way, 3])
        a_fin[...] = add(grads[pl.ds(0, 2), z], a_got[0, 3], a_got[1, 3])
        wires.put(a_e2, a_fin.at[:, pl.ds(2 - 2 * p, 2)], a_e2got, info["e2"])

    def b_finish():
        last = b_start(0, 0, 7)
        for way in range(2):
            wires.got(b_slot[way][3], b_got.at[way, 3])
        w_pair[pl.ds(2, 2)] = add(last, b_got[0, 3], b_got[1, 3])
        wires.put(
            r_e1[1], w_pair.at[pl.ds(2, 2), 1 - odd], w_res.at[q, pl.ds(2, 2)], info["e1"]
        )
        w_res[q, pl.ds(2, 2)] = w_pair[pl.ds(2, 2), odd]

    def a_end():
        wires.got(a_e2, a_e2got)
        w_pair[pl.ds(0, 2)] = add(a_fin[:, pl.ds(2 * p, 2)], a_e2got[...])
        wires.put(
            r_e1[0], w_pair.at[pl.ds(0, 2), 1 - odd], w_res.at[q, pl.ds(0, 2)], info["e1"]
        )
        w_res[q, pl.ds(0, 2)] = w_pair[pl.ds(0, 2), odd]

    def part_settle():
        done = wires.started[:-8]
        wires.started = wires.started[-8:]
        settle(done)

    def w_end():
        for part in range(2):
            wires.got(r_e1[part], w_res.at[1 - q, pl.ds(2 * part, 2)])
        for half in range(2):
            lanes = slice(half * 256, half * 256 + 256)
            for s in range(3):
                qkv_res[0, s, :, lanes] = w_res[half, (Q, K, V)[s]]
            wo_res[0, :, lanes] = w_res[half, O]

    def t_end():
        wires.got(s_e1, t_e1)

        @pl.when(odd == 0)
        def _():
            t_res[...] = add(t_fin[2], t_e1[...])
            pltpu.make_async_copy(t_pass, t_pass, send.at[s_halo]).wait()

        @pl.when(odd == 1)
        def _():
            wires.got(s_halo, t_halo)
            t_res[...] = add(t_fin[2], t_e1[...], t_halo[...])
            pltpu.make_async_copy(t_halo, t_halo, send.at[s_half]).wait()

    a_part(4)
    tiles_back(0, 4)
    a_part(3)
    tiles_back(4, 5)
    a_step(1, 1)
    a_step(0, 1)
    tiles_back(5, 6)
    pack()
    b_part(4)
    hsettle()
    b_part(3)
    state_grads(0)
    a_part(2)
    b_begin()
    a_step(1, 2)
    a_step(0, 2)
    state_grads(1)
    fold_twin(0)
    b_part(2)
    a_part(1)
    b_step(0, 1)
    b_step(1, 1)
    fold_twin(1)
    b_part(1)
    a_step(0, 3)
    a_step(1, 3)
    a_part(0)
    fold_far(0)
    fold_near(0)
    state_grads(2)
    b_step(1, 2)
    b_step(0, 2)
    fold_far(1)
    fold_near(1)
    b_part(0)
    fold_second(0)
    fold_twin(2)
    a_finish()
    fold_second(1)
    wsettle()
    b_step(1, 3)
    b_step(0, 3)
    halo_pass()
    fold_far(2)
    fold_near(2)
    a_end()
    part_settle()
    b_finish()
    fold_second(2)
    t_end()
    w_end()
    wires.finish()


def hand_over(a_ref, b_ref, c_ref, a_out, b_out, c_out):
    a_out[...] = a_ref[...]
    b_out[...] = b_ref[...]
    c_out[...] = c_ref[...]


def per_device(hidden_states, norm_gain, qkv_weight, out_weight, cotangent, segment_ids):
    anywhere = pl.BlockSpec(memory_space=pl.ANY)
    in_vmem = pl.BlockSpec(memory_space=pltpu.VMEM)
    first = [
        (2, 4, 64, 256), (3, 384, 2048), (1152, 2048), (4, 8, 4, 64, 256), (768, 2048),
    ]
    wide = [(3, 384, 128), (3, 1152, 256)]
    heads = [(1152, 256), (1152, 256), (1152, 256), (768, 256)]
    later = [
        (1152, 768), (768, 256), (4, 8, 4, 64, 256),
        (2, 4, 2, 4, 64, 256), (8, 2, 2, 64, 256), (2, 4, 2, 2, 64, 256),
        (2, 4, 64, 256), (2, 2, 64, 256), (4, 2, 64, 256), (2, 4, 64, 256),
        (3, 2, 384, 512), (3, 192, 512), (3, 192, 256), (3, 2, 192, 256), (3, 192, 256),
        (3, 2, 192, 256), (3, 2, 192, 256),
        (3, 384, 256), (384, 256), (384, 256), (384, 256),
    ]

    def vmem(shapes, dtype):
        return [pltpu.VMEM(shape, dtype) for shape in shapes]

    results = pl.pallas_call(
        kernel,
        out_shape=(
            jax.ShapeDtypeStruct((384, 256), BF),
            jax.ShapeDtypeStruct((1, 3, 64, 512), BF),
            jax.ShapeDtypeStruct((1, 64, 512), BF),
        ),
        in_specs=[anywhere, in_vmem, in_vmem, anywhere, in_vmem, in_vmem],
        out_specs=(in_vmem,) * 3,
        scratch_shapes=vmem(first, BF)
        + vmem(wide, F32)
        + vmem(heads, BF)
        + vmem([(1152, 128), (1152, 128), (6, 512, 512)], F32)
        + vmem(later, BF)
        + [
            pltpu.SemaphoreType.DMA((SLOTS,)),
            pltpu.SemaphoreType.DMA((SLOTS,)),
            pltpu.SemaphoreType.DMA((2,)),
        ],
        compiler_params=pltpu.CompilerParams(
            collective_id=0, has_side_effects=True, vmem_limit_bytes=VMEM_LIMIT
        ),
        name="whole",
    )(
        hidden_states,
        jnp.transpose(qkv_weight, (0, 2, 1, 3)),
        out_weight,
        cotangent,
        norm_gain,
        segment_ids.reshape(96, 128),
    )
    trunk_grad, qkv_grad, out_grad = pl.pallas_call(
        hand_over,
        out_shape=tuple(jax.ShapeDtypeStruct(result.shape, BF) for result in results),
        in_specs=[in_vmem] * 3,
        out_specs=(in_vmem,) * 3,
        name="hand_over",
    )(*results)
    return (trunk_grad, jnp.transpose(qkv_grad, (0, 2, 1, 3)), out_grad)


def solution(mesh):
    placed = (
        P("seq", ("head", "mp")),
        P("head", None),
        P("head", "seq", None, "mp"),
        P("head", "seq", "mp"),
        P("head", "seq", None),
        P(),
    )
    return jax.shard_map(
        per_device,
        mesh=mesh,
        in_specs=placed,
        out_specs=(P("seq", ("head", "mp")), P("head", "seq", None, "mp"), P("head", "seq", "mp")),
        check_vma=False,
    )
```

```python
import math

import jax
import jax.numpy as jnp
from jax import lax
from jax.experimental import pallas as pl
from jax.experimental.pallas import tpu as pltpu
from jax.sharding import PartitionSpec as P

HD = 64
EPS = 1e-05
MASKED = -1e30
MESH = pl.DeviceIdType.MESH
VMEM_LIMIT = 60 * 1024 * 1024
BF = jnp.bfloat16
F32 = jnp.float32


def places():
    head, seq, mp = (lax.axis_index(name) for name in ("head", "seq", "mp"))
    z, x = seq // 4, seq % 4
    odd = x % 2
    info = {
        "head": head,
        "mp": mp,
        "z": z,
        "x": x,
        "odd": odd,
        "pair": x // 2,
        "quarter": ((x + 1) // 2) % 2,
        "core": head % 2,
        "hi": head // 2,
        "e1": (head, seq + 1 - 2 * odd, mp),
        "e2": (head, z * 4 + 3 - x, mp),
        "zp": (head, ((z + 1) % 8) * 4 + x, mp),
        "zm": (head, ((z + 7) % 8) * 4 + x, mp),
        "near": (head, seq, 1 - mp),
        "far": ((head + 2) % 4, seq, 1 - mp),
        "twin": (head + 1 - 2 * (head % 2), seq, mp),
        "halo": (head, (seq + 31 + 2 * odd) % 32, mp),
    }
    return info


def greet(info):
    barrier = pltpu.get_barrier_semaphore()
    names = ("e1", "e2", "zp", "zm", "near", "far", "twin", "halo")
    for name in names:
        pl.semaphore_signal(barrier, inc=1, device_id=info[name], device_id_type=MESH)
    pl.semaphore_wait(barrier, len(names))


GROUPS = ("hidden", "weights", "cotangent", "grads", "trunk")


class Wires:
    def __init__(self, send, recv):
        self.send, self.recv, self.count = send, recv, 0
        self.sent = dict.fromkeys(GROUPS, 0)

    def slot(self):
        self.count += 1
        return self.count - 1

    def put(self, group, slot, src, dst, device):
        pltpu.make_async_remote_copy(
            src_ref=src,
            dst_ref=dst,
            send_sem=self.send.at[GROUPS.index(group)],
            recv_sem=self.recv.at[slot],
            device_id=device,
            device_id_type=MESH,
        ).start()
        self.sent[group] += math.prod(src.shape)

    def got(self, slot, dst):
        pltpu.make_async_copy(dst, dst, self.recv.at[slot]).wait()

    def settle(self, group, like):
        rows, rest = divmod(self.sent[group], like.shape[1])
        assert rest == 0 and rows <= like.shape[0]
        ref = like.at[0:rows]
        pltpu.make_async_copy(ref, ref, self.send.at[GROUPS.index(group)]).wait()


NT = (((1,), (1,)), ((), ()))
TN = (((0,), (0,)), ((), ()))
COT_PARTS = 6
COT_ROWS = 192 // COT_PARTS
SLOTS = 200
V, Q, K, O = range(4)
CROSSING = (O, K)


def add(*terms):
    total = terms[0].astype(F32)
    for term in terms[1:]:
        total = total + term.astype(F32)
    return total.astype(BF)


def kernel(
    hid, qkv, wo, cot, gain, seg,
    t_res, qkv_res, wo_res,
    ws, hv, nv, wv, cv, inv, acc, q_s, k_s, v_s, g_s, segk, means, probs, dqkv, attn, grads,
    a_got, b_e2got, b_got, a_fin, a_e2got, w_pair, w_res,
    t_twin, t_far1, t_far2, t_near1, t_near2, t_mid1, t_mid2, t_fin, t_e1, t_halo, t_pass,
    send, recv, local,
):
    info = places()
    z, x, odd, p, q = (info[name] for name in ("z", "x", "odd", "pair", "quarter"))
    mp, core, hi = info["mp"], info["core"], info["hi"]
    seq = z * 4 + x
    wires = Wires(send, recv)
    ways = ("zp", "zm")
    mate = x + 1 - 2 * odd
    b = 1 + odd
    order = (b, 3 - b, 0)

    def cols(block, head_hi, head_core, part):
        start = pl.multiple_of(((head_hi * 2 + head_core) * 2 + part) * 256, 256)
        return hv.at[block, :, pl.ds(start, 256)]

    own_h = pltpu.make_async_copy(hid, cols(b, hi, core, mp), local.at[0])
    own_h.start()
    own_rows = pl.ds(pl.multiple_of(odd * 384, 384), 384)
    own_c = pltpu.make_async_copy(cot.at[0], cv.at[own_rows], local.at[1])
    own_c.start()
    for half in range(2):
        lanes = slice(half * 256, half * 256 + 256)
        for s in range(3):
            ws[half, (Q, K, V)[s]] = qkv[0, s, :, lanes]
        ws[half, O] = wo[0, :, lanes]
    wv[:, z, x] = ws[q]

    greet(info)

    def slots(count):
        return [wires.slot() for _ in range(count)]

    w_e1, o_e1 = slots(2)
    h_e1, h_halo = slots(2)
    h_near, h_far, h_opp = slots(3), slots(3), slots(3)
    h_twin = [slots(2) for _ in range(3)]
    w_z = [[slots(4) for _ in range(2)] for _ in range(2)]
    x_z = [slots(4) for _ in range(2)]
    first_e2 = slots(2)
    b_e2in = [slots(5) for _ in range(2)]
    o_z = [slots(4) for _ in range(2)]
    o_e2in = [slots(5) for _ in range(2)]
    c_e1, c_near = slots(COT_PARTS), slots(COT_PARTS)

    def one(first, count, layer, place):
        return wv.at[pl.ds(first, count), layer, pl.ds(place, 1)]

    def other_pair(first, count, layer):
        return wv.at[pl.ds(first, count), layer, pl.ds(2 - 2 * p, 2)]

    def own_pair(first, count, layer):
        return wv.at[pl.ds(first, count), layer, pl.ds(2 * p, 2)]

    def span(way, hop, count):
        if hop < 4:
            return 0, count
        return ((0, 2), (2, 1))[way] if count == 3 else (way, 1)

    def layer_from(way, hop):
        return (z + 8 - hop) % 8 if way == 0 else (z + hop) % 8

    mine = cols(b, hi, core, mp)
    halo_own = cols(0, hi, core, mp)
    wires.put("weights", w_e1, ws.at[1 - q, 0:3], wv.at[0:3, z, x], info["e1"])
    wires.put("hidden", h_e1, hid, mine, info["e1"])
    own_rows_w = ws.at[q, 0:3]
    own_place = wv.at[0:3, z, x]
    for way in range(2):
        wires.put("weights", w_z[0][way][0], own_rows_w, own_place, info[ways[way]])
    wires.put("weights", first_e2[0], own_rows_w, own_place, info["e2"])

    @pl.when(odd == 1)
    def _():
        pltpu.make_async_remote_copy(
            src_ref=hid,
            dst_ref=halo_own,
            send_sem=send.at[GROUPS.index("hidden")],
            recv_sem=recv.at[h_halo],
            device_id=info["halo"],
            device_id_type=MESH,
        ).start()

    def spread(r):
        dst = cols(order[r], hi, core, mp)
        if r == 1:
            wires.got(h_e1, dst)
        src = hid if r == 0 else dst
        wires.put("hidden", h_near[r], src, dst, info["near"])
        wires.put("hidden", h_far[r], src, dst, info["far"])

    spread(0)
    wires.put("weights", o_e1, ws.at[1 - q, O], wv.at[O, z, x], info["e1"])

    def half_cols(block, head_hi, head_core):
        start = pl.multiple_of((head_hi * 2 + head_core) * 512, 512)
        return hv.at[block, :, pl.ds(start, 512)]

    def halo_on():
        wires.got(h_halo, halo_own)

        @pl.when(odd == 0)
        def _():
            pltpu.make_async_remote_copy(
                src_ref=halo_own,
                dst_ref=halo_own,
                send_sem=send.at[GROUPS.index("hidden")],
                recv_sem=recv.at[h_halo],
                device_id=info["e1"],
                device_id_type=MESH,
            ).start()

        wires.sent["hidden"] += 384 * 256

    def from_near(r):
        got = cols(order[r], hi, core, 1 - mp)
        wires.got(h_near[r], got)
        wires.put("hidden", h_opp[r], got, got, info["far"])
        if r == 0:
            own_h.wait()
        both = half_cols(order[r], hi, core)
        wires.put("hidden", h_twin[r][0], both, both, info["twin"])

    def from_far(r):
        wires.got(h_far[r], cols(order[r], 1 - hi, core, 1 - mp))
        wires.got(h_opp[r], cols(order[r], 1 - hi, core, mp))
        both = half_cols(order[r], 1 - hi, core)
        wires.put("hidden", h_twin[r][1], both, both, info["twin"])

    def from_twin(r):
        wires.got(h_twin[r][0], half_cols(order[r], hi, 1 - core))
        wires.got(h_twin[r][1], half_cols(order[r], 1 - hi, 1 - core))
        block = order[r]

        def rows_step(i, carry):
            rows = pl.ds(pl.multiple_of(i * 32, 32), 32)
            states = hv[block, rows, :].astype(F32)
            inverse = lax.rsqrt(jnp.mean(states * states, axis=1, keepdims=True) + EPS)
            there = pl.ds(pl.multiple_of(block * 384 + i * 32, 32), 32)
            nv[there, :] = (states * inverse * gain[...].astype(F32)).astype(BF)
            inv[block, rows, :] = jnp.broadcast_to(inverse, (32, 128))
            return carry

        lax.fori_loop(0, 12, rows_step, 0)

    def c_rows(block, part, k):
        start = pl.multiple_of(block * 384 + part * 192 + k * COT_ROWS, COT_ROWS)
        return cv.at[pl.ds(start, COT_ROWS)]

    def c_send(k):
        start = pl.multiple_of(mp * 192 + k * COT_ROWS, COT_ROWS)
        wires.put("cotangent", c_e1[k], cot.at[0, pl.ds(start, COT_ROWS)], c_rows(odd, mp, k), info["e1"])

    c_send(0)

    def c_on(k):
        ref = c_rows(1 - odd, mp, k)
        wires.got(c_e1[k], ref)
        wires.put("cotangent", c_near[k], ref, ref, info["near"])

    def c_got(k):
        wires.got(c_near[k], c_rows(1 - odd, 1 - mp, k))

    def second():
        ref = wv.at[0:3, z, mate]
        wires.got(w_e1, ref)
        wires.put("weights", first_e2[1], ref, ref, info["e2"])
        for way in range(2):
            wires.put("weights", w_z[1][way][0], ref, ref, info[ways[way]])

    def w_hop(hop, way, member):
        place = (x, mate)[member]
        layer = layer_from(way, hop)
        lo, count = span(way, hop, 3)
        wires.got(w_z[member][way][hop - 1], one(lo, count, layer, place))
        if hop < 4:
            lo, count = span(way, hop + 1, 3)
            on = one(lo, count, layer, place)
            wires.put("weights", w_z[member][way][hop], on, on, info[ways[way]])
        if member == 1 and (hop < 4 or way == 1):
            ref = own_pair(K, 1, layer)
            wires.put("weights", b_e2in[way][hop], ref, ref, info["e2"])

    def o_second():
        wires.got(o_e1, wv.at[O, z, mate])
        ref = own_pair(O, 1, z)
        for way in range(2):
            wires.put("weights", o_z[way][0], ref, ref, info[ways[way]])
        wires.put("weights", o_e2in[0][0], ref, ref, info["e2"])

    def o_hop(hop, way):
        ref = own_pair(O, 1, layer_from(way, hop))
        wires.got(o_z[way][hop - 1], ref)
        if hop < 3 or (hop == 3 and way == 1):
            wires.put("weights", o_z[way][hop], ref, ref, info[ways[way]])
        wires.put("weights", o_e2in[way][hop], ref, ref, info["e2"])

    def o_got(hop, way):
        wires.got(o_e2in[way][hop], other_pair(O, 1, layer_from(way, hop)))

    def x_hop(hop, way):
        if hop == 0:
            wires.got(first_e2[0], wv.at[0:3, z, 3 - x])
            wires.got(first_e2[1], wv.at[0:3, z, 3 - mate])
            ref = other_pair(0, 2, z)
            for each in range(2):
                wires.put("weights", x_z[each][0], ref, ref, info[ways[each]])
            return
        lo, count = span(way, hop, 2)
        layer = layer_from(way, hop)
        wires.got(x_z[way][hop - 1], other_pair(lo, count, layer))
        if hop < 4:
            lo, count = span(way, hop + 1, 2)
            on = other_pair(lo, count, layer)
            wires.put("weights", x_z[way][hop], on, on, info[ways[way]])

    def e2_got(hop, way):
        wires.got(b_e2in[way][hop], other_pair(K, 1, layer_from(way, hop)))

    def project(hop, r):
        here = pl.ds(pl.multiple_of(order[r] * 384, 384), 384)

        def step(way, carry):
            layer = (z + hop + way * (8 - 2 * hop)) % 8
            lanes = pl.ds(pl.multiple_of(layer * 256, 256), 256)
            rows = nv[here, lanes]
            for s in range(1 if r == 2 else 0, 3):
                weight = wv[(Q, K, V)[s], layer].reshape(256, 256)
                term = jnp.dot(rows, weight, preferred_element_type=F32)
                if hop == 0:
                    acc[s, here] = term
                else:
                    acc[s, here] += term
            return carry

        lax.fori_loop(0, 1 if hop in (0, 4) else 2, step, 0)

    def grad_block(block):
        rows = pl.ds(pl.multiple_of(block * 384, 384), 384)
        g_s[rows] = jnp.dot(
            cv[rows], wv[O].reshape(2048, 256), preferred_element_type=F32
        ).astype(BF)

    first_row = (seq - odd) * 3 - 3

    def seg_step(i, carry):
        row = first_row + i
        values = seg[pl.ds(jnp.maximum(row, 0), 1), :].astype(F32)
        values = jnp.where(row < 0, -1.0, values)
        segk[pl.ds(pl.multiple_of(i * 128, 128), 128), :] = jnp.broadcast_to(values, (128, 128)).T
        return carry

    lax.fori_loop(0, 9, seg_step, 0)

    def extract():
        lax.fori_loop(0, 9, extract_step, 0)
        dqkv[0:384, 0:256] = jnp.zeros((384, 256), BF)
        q_s[0:384] = jnp.zeros((384, 256), BF)

    def extract_step(i, carry):
        rows = pl.ds(pl.multiple_of(i * 128, 128), 128)
        q_s[rows] = (acc[0, rows] * HD**-0.5).astype(BF)
        k_s[rows] = acc[1, rows].astype(BF)
        v_s[rows] = acc[2, rows].astype(BF)
        acc[1, rows] = jnp.zeros((128, 256), F32)
        acc[2, rows] = jnp.zeros((128, 256), F32)
        return carry

    lane_head = lax.broadcasted_iota(jnp.int32, (128, 256), 1) // HD

    def by_head(rows):
        return jnp.concatenate(
            [jnp.where(lane_head == h, rows, jnp.zeros_like(rows)) for h in range(4)], axis=0
        )

    def gather_heads(rows, weights):
        parts = []
        for pair in range(2):
            wide = lax.dot_general(
                rows[:, pair * 128 : (pair + 1) * 128],
                weights[:, pair * 256 : (pair + 1) * 256],
                TN,
                preferred_element_type=F32,
            )
            parts += [wide[0:HD, 0:128], wide[HD : 2 * HD, 128:256]]
        return jnp.concatenate(parts, axis=0).T

    key_at = lax.broadcasted_iota(jnp.int32, (512, 128), 0)
    query_at = lax.broadcasted_iota(jnp.int32, (512, 128), 1) + 384
    causal = key_at <= query_at

    def tile_rows(t):
        start = pl.multiple_of(t * 128, 128)
        return (
            pl.ds(start, 128), pl.ds(start, 512), pl.ds(pl.multiple_of(start + 384, 128), 128)
        )

    def tile_front(t, carry):
        here, window, there = tile_rows(t)
        queries = by_head(q_s[there, :])
        keys, values = k_s[window, :], v_s[window, :]
        own_seg = seg[pl.ds(first_row + 3 + t, 1), :].astype(F32)
        allowed = causal & (segk[window, :] == own_seg)
        allowed = jnp.concatenate([allowed] * 4, axis=1)
        scores = lax.dot_general(keys, queries, NT, preferred_element_type=F32)
        scores = jnp.where(allowed, scores, MASKED)
        expo = jnp.exp(scores - jnp.max(scores, axis=0, keepdims=True))
        rows = expo * (1.0 / jnp.sum(expo, axis=0, keepdims=True))
        prob_rows = rows.astype(BF)
        probs[t] = prob_rows
        attn[here, :] = gather_heads(values, prob_rows).astype(BF)
        return carry

    def unrolled(step, low_tile, high_tile):
        def all_of_them(i, carry):
            for t in range(low_tile, high_tile):
                step(i + t, carry)
            return carry

        lax.fori_loop(0, 1, all_of_them, 0)

    def tiles_front(low_tile, high_tile):
        unrolled(tile_front, low_tile, high_tile)

    def tiles_value():
        def value_step(t, carry):
            here, window, there = tile_rows(t)
            acc[2, window] += jnp.dot(
                probs[t], by_head(g_s[here, :]), preferred_element_type=F32
            )
            return carry

        unrolled(value_step, 0, 6)

        def pack_values(i, carry):
            rows = pl.ds(pl.multiple_of(i * 128, 128), 128)
            dqkv[rows, 512:768] = acc[2, rows].astype(BF)
            return carry

        lax.fori_loop(0, 9, pack_values, 0)

    def tile_step(t, carry):
        here, window, there = tile_rows(t)
        queries, out_grads = by_head(q_s[there, :]), by_head(g_s[here, :])
        keys, values = k_s[window, :], v_s[window, :]
        rows = probs[t].astype(F32)
        prob_grad = lax.dot_general(values, out_grads, NT, preferred_element_type=F32)
        delta = jnp.sum(rows * prob_grad, axis=0, keepdims=True)
        score_grad = (rows * (prob_grad - delta)).astype(BF)
        acc[1, window] += jnp.dot(score_grad, queries, preferred_element_type=F32)
        dqkv[there, 0:256] = (gather_heads(keys, score_grad) * HD**-0.5).astype(BF)
        return carry

    def tiles_back(low_tile, high_tile):
        unrolled(tile_step, low_tile, high_tile)

    def pack():
        def step(i, carry):
            rows = pl.ds(pl.multiple_of(i * 128, 128), 128)
            dqkv[rows, 256:512] = acc[1, rows].astype(BF)
            products = (
                dqkv[rows, 0:256].astype(F32) * q_s[rows].astype(F32) * HD**0.5
                + dqkv[rows, 256:512].astype(F32) * k_s[rows].astype(F32)
                + dqkv[rows, 512:768].astype(F32) * v_s[rows].astype(F32)
            )
            mean = jnp.sum(products, axis=1, keepdims=True) * (1.0 / 2048)
            means[rows] = jnp.broadcast_to(mean, (128, 128))
            return carry

        lax.fori_loop(0, 9, step, 0)

    w_hop(1, 1, 0)
    w_hop(1, 0, 0)
    second()
    from_near(0)
    w_hop(2, 1, 0)
    w_hop(2, 0, 0)
    x_hop(0, 0)
    spread(1)
    w_hop(1, 1, 1)
    o_second()
    w_hop(3, 1, 0)
    w_hop(3, 0, 0)
    from_far(0)
    w_hop(1, 0, 1)
    halo_on()
    from_near(1)
    w_hop(2, 1, 1)
    c_send(2)
    e2_got(1, 0)
    o_got(0, 0)
    e2_got(1, 1)
    c_send(3)
    x_hop(1, 0)
    w_hop(4, 0, 0)
    spread(2)
    o_hop(1, 1)
    o_hop(1, 0)
    w_hop(2, 0, 1)
    w_hop(4, 1, 0)
    c_send(5)
    from_twin(0)
    x_hop(1, 1)
    project(0, 0)
    c_send(4)
    e2_got(2, 1)
    c_send(1)
    w_hop(3, 1, 1)
    c_on(2)
    o_hop(2, 1)
    from_far(1)
    project(1, 0)
    o_got(1, 1)
    x_hop(2, 0)
    o_hop(2, 0)
    from_near(2)
    c_on(3)
    o_got(1, 0)
    c_on(0)
    e2_got(2, 0)
    x_hop(2, 1)
    w_hop(3, 0, 1)
    project(2, 0)
    w_hop(4, 1, 1)
    e2_got(3, 1)
    from_twin(1)
    project(0, 1)
    o_got(2, 1)
    x_hop(3, 0)
    o_hop(3, 1)
    c_on(5)
    project(2, 1)
    project(1, 1)
    c_got(3)
    o_hop(3, 0)
    e2_got(3, 0)
    x_hop(3, 1)
    c_on(4)
    o_got(2, 0)
    project(3, 1)
    from_far(2)
    project(3, 0)
    w_hop(4, 0, 1)
    e2_got(4, 1)
    c_got(0)
    o_got(3, 1)
    c_on(1)
    o_hop(4, 1)
    x_hop(4, 0)
    x_hop(4, 1)
    project(4, 1)
    from_twin(2)
    project(4, 0)
    project(0, 2)
    c_got(5)
    o_got(4, 1)
    o_got(3, 0)
    project(1, 2)
    project(3, 2)
    project(2, 2)
    project(4, 2)
    c_got(4)
    extract()
    own_c.wait()
    grad_block(odd)
    tiles_front(0, 2)
    c_got(1)
    c_got(2)
    tiles_front(2, 4)
    tiles_front(4, 6)
    grad_block(1 - odd)
    tiles_value()

    a_slot, b_slot = ([[slots(4) for _ in range(2)] for _ in range(2)] for _ in range(2))
    b_e2 = [slots(2) for _ in range(8)]
    a_e2 = slots(2)
    r_e1 = [slots(2) for _ in range(2)]
    s_twin = [slots(2) for _ in range(3)]
    s_far1, s_far2, s_near1, s_near2, s_near3 = (slots(3) for _ in range(5))
    s_e1, s_half, s_halo = slots(3)
    blocks = (0, 2 - odd, 1 + odd)
    top, low = pl.ds(0, 192), pl.ds(192, 192)

    def to_layer(way, left):
        return (z + left) % 8 if way == 0 else (z + 8 - left) % 8

    def layers(left, body):
        def step(way, carry):
            layer = (z + left + way * (8 - 2 * left)) % 8
            body(layer, pl.ds(pl.multiple_of(layer * 256, 256), 256))
            return carry

        lax.fori_loop(0, 1 if left in (0, 4) else 2, step, 0)

    def store(s, layer, value):
        grads[s, layer] = value.astype(BF).reshape(4, 64, 256)

    def qk_grads(layer, lanes):
        pair = lax.dot_general(nv[:, lanes], dqkv[:, 0:512], TN, preferred_element_type=F32)
        store(Q, layer, pair[:, 0:256])
        store(K, layer, pair[:, 256:512])

    def vo_grads(layer, lanes):
        store(
            V,
            layer,
            lax.dot_general(nv[:, lanes], dqkv[:, 512:768], TN, preferred_element_type=F32),
        )
        store(O, layer, lax.dot_general(cv[:, lanes], attn[...], TN, preferred_element_type=F32))

    def part(m, left):
        layers(left, (vo_grads, qk_grads)[m])
        if left == 4:
            wires.put("grads",
                a_slot[m][m][0],
                grads.at[m, to_layer(m, 4)],
                a_got.at[m, 0, m],
                info[ways[m]],
            )
        for way in range(1 if left in (0, 4) else 2):
            k = 0 if left == 4 else 7 - 2 * left + way
            wires.put("grads",
                b_e2[k][m],
                grads.at[CROSSING[m], to_layer(way, left), pl.ds(2 - 2 * p, 2)],
                b_e2got.at[k, m],
                info["e2"],
            )

    def early_part(left):
        part(0, left)

    def late_part(left):
        part(1, left)

    def hsettle():
        wires.settle("hidden", nv)

    def wsettle():
        wires.settle("weights", nv)
        wires.settle("cotangent", nv)

    def state_grads(r):
        block = blocks[r]
        start = pl.multiple_of(block * 384, 384)
        factor = inv[block, :, 0:1]

        mean = means[pl.ds(start, 384), 0:1]
        once = jnp.where(mp == 0, 1.0, 0.0)

        def final(c, carry):
            lanes = pl.ds(pl.multiple_of(c * 256, 256), 256)
            total = None
            for s in range(1 if r == 0 else 0, 3):
                term = lax.dot_general(
                    dqkv[pl.ds(start, 384), s * 256 : (s + 1) * 256],
                    wv[(Q, K, V)[s], c].reshape(256, 256),
                    NT,
                    preferred_element_type=F32,
                )
                total = term if total is None else total + term
            units = hv[block, :, lanes].astype(F32) * factor
            result = factor * (total * gain[:, lanes].astype(F32) - units * mean)
            if r == 2:
                result = result + cv[own_rows, lanes].astype(F32) * once
            hv[block, :, lanes] = result.astype(BF)
            return carry

        lax.fori_loop(0, 8, final, 0)
        for side in range(2):
            lanes = pl.ds(pl.multiple_of(side * 1024 + (1 - core) * 512, 512), 512)
            wires.put("trunk", s_twin[r][side], hv.at[block, :, lanes], t_twin.at[r, side], info["twin"])

    def fold_twin(r):
        for side in (0, 1):
            lanes = pl.ds(pl.multiple_of(side * 1024 + core * 512, 512), 512)
            wires.got(s_twin[r][side], t_twin.at[r, side])
            t_twin[r, side] = add(t_twin[r, side], hv[blocks[r], :, lanes])
        wires.put("trunk", s_far1[r], t_twin.at[r, 1 - hi, top], t_far1.at[r], info["far"])
        there = pl.ds(pl.multiple_of((1 - mp) * 256, 256), 256)
        wires.put("trunk", s_near1[r], t_twin.at[r, hi, low, there], t_near1.at[r, 0], info["near"])
        there = pl.ds(pl.multiple_of(mp * 256, 256), 256)
        wires.put("trunk", s_near3[r], t_twin.at[r, 1 - hi, low, there], t_near1.at[r, 1], info["near"])

    def fold_far(r):
        wires.got(s_far1[r], t_far1.at[r])
        for part in range(2):
            lanes = slice(part * 256, part * 256 + 256)
            t_mid1[r, part] = add(t_twin[r, hi, 0:192, lanes], t_far1[r, :, lanes])
        wires.put("trunk", s_near2[r], t_mid1.at[r, 1 - mp], t_near2.at[r], info["near"])

    def fold_near(r):
        wires.got(s_near3[r], t_near1.at[r, 1])
        there = pl.ds(pl.multiple_of((1 - mp) * 256, 256), 256)
        t_mid2[r, 1] = add(t_twin[r, 1 - hi, 192:384, there], t_near1[r, 1])
        wires.put("trunk", s_far2[r], t_mid2.at[r, 1], t_far2.at[r], info["far"])
        wires.got(s_near1[r], t_near1.at[r, 0])
        there = pl.ds(pl.multiple_of(mp * 256, 256), 256)
        t_mid2[r, 0] = add(t_twin[r, hi, 192:384, there], t_near1[r, 0])

    def fold_second(r):
        wires.got(s_near2[r], t_near2.at[r])
        t_fin[r, 0:192] = add(t_mid1[r, mp], t_near2[r])
        wires.got(s_far2[r], t_far2.at[r])
        t_fin[r, 192:384] = add(t_mid2[r, 0], t_far2[r])
        if r == 0:
            @pl.when(odd == 1)
            def _():
                pltpu.make_async_remote_copy(
                    src_ref=t_fin.at[0],
                    dst_ref=t_halo,
                    send_sem=send.at[len(GROUPS)],
                    recv_sem=recv.at[s_half],
                    device_id=info["e1"],
                    device_id_type=MESH,
                ).start()

        if r == 1:
            wires.put("trunk", s_e1, t_fin.at[1], t_e1, info["e1"])

    def halo_pass():
        @pl.when(odd == 0)
        def _():
            wires.got(s_half, t_halo)
            t_pass[...] = add(t_fin[0], t_halo[...])
            pltpu.make_async_remote_copy(
                src_ref=t_pass,
                dst_ref=t_halo,
                send_sem=send.at[len(GROUPS)],
                recv_sem=recv.at[s_halo],
                device_id=info["halo"],
                device_id_type=MESH,
            ).start()

    def a_step(way, step, m):
        layer = to_layer(way, 4 - step)
        on = a_got.at[way, step, m]
        if step == 1 and m != way:
            wires.put("grads", a_slot[m][way][1], grads.at[m, layer], on, info[ways[way]])
            return
        here = a_got.at[way, step - 1, m]
        wires.got(a_slot[m][way][step - 1], here)
        here[...] = add(grads[m, layer], here[...])
        wires.put("grads", a_slot[m][way][step], here, on, info[ways[way]])

    def b_start(way, left, k, m):
        wires.got(b_e2[k][m], b_e2got.at[k, m])
        return add(grads[CROSSING[m], to_layer(way, left), pl.ds(2 * p, 2)], b_e2got[k, m])

    def b_begin(m):
        b_e2got[0, m] = b_start(m, 4, 0, m)
        wires.put("grads", b_slot[m][m][0], b_e2got.at[0, m], b_got.at[m, 0, m], info[ways[m]])

    def b_step(way, step, m):
        k = 2 * step - 1 + way
        added = b_start(way, 4 - step, k, m)
        here = b_got.at[way, step - 1, m]
        if step == 1 and m != way:
            here[...] = added
        else:
            wires.got(b_slot[m][way][step - 1], here)
            here[...] = add(added, here[...])
        wires.put("grads", b_slot[m][way][step], here, b_got.at[way, step, m], info[ways[way]])

    def a_finish(m):
        for way in range(2):
            wires.got(a_slot[m][way][3], a_got.at[way, 3, m])
        a_fin[m] = add(grads[m, z], a_got[0, 3, m], a_got[1, 3, m])
        wires.put("grads", a_e2[m], a_fin.at[m, pl.ds(2 - 2 * p, 2)], a_e2got.at[m], info["e2"])

    def swap(s, m, kind):
        wires.put("grads", r_e1[kind][m], w_pair.at[s, 1 - odd], w_res.at[q, s], info["e1"])
        w_res[q, s] = w_pair[s, odd]

    def b_finish(m):
        last = b_start(0, 0, 7, m)
        for way in range(2):
            wires.got(b_slot[m][way][3], b_got.at[way, 3, m])
        w_pair[CROSSING[m]] = add(last, b_got[0, 3, m], b_got[1, 3, m])
        swap(CROSSING[m], m, 1)

    def a_end(m):
        wires.got(a_e2[m], a_e2got.at[m])
        w_pair[m] = add(a_fin[m, pl.ds(2 * p, 2)], a_e2got[m])
        swap(m, m, 0)

    def w_end():
        for kind in range(2):
            for m in range(2):
                wires.got(r_e1[kind][m], w_res.at[1 - q, (m, CROSSING[m])[kind]])
        for half in range(2):
            lanes = slice(half * 256, half * 256 + 256)
            for s in range(3):
                qkv_res[0, s, :, lanes] = w_res[half, (Q, K, V)[s]]
            wo_res[0, :, lanes] = w_res[half, O]

    def t_end():
        wires.got(s_e1, t_e1)

        @pl.when(odd == 0)
        def _():
            t_res[...] = add(t_fin[2], t_e1[...])
            pltpu.make_async_copy(t_pass, t_pass, send.at[len(GROUPS)]).wait()

        @pl.when(odd == 1)
        def _():
            wires.got(s_halo, t_halo)
            t_res[...] = add(t_fin[2], t_e1[...], t_halo[...])
            pltpu.make_async_copy(t_halo, t_halo, send.at[len(GROUPS)]).wait()

    early_part(4)
    early_part(3)
    a_step(1, 1, 0)
    tiles_back(0, 4)
    a_step(0, 1, 0)
    tiles_back(4, 6)
    pack()
    hsettle()
    late_part(4)
    b_step(1, 1, 0)
    late_part(3)
    state_grads(0)
    b_begin(0)
    a_step(0, 1, 1)
    early_part(2)
    a_step(1, 1, 1)
    state_grads(1)
    fold_twin(0)
    a_step(0, 2, 0)
    a_step(1, 2, 0)
    late_part(2)
    b_step(0, 1, 0)
    b_begin(1)
    b_step(0, 1, 1)
    a_step(0, 2, 1)
    fold_twin(1)
    a_step(1, 2, 1)
    early_part(1)
    a_step(0, 3, 0)
    a_step(1, 3, 0)
    late_part(1)
    fold_far(0)
    b_step(0, 2, 0)
    b_step(1, 1, 1)
    fold_near(0)
    state_grads(2)
    a_step(1, 3, 1)
    a_step(0, 3, 1)
    b_step(0, 2, 1)
    wsettle()
    fold_near(1)
    fold_far(1)
    b_step(1, 2, 0)
    fold_second(0)
    early_part(0)
    fold_twin(2)
    late_part(0)
    b_step(1, 2, 1)
    a_finish(0)
    b_step(0, 3, 0)
    fold_second(1)
    a_finish(1)
    b_step(1, 3, 0)
    halo_pass()
    b_step(0, 3, 1)
    b_step(1, 3, 1)
    fold_far(2)
    fold_near(2)
    a_end(0)
    b_finish(0)
    a_end(1)
    b_finish(1)
    fold_second(2)
    t_end()
    w_end()
    wires.settle("grads", nv)
    wires.settle("trunk", nv)


def hand_over(a_ref, b_ref, c_ref, a_out, b_out, c_out):
    a_out[...] = a_ref[...]
    b_out[...] = b_ref[...]
    c_out[...] = c_ref[...]


def per_device(hidden_states, norm_gain, qkv_weight, out_weight, cotangent, segment_ids):
    anywhere = pl.BlockSpec(memory_space=pl.ANY)
    in_vmem = pl.BlockSpec(memory_space=pltpu.VMEM)
    first = [
        (2, 4, 64, 256), (3, 384, 2048), (1152, 2048), (4, 8, 4, 64, 256), (768, 2048),
    ]
    wide = [(3, 384, 128), (3, 1152, 256)]
    heads = [(1152, 256), (1152, 256), (1152, 256), (768, 256)]
    later = [
        (1152, 768), (768, 256), (4, 8, 4, 64, 256),
        (2, 4, 2, 4, 64, 256), (8, 2, 2, 64, 256), (2, 4, 2, 2, 64, 256),
        (2, 4, 64, 256), (2, 2, 64, 256), (4, 2, 64, 256), (2, 4, 64, 256),
        (3, 2, 384, 512), (3, 192, 512), (3, 192, 256), (3, 2, 192, 256), (3, 192, 256),
        (3, 2, 192, 256), (3, 2, 192, 256),
        (3, 384, 256), (384, 256), (384, 256), (384, 256),
    ]

    def vmem(shapes, dtype):
        return [pltpu.VMEM(shape, dtype) for shape in shapes]

    results = pl.pallas_call(
        kernel,
        out_shape=(
            jax.ShapeDtypeStruct((384, 256), BF),
            jax.ShapeDtypeStruct((1, 3, 64, 512), BF),
            jax.ShapeDtypeStruct((1, 64, 512), BF),
        ),
        in_specs=[anywhere, in_vmem, in_vmem, anywhere, in_vmem, in_vmem],
        out_specs=(in_vmem,) * 3,
        scratch_shapes=vmem(first, BF)
        + vmem(wide, F32)
        + vmem(heads, BF)
        + vmem([(1152, 128), (1152, 128)], F32)
        + vmem([(6, 512, 512)] + later, BF)
        + [
            pltpu.SemaphoreType.DMA((len(GROUPS) + 1,)),
            pltpu.SemaphoreType.DMA((SLOTS,)),
            pltpu.SemaphoreType.DMA((2,)),
        ],
        compiler_params=pltpu.CompilerParams(
            collective_id=0, has_side_effects=True, vmem_limit_bytes=VMEM_LIMIT
        ),
        name="whole",
    )(
        hidden_states,
        jnp.transpose(qkv_weight, (0, 2, 1, 3)),
        out_weight,
        cotangent,
        norm_gain,
        segment_ids.reshape(96, 128),
    )
    trunk_grad, qkv_grad, out_grad = pl.pallas_call(
        hand_over,
        out_shape=tuple(jax.ShapeDtypeStruct(result.shape, BF) for result in results),
        in_specs=[in_vmem] * 3,
        out_specs=(in_vmem,) * 3,
        name="hand_over",
    )(*results)
    return (trunk_grad, jnp.transpose(qkv_grad, (0, 2, 1, 3)), out_grad)


def solution(mesh):
    placed = (
        P("seq", ("head", "mp")),
        P("head", None),
        P("head", "seq", None, "mp"),
        P("head", "seq", "mp"),
        P("head", "seq", None),
        P(),
    )
    return jax.shard_map(
        per_device,
        mesh=mesh,
        in_specs=placed,
        out_specs=(P("seq", ("head", "mp")), P("head", "seq", None, "mp"), P("head", "seq", "mp")),
        check_vma=False,
    )
```

```python
import math

import jax
import jax.numpy as jnp
from jax import lax
from jax.experimental import pallas as pl
from jax.experimental.pallas import tpu as pltpu
from jax.sharding import PartitionSpec as P

HD = 64
EPS = 1e-05
MASKED = -1e30
MESH = pl.DeviceIdType.MESH
VMEM_LIMIT = 60 * 1024 * 1024
BF = jnp.bfloat16
F32 = jnp.float32


def places():
    head, seq, mp = (lax.axis_index(name) for name in ("head", "seq", "mp"))
    z, x = seq // 4, seq % 4
    odd = x % 2
    info = {
        "head": head,
        "mp": mp,
        "z": z,
        "x": x,
        "odd": odd,
        "pair": x // 2,
        "quarter": ((x + 1) // 2) % 2,
        "core": head % 2,
        "hi": head // 2,
        "e1": (head, seq + 1 - 2 * odd, mp),
        "e2": (head, z * 4 + 3 - x, mp),
        "zp": (head, ((z + 1) % 8) * 4 + x, mp),
        "zm": (head, ((z + 7) % 8) * 4 + x, mp),
        "near": (head, seq, 1 - mp),
        "far": ((head + 2) % 4, seq, 1 - mp),
        "twin": (head + 1 - 2 * (head % 2), seq, mp),
        "halo": (head, (seq + 31 + 2 * odd) % 32, mp),
    }
    return info


def greet(info):
    barrier = pltpu.get_barrier_semaphore()
    names = ("e1", "e2", "zp", "zm", "near", "far", "twin", "halo")
    for name in names:
        pl.semaphore_signal(barrier, inc=1, device_id=info[name], device_id_type=MESH)
    pl.semaphore_wait(barrier, len(names))


GROUPS = ("hidden", "weights", "cotangent", "grads", "trunk")


class Wires:
    def __init__(self, send, recv):
        self.send, self.recv, self.count = send, recv, 0
        self.sent = dict.fromkeys(GROUPS, 0)

    def slot(self):
        self.count += 1
        return self.count - 1

    def put(self, group, slot, src, dst, device):
        pltpu.make_async_remote_copy(
            src_ref=src,
            dst_ref=dst,
            send_sem=self.send.at[GROUPS.index(group)],
            recv_sem=self.recv.at[slot],
            device_id=device,
            device_id_type=MESH,
        ).start()
        self.sent[group] += math.prod(src.shape)

    def got(self, slot, dst):
        pltpu.make_async_copy(dst, dst, self.recv.at[slot]).wait()

    def settle(self, group, like):
        rows, rest = divmod(self.sent[group], like.shape[1])
        assert rest == 0 and rows <= like.shape[0]
        ref = like.at[0:rows]
        pltpu.make_async_copy(ref, ref, self.send.at[GROUPS.index(group)]).wait()


NT = (((1,), (1,)), ((), ()))
TN = (((0,), (0,)), ((), ()))
COT_PARTS = 6
COT_ROWS = 192 // COT_PARTS
SLOTS = 180
Q, K, V, O = 1, 3, 0, 2


def add(*terms):
    total = terms[0].astype(F32)
    for term in terms[1:]:
        total = total + term.astype(F32)
    return total.astype(BF)


def kernel(
    hid, qkv, wo, cot, gain, seg,
    t_res, qkv_res, wo_res,
    ws, hv, nv, wv, cv, inv, acc, q_s, k_s, v_s, g_s, segk, means, probs, dqkv, attn, grads,
    a_got, b_e2got, b_got, a_fin, a_e2got, w_pair, w_res,
    t_twin, t_far1, t_far2, t_near1, t_near2, t_mid1, t_mid2, t_fin, t_e1, t_halo, t_pass,
    send, recv, local,
):
    info = places()
    z, x, odd, p, q = (info[name] for name in ("z", "x", "odd", "pair", "quarter"))
    mp, core, hi = info["mp"], info["core"], info["hi"]
    seq = z * 4 + x
    wires = Wires(send, recv)
    ways = ("zp", "zm")
    mate = x + 1 - 2 * odd
    b = 1 + odd
    order = (b, 3 - b, 0)

    def cols(block, head_hi, head_core, part):
        start = pl.multiple_of(((head_hi * 2 + head_core) * 2 + part) * 256, 256)
        return hv.at[block, :, pl.ds(start, 256)]

    own_h = pltpu.make_async_copy(hid, cols(b, hi, core, mp), local.at[0])
    own_h.start()
    own_rows = pl.ds(pl.multiple_of(odd * 384, 384), 384)
    own_c = pltpu.make_async_copy(cot.at[0], cv.at[own_rows], local.at[1])
    own_c.start()
    for half in range(2):
        lanes = slice(half * 256, half * 256 + 256)
        for s in range(3):
            ws[half, (Q, K, V)[s]] = qkv[0, s, :, lanes]
        ws[half, O] = wo[0, :, lanes]
    wv[:, z, x] = ws[q]

    greet(info)

    def slots(count):
        return [wires.slot() for _ in range(count)]

    (w_e1,) = slots(1)
    h_e1, h_halo = slots(2)
    h_near, h_far, h_opp = slots(3), slots(3), slots(3)
    h_twin = [slots(2) for _ in range(3)]
    w_z = [[slots(4) for _ in range(2)] for _ in range(2)]
    x_z = [slots(4) for _ in range(2)]
    first_e2 = slots(2)
    b_e2in = [slots(5) for _ in range(2)]
    c_e1, c_near = slots(COT_PARTS), slots(COT_PARTS)

    def one(first, count, layer, place):
        return wv.at[pl.ds(first, count), layer, pl.ds(place, 1)]

    def other_pair(first, count, layer):
        return wv.at[pl.ds(first, count), layer, pl.ds(2 - 2 * p, 2)]

    def own_pair(first, count, layer):
        return wv.at[pl.ds(first, count), layer, pl.ds(2 * p, 2)]

    def span(way, hop, count):
        return (0, count) if hop < 4 else (way * count // 2, count // 2)

    def layer_from(way, hop):
        return (z + 8 - hop) % 8 if way == 0 else (z + hop) % 8

    mine = cols(b, hi, core, mp)
    halo_own = cols(0, hi, core, mp)
    wires.put("weights", w_e1, ws.at[1 - q], wv.at[:, z, x], info["e1"])
    wires.put("hidden", h_e1, hid, mine, info["e1"])
    own_rows_w = ws.at[q]
    own_place = wv.at[:, z, x]
    for way in range(2):
        wires.put("weights", w_z[0][way][0], own_rows_w, own_place, info[ways[way]])
    wires.put("weights", first_e2[0], own_rows_w, own_place, info["e2"])

    @pl.when(odd == 1)
    def _():
        pltpu.make_async_remote_copy(
            src_ref=hid,
            dst_ref=halo_own,
            send_sem=send.at[GROUPS.index("hidden")],
            recv_sem=recv.at[h_halo],
            device_id=info["halo"],
            device_id_type=MESH,
        ).start()

    def spread(r):
        dst = cols(order[r], hi, core, mp)
        if r == 1:
            wires.got(h_e1, dst)
        src = hid if r == 0 else dst
        wires.put("hidden", h_near[r], src, dst, info["near"])
        wires.put("hidden", h_far[r], src, dst, info["far"])

    spread(0)

    def half_cols(block, head_hi, head_core):
        start = pl.multiple_of((head_hi * 2 + head_core) * 512, 512)
        return hv.at[block, :, pl.ds(start, 512)]

    def halo_on():
        wires.got(h_halo, halo_own)

        @pl.when(odd == 0)
        def _():
            pltpu.make_async_remote_copy(
                src_ref=halo_own,
                dst_ref=halo_own,
                send_sem=send.at[GROUPS.index("hidden")],
                recv_sem=recv.at[h_halo],
                device_id=info["e1"],
                device_id_type=MESH,
            ).start()

        wires.sent["hidden"] += 384 * 256

    def from_near(r):
        got = cols(order[r], hi, core, 1 - mp)
        wires.got(h_near[r], got)
        wires.put("hidden", h_opp[r], got, got, info["far"])
        if r == 0:
            own_h.wait()
        both = half_cols(order[r], hi, core)
        wires.put("hidden", h_twin[r][0], both, both, info["twin"])

    def from_far(r):
        wires.got(h_far[r], cols(order[r], 1 - hi, core, 1 - mp))
        wires.got(h_opp[r], cols(order[r], 1 - hi, core, mp))
        both = half_cols(order[r], 1 - hi, core)
        wires.put("hidden", h_twin[r][1], both, both, info["twin"])

    def from_twin(r):
        wires.got(h_twin[r][0], half_cols(order[r], hi, 1 - core))
        wires.got(h_twin[r][1], half_cols(order[r], 1 - hi, 1 - core))
        block = order[r]

        def rows_step(i, carry):
            rows = pl.ds(pl.multiple_of(i * 32, 32), 32)
            states = hv[block, rows, :].astype(F32)
            inverse = lax.rsqrt(jnp.mean(states * states, axis=1, keepdims=True) + EPS)
            there = pl.ds(pl.multiple_of(block * 384 + i * 32, 32), 32)
            nv[there, :] = (states * inverse * gain[...].astype(F32)).astype(BF)
            inv[block, rows, :] = jnp.broadcast_to(inverse, (32, 128))
            return carry

        lax.fori_loop(0, 12, rows_step, 0)

    def c_rows(block, part, k):
        start = pl.multiple_of(block * 384 + part * 192 + k * COT_ROWS, COT_ROWS)
        return cv.at[pl.ds(start, COT_ROWS)]

    def c_send(k):
        start = pl.multiple_of(mp * 192 + k * COT_ROWS, COT_ROWS)
        wires.put("cotangent", c_e1[k], cot.at[0, pl.ds(start, COT_ROWS)], c_rows(odd, mp, k), info["e1"])

    c_send(0)

    def c_on(k):
        ref = c_rows(1 - odd, mp, k)
        wires.got(c_e1[k], ref)
        wires.put("cotangent", c_near[k], ref, ref, info["near"])

    def c_got(k):
        wires.got(c_near[k], c_rows(1 - odd, 1 - mp, k))

    def second():
        ref = wv.at[:, z, mate]
        wires.got(w_e1, ref)
        wires.put("weights", first_e2[1], ref, ref, info["e2"])
        for way in range(2):
            wires.put("weights", w_z[1][way][0], ref, ref, info[ways[way]])

    def w_hop(hop, way, member):
        place = (x, mate)[member]
        layer = layer_from(way, hop)
        lo, count = span(way, hop, 4)
        wires.got(w_z[member][way][hop - 1], one(lo, count, layer, place))
        if hop < 4:
            lo, count = span(way, hop + 1, 4)
            on = one(lo, count, layer, place)
            wires.put("weights", w_z[member][way][hop], on, on, info[ways[way]])
        if member == 1 and (hop < 4 or way == 1):
            ref = own_pair(2, 2, layer)
            wires.put("weights", b_e2in[way][hop], ref, ref, info["e2"])

    def x_hop(hop, way):
        if hop == 0:
            wires.got(first_e2[0], wv.at[:, z, 3 - x])
            wires.got(first_e2[1], wv.at[:, z, 3 - mate])
            ref = other_pair(0, 2, z)
            for each in range(2):
                wires.put("weights", x_z[each][0], ref, ref, info[ways[each]])
            return
        lo, count = span(way, hop, 2)
        layer = layer_from(way, hop)
        wires.got(x_z[way][hop - 1], other_pair(lo, count, layer))
        if hop < 4:
            lo, count = span(way, hop + 1, 2)
            on = other_pair(lo, count, layer)
            wires.put("weights", x_z[way][hop], on, on, info[ways[way]])

    def e2_got(hop, way):
        wires.got(b_e2in[way][hop], other_pair(2, 2, layer_from(way, hop)))

    def project(hop, r):
        here = pl.ds(pl.multiple_of(order[r] * 384, 384), 384)

        def step(way, carry):
            layer = (z + hop + way * (8 - 2 * hop)) % 8
            lanes = pl.ds(pl.multiple_of(layer * 256, 256), 256)
            rows = nv[here, lanes]
            for s in range(1 if r == 2 else 0, 3):
                weight = wv[(Q, K, V)[s], layer].reshape(256, 256)
                term = jnp.dot(rows, weight, preferred_element_type=F32)
                if hop == 0:
                    acc[s, here] = term
                else:
                    acc[s, here] += term
            return carry

        lax.fori_loop(0, 1 if hop in (0, 4) else 2, step, 0)

    def grad_block(block):
        rows = pl.ds(pl.multiple_of(block * 384, 384), 384)
        g_s[rows] = jnp.dot(
            cv[rows], wv[O].reshape(2048, 256), preferred_element_type=F32
        ).astype(BF)

    first_row = (seq - odd) * 3 - 3

    def seg_step(i, carry):
        row = first_row + i
        values = seg[pl.ds(jnp.maximum(row, 0), 1), :].astype(F32)
        values = jnp.where(row < 0, -1.0, values)
        segk[pl.ds(pl.multiple_of(i * 128, 128), 128), :] = jnp.broadcast_to(values, (128, 128)).T
        return carry

    lax.fori_loop(0, 9, seg_step, 0)

    def extract():
        lax.fori_loop(0, 9, extract_step, 0)
        dqkv[0:384, 0:256] = jnp.zeros((384, 256), BF)
        q_s[0:384] = jnp.zeros((384, 256), BF)

    def extract_step(i, carry):
        rows = pl.ds(pl.multiple_of(i * 128, 128), 128)
        q_s[rows] = (acc[0, rows] * HD**-0.5).astype(BF)
        k_s[rows] = acc[1, rows].astype(BF)
        v_s[rows] = acc[2, rows].astype(BF)
        acc[1, rows] = jnp.zeros((128, 256), F32)
        acc[2, rows] = jnp.zeros((128, 256), F32)
        return carry

    lane_head = lax.broadcasted_iota(jnp.int32, (128, 256), 1) // HD

    def by_head(rows):
        return jnp.concatenate(
            [jnp.where(lane_head == h, rows, jnp.zeros_like(rows)) for h in range(4)], axis=0
        )

    def fold(wide):
        return jnp.concatenate(
            [wide[h * HD : (h + 1) * HD, h * 128 : (h + 1) * 128] for h in range(4)], axis=0
        ).T

    key_at = lax.broadcasted_iota(jnp.int32, (512, 128), 0)
    query_at = lax.broadcasted_iota(jnp.int32, (512, 128), 1) + 384
    causal = key_at <= query_at

    def tile_rows(t):
        start = pl.multiple_of(t * 128, 128)
        return (
            pl.ds(start, 128), pl.ds(start, 512), pl.ds(pl.multiple_of(start + 384, 128), 128)
        )

    def tile_front(t, carry):
        here, window, there = tile_rows(t)
        queries = by_head(q_s[there, :])
        keys, values = k_s[window, :], v_s[window, :]
        own_seg = seg[pl.ds(first_row + 3 + t, 1), :].astype(F32)
        allowed = causal & (segk[window, :] == own_seg)
        allowed = jnp.concatenate([allowed] * 4, axis=1)
        scores = lax.dot_general(keys, queries, NT, preferred_element_type=F32)
        scores = jnp.where(allowed, scores, MASKED)
        expo = jnp.exp(scores - jnp.max(scores, axis=0, keepdims=True))
        rows = expo * (1.0 / jnp.sum(expo, axis=0, keepdims=True))
        prob_rows = rows.astype(BF)
        probs[t] = prob_rows
        attn[here, :] = fold(
            lax.dot_general(values, prob_rows, TN, preferred_element_type=F32)
        ).astype(BF)
        return carry

    def tiles_front(low_tile, high_tile):
        def pair(i, carry):
            tile_front(low_tile + 2 * i, 0)
            tile_front(low_tile + 2 * i + 1, 0)
            return carry

        lax.fori_loop(0, (high_tile - low_tile) // 2, pair, 0)

    def tiles_value():
        def value_step(t, carry):
            here, window, there = tile_rows(t)
            acc[2, window] += jnp.dot(
                probs[t], by_head(g_s[here, :]), preferred_element_type=F32
            )
            return carry

        lax.fori_loop(0, 6, value_step, 0)

        def pack_values(i, carry):
            rows = pl.ds(pl.multiple_of(i * 128, 128), 128)
            dqkv[rows, 512:768] = acc[2, rows].astype(BF)
            return carry

        lax.fori_loop(0, 9, pack_values, 0)

    def tile_step(t, carry):
        here, window, there = tile_rows(t)
        queries, out_grads = by_head(q_s[there, :]), by_head(g_s[here, :])
        keys, values = k_s[window, :], v_s[window, :]
        rows = probs[t].astype(F32)
        prob_grad = lax.dot_general(values, out_grads, NT, preferred_element_type=F32)
        delta = jnp.sum(rows * prob_grad, axis=0, keepdims=True)
        score_grad = (rows * (prob_grad - delta)).astype(BF)
        acc[1, window] += jnp.dot(score_grad, queries, preferred_element_type=F32)
        dqkv[there, 0:256] = (
            fold(lax.dot_general(keys, score_grad, TN, preferred_element_type=F32)) * HD**-0.5
        ).astype(BF)
        return carry

    def tiles_back(low_tile, high_tile):
        def pair(i, carry):
            tile_step(low_tile + 2 * i, 0)
            tile_step(low_tile + 2 * i + 1, 0)
            return carry

        pairs = (high_tile - low_tile) // 2
        lax.fori_loop(0, pairs, pair, 0)
        if high_tile - low_tile > 2 * pairs:
            lax.fori_loop(high_tile - 1, high_tile, tile_step, 0)

    def pack():
        def step(i, carry):
            rows = pl.ds(pl.multiple_of(i * 128, 128), 128)
            dqkv[rows, 256:512] = acc[1, rows].astype(BF)
            products = (
                dqkv[rows, 0:256].astype(F32) * q_s[rows].astype(F32) * HD**0.5
                + dqkv[rows, 256:512].astype(F32) * k_s[rows].astype(F32)
                + dqkv[rows, 512:768].astype(F32) * v_s[rows].astype(F32)
            )
            mean = jnp.sum(products, axis=1, keepdims=True) * (1.0 / 2048)
            means[rows] = jnp.broadcast_to(mean, (128, 128))
            return carry

        lax.fori_loop(0, 9, step, 0)

    w_hop(1, 1, 0)
    w_hop(1, 0, 0)
    second()
    from_near(0)
    w_hop(2, 0, 0)
    w_hop(2, 1, 0)
    spread(1)
    w_hop(1, 0, 1)
    w_hop(1, 1, 1)
    x_hop(0, 0)
    halo_on()
    from_near(1)
    e2_got(1, 0)
    c_send(5)
    w_hop(2, 0, 1)
    w_hop(3, 1, 0)
    from_far(0)
    c_send(1)
    spread(2)
    c_send(3)
    c_send(2)
    c_on(0)
    w_hop(2, 1, 1)
    e2_got(1, 1)
    c_send(4)
    x_hop(1, 0)
    w_hop(3, 0, 0)
    x_hop(1, 1)
    from_twin(0)
    c_on(5)
    w_hop(3, 0, 1)
    e2_got(2, 0)
    w_hop(4, 1, 0)
    project(0, 0)
    from_far(1)
    w_hop(3, 1, 1)
    project(1, 0)
    x_hop(2, 0)
    e2_got(2, 1)
    from_near(2)
    from_twin(1)
    x_hop(2, 1)
    w_hop(4, 0, 0)
    project(0, 1)
    c_got(0)
    c_on(3)
    c_on(1)
    w_hop(4, 1, 1)
    project(2, 1)
    e2_got(3, 0)
    w_hop(4, 0, 1)
    project(2, 0)
    project(1, 1)
    c_got(5)
    c_on(2)
    x_hop(3, 0)
    from_far(2)
    e2_got(3, 1)
    x_hop(3, 1)
    project(3, 0)
    project(3, 1)
    e2_got(4, 1)
    c_got(3)
    c_on(4)
    from_twin(2)
    x_hop(4, 0)
    x_hop(4, 1)
    c_got(1)
    project(4, 0)
    project(4, 1)
    project(0, 2)
    project(2, 2)
    project(4, 2)
    project(3, 2)
    c_got(2)
    project(1, 2)
    extract()
    own_c.wait()
    grad_block(odd)
    tiles_front(0, 2)
    c_got(4)
    grad_block(1 - odd)
    tiles_front(2, 4)
    tiles_front(4, 6)
    tiles_value()

    a_slot, b_slot = ([[slots(4) for _ in range(2)] for _ in range(2)] for _ in range(2))
    b_e2 = [slots(2) for _ in range(8)]
    a_e2 = slots(2)
    r_e1 = [slots(2) for _ in range(2)]
    s_twin = [slots(2) for _ in range(3)]
    s_far1, s_far2, s_near1, s_near2, s_near3 = (slots(3) for _ in range(5))
    s_e1, s_half, s_halo = slots(3)
    blocks = (0, 2 - odd, 1 + odd)
    top, low = pl.ds(0, 192), pl.ds(192, 192)

    def to_layer(way, left):
        return (z + left) % 8 if way == 0 else (z + 8 - left) % 8

    def layers(left, body):
        def step(way, carry):
            layer = (z + left + way * (8 - 2 * left)) % 8
            body(layer, pl.ds(pl.multiple_of(layer * 256, 256), 256))
            return carry

        lax.fori_loop(0, 1 if left in (0, 4) else 2, step, 0)

    def store(s, layer, value):
        grads[s, layer] = value.astype(BF).reshape(4, 64, 256)

    def qk_grads(layer, lanes):
        pair = lax.dot_general(nv[:, lanes], dqkv[:, 0:512], TN, preferred_element_type=F32)
        store(Q, layer, pair[:, 0:256])
        store(K, layer, pair[:, 256:512])

    def vo_grads(layer, lanes):
        store(
            V,
            layer,
            lax.dot_general(nv[:, lanes], dqkv[:, 512:768], TN, preferred_element_type=F32),
        )
        store(O, layer, lax.dot_general(cv[:, lanes], attn[...], TN, preferred_element_type=F32))

    def part(m, left):
        layers(left, (vo_grads, qk_grads)[m])
        if left == 4:
            wires.put("grads",
                a_slot[m][m][0],
                grads.at[m, to_layer(m, 4)],
                a_got.at[m, 0, m],
                info[ways[m]],
            )
        for way in range(1 if left in (0, 4) else 2):
            k = 0 if left == 4 else 7 - 2 * left + way
            wires.put("grads",
                b_e2[k][m],
                grads.at[2 + m, to_layer(way, left), pl.ds(2 - 2 * p, 2)],
                b_e2got.at[k, m],
                info["e2"],
            )

    def early_part(left):
        part(0, left)

    def late_part(left):
        part(1, left)

    def hsettle():
        wires.settle("hidden", nv)

    def wsettle():
        wires.settle("weights", nv)
        wires.settle("cotangent", nv)

    def state_grads(r):
        block = blocks[r]
        start = pl.multiple_of(block * 384, 384)
        factor = inv[block, :, 0:1]

        mean = means[pl.ds(start, 384), 0:1]
        once = jnp.where(mp == 0, 1.0, 0.0)

        def final(c, carry):
            lanes = pl.ds(pl.multiple_of(c * 256, 256), 256)
            total = None
            for s in range(1 if r == 0 else 0, 3):
                term = lax.dot_general(
                    dqkv[pl.ds(start, 384), s * 256 : (s + 1) * 256],
                    wv[(Q, K, V)[s], c].reshape(256, 256),
                    NT,
                    preferred_element_type=F32,
                )
                total = term if total is None else total + term
            units = hv[block, :, lanes].astype(F32) * factor
            result = factor * (total * gain[:, lanes].astype(F32) - units * mean)
            if r == 2:
                result = result + cv[own_rows, lanes].astype(F32) * once
            hv[block, :, lanes] = result.astype(BF)
            return carry

        lax.fori_loop(0, 8, final, 0)
        for side in range(2):
            lanes = pl.ds(pl.multiple_of(side * 1024 + (1 - core) * 512, 512), 512)
            wires.put("trunk", s_twin[r][side], hv.at[block, :, lanes], t_twin.at[r, side], info["twin"])

    def fold_twin(r):
        for side in (0, 1):
            lanes = pl.ds(pl.multiple_of(side * 1024 + core * 512, 512), 512)
            wires.got(s_twin[r][side], t_twin.at[r, side])
            t_twin[r, side] = add(t_twin[r, side], hv[blocks[r], :, lanes])
        wires.put("trunk", s_far1[r], t_twin.at[r, 1 - hi, top], t_far1.at[r], info["far"])
        there = pl.ds(pl.multiple_of((1 - mp) * 256, 256), 256)
        wires.put("trunk", s_near1[r], t_twin.at[r, hi, low, there], t_near1.at[r, 0], info["near"])
        there = pl.ds(pl.multiple_of(mp * 256, 256), 256)
        wires.put("trunk", s_near3[r], t_twin.at[r, 1 - hi, low, there], t_near1.at[r, 1], info["near"])

    def fold_far(r):
        wires.got(s_far1[r], t_far1.at[r])
        for part in range(2):
            lanes = slice(part * 256, part * 256 + 256)
            t_mid1[r, part] = add(t_twin[r, hi, 0:192, lanes], t_far1[r, :, lanes])
        wires.put("trunk", s_near2[r], t_mid1.at[r, 1 - mp], t_near2.at[r], info["near"])

    def fold_near(r):
        wires.got(s_near3[r], t_near1.at[r, 1])
        there = pl.ds(pl.multiple_of((1 - mp) * 256, 256), 256)
        t_mid2[r, 1] = add(t_twin[r, 1 - hi, 192:384, there], t_near1[r, 1])
        wires.put("trunk", s_far2[r], t_mid2.at[r, 1], t_far2.at[r], info["far"])
        wires.got(s_near1[r], t_near1.at[r, 0])
        there = pl.ds(pl.multiple_of(mp * 256, 256), 256)
        t_mid2[r, 0] = add(t_twin[r, hi, 192:384, there], t_near1[r, 0])

    def fold_second(r):
        wires.got(s_near2[r], t_near2.at[r])
        t_fin[r, 0:192] = add(t_mid1[r, mp], t_near2[r])
        wires.got(s_far2[r], t_far2.at[r])
        t_fin[r, 192:384] = add(t_mid2[r, 0], t_far2[r])
        if r == 0:
            @pl.when(odd == 1)
            def _():
                pltpu.make_async_remote_copy(
                    src_ref=t_fin.at[0],
                    dst_ref=t_halo,
                    send_sem=send.at[len(GROUPS)],
                    recv_sem=recv.at[s_half],
                    device_id=info["e1"],
                    device_id_type=MESH,
                ).start()

        if r == 1:
            wires.put("trunk", s_e1, t_fin.at[1], t_e1, info["e1"])

    def halo_pass():
        @pl.when(odd == 0)
        def _():
            wires.got(s_half, t_halo)
            t_pass[...] = add(t_fin[0], t_halo[...])
            pltpu.make_async_remote_copy(
                src_ref=t_pass,
                dst_ref=t_halo,
                send_sem=send.at[len(GROUPS)],
                recv_sem=recv.at[s_halo],
                device_id=info["halo"],
                device_id_type=MESH,
            ).start()

    def a_step(way, step, m):
        layer = to_layer(way, 4 - step)
        on = a_got.at[way, step, m]
        if step == 1 and m != way:
            wires.put("grads", a_slot[m][way][1], grads.at[m, layer], on, info[ways[way]])
            return
        here = a_got.at[way, step - 1, m]
        wires.got(a_slot[m][way][step - 1], here)
        here[...] = add(grads[m, layer], here[...])
        wires.put("grads", a_slot[m][way][step], here, on, info[ways[way]])

    def b_start(way, left, k, m):
        wires.got(b_e2[k][m], b_e2got.at[k, m])
        return add(grads[2 + m, to_layer(way, left), pl.ds(2 * p, 2)], b_e2got[k, m])

    def b_begin(m):
        b_e2got[0, m] = b_start(m, 4, 0, m)
        wires.put("grads", b_slot[m][m][0], b_e2got.at[0, m], b_got.at[m, 0, m], info[ways[m]])

    def b_step(way, step, m):
        k = 2 * step - 1 + way
        added = b_start(way, 4 - step, k, m)
        here = b_got.at[way, step - 1, m]
        if step == 1 and m != way:
            here[...] = added
        else:
            wires.got(b_slot[m][way][step - 1], here)
            here[...] = add(added, here[...])
        wires.put("grads", b_slot[m][way][step], here, b_got.at[way, step, m], info[ways[way]])

    def a_finish(m):
        for way in range(2):
            wires.got(a_slot[m][way][3], a_got.at[way, 3, m])
        a_fin[m] = add(grads[m, z], a_got[0, 3, m], a_got[1, 3, m])
        wires.put("grads", a_e2[m], a_fin.at[m, pl.ds(2 - 2 * p, 2)], a_e2got.at[m], info["e2"])

    def swap(s, m, kind):
        wires.put("grads", r_e1[kind][m], w_pair.at[s, 1 - odd], w_res.at[q, s], info["e1"])
        w_res[q, s] = w_pair[s, odd]

    def b_finish(m):
        last = b_start(0, 0, 7, m)
        for way in range(2):
            wires.got(b_slot[m][way][3], b_got.at[way, 3, m])
        w_pair[2 + m] = add(last, b_got[0, 3, m], b_got[1, 3, m])
        swap(2 + m, m, 1)

    def a_end(m):
        wires.got(a_e2[m], a_e2got.at[m])
        w_pair[m] = add(a_fin[m, pl.ds(2 * p, 2)], a_e2got[m])
        swap(m, m, 0)

    def w_end():
        for kind in range(2):
            for m in range(2):
                wires.got(r_e1[kind][m], w_res.at[1 - q, 2 * kind + m])
        for half in range(2):
            lanes = slice(half * 256, half * 256 + 256)
            for s in range(3):
                qkv_res[0, s, :, lanes] = w_res[half, (Q, K, V)[s]]
            wo_res[0, :, lanes] = w_res[half, O]

    def t_end():
        wires.got(s_e1, t_e1)

        @pl.when(odd == 0)
        def _():
            t_res[...] = add(t_fin[2], t_e1[...])
            pltpu.make_async_copy(t_pass, t_pass, send.at[len(GROUPS)]).wait()

        @pl.when(odd == 1)
        def _():
            wires.got(s_halo, t_halo)
            t_res[...] = add(t_fin[2], t_e1[...], t_halo[...])
            pltpu.make_async_copy(t_halo, t_halo, send.at[len(GROUPS)]).wait()

    early_part(4)
    tiles_back(0, 1)
    early_part(3)
    a_step(1, 1, 0)
    tiles_back(1, 4)
    b_begin(0)
    tiles_back(4, 6)
    b_step(1, 1, 0)
    a_step(0, 1, 0)
    pack()
    late_part(4)
    b_step(0, 1, 0)
    hsettle()
    state_grads(0)
    b_begin(1)
    late_part(3)
    a_step(0, 1, 1)
    state_grads(1)
    a_step(1, 1, 1)
    fold_twin(0)
    b_step(0, 1, 1)
    early_part(2)
    a_step(0, 2, 0)
    a_step(1, 2, 0)
    fold_twin(1)
    late_part(2)
    a_step(0, 2, 1)
    a_step(1, 2, 1)
    state_grads(2)
    fold_far(0)
    b_step(1, 2, 0)
    fold_near(0)
    early_part(1)
    a_step(1, 3, 0)
    b_step(0, 2, 1)
    a_step(0, 3, 0)
    b_step(1, 1, 1)
    fold_far(1)
    late_part(1)
    fold_near(1)
    a_step(1, 3, 1)
    fold_second(0)
    a_step(0, 3, 1)
    b_step(0, 2, 0)
    late_part(0)
    fold_twin(2)
    b_step(1, 2, 1)
    early_part(0)
    b_step(0, 3, 1)
    b_step(1, 3, 0)
    fold_second(1)
    a_finish(0)
    a_finish(1)
    b_step(1, 3, 1)
    b_step(0, 3, 0)
    halo_pass()
    a_end(0)
    fold_near(2)
    fold_far(2)
    a_end(1)
    b_finish(1)
    b_finish(0)
    wsettle()
    fold_second(2)
    w_end()
    t_end()
    wires.settle("grads", nv)
    wires.settle("trunk", nv)


def hand_over(a_ref, b_ref, c_ref, a_out, b_out, c_out):
    a_out[...] = a_ref[...]
    b_out[...] = b_ref[...]
    c_out[...] = c_ref[...]


def per_device(hidden_states, norm_gain, qkv_weight, out_weight, cotangent, segment_ids):
    anywhere = pl.BlockSpec(memory_space=pl.ANY)
    in_vmem = pl.BlockSpec(memory_space=pltpu.VMEM)
    first = [
        (2, 4, 64, 256), (3, 384, 2048), (1152, 2048), (4, 8, 4, 64, 256), (768, 2048),
    ]
    wide = [(3, 384, 128), (3, 1152, 256)]
    heads = [(1152, 256), (1152, 256), (1152, 256), (768, 256)]
    later = [
        (1152, 768), (768, 256), (4, 8, 4, 64, 256),
        (2, 4, 2, 4, 64, 256), (8, 2, 2, 64, 256), (2, 4, 2, 2, 64, 256),
        (2, 4, 64, 256), (2, 2, 64, 256), (4, 2, 64, 256), (2, 4, 64, 256),
        (3, 2, 384, 512), (3, 192, 512), (3, 192, 256), (3, 2, 192, 256), (3, 192, 256),
        (3, 2, 192, 256), (3, 2, 192, 256),
        (3, 384, 256), (384, 256), (384, 256), (384, 256),
    ]

    def vmem(shapes, dtype):
        return [pltpu.VMEM(shape, dtype) for shape in shapes]

    results = pl.pallas_call(
        kernel,
        out_shape=(
            jax.ShapeDtypeStruct((384, 256), BF),
            jax.ShapeDtypeStruct((1, 3, 64, 512), BF),
            jax.ShapeDtypeStruct((1, 64, 512), BF),
        ),
        in_specs=[anywhere, in_vmem, in_vmem, anywhere, in_vmem, in_vmem],
        out_specs=(in_vmem,) * 3,
        scratch_shapes=vmem(first, BF)
        + vmem(wide, F32)
        + vmem(heads, BF)
        + vmem([(1152, 128), (1152, 128)], F32)
        + vmem([(6, 512, 512)] + later, BF)
        + [
            pltpu.SemaphoreType.DMA((len(GROUPS) + 1,)),
            pltpu.SemaphoreType.DMA((SLOTS,)),
            pltpu.SemaphoreType.DMA((2,)),
        ],
        compiler_params=pltpu.CompilerParams(
            collective_id=0, has_side_effects=True, vmem_limit_bytes=VMEM_LIMIT
        ),
        name="whole",
    )(
        hidden_states,
        jnp.transpose(qkv_weight, (0, 2, 1, 3)),
        out_weight,
        cotangent,
        norm_gain,
        segment_ids.reshape(96, 128),
    )
    trunk_grad, qkv_grad, out_grad = pl.pallas_call(
        hand_over,
        out_shape=tuple(jax.ShapeDtypeStruct(result.shape, BF) for result in results),
        in_specs=[in_vmem] * 3,
        out_specs=(in_vmem,) * 3,
        name="hand_over",
    )(*results)
    return (trunk_grad, jnp.transpose(qkv_grad, (0, 2, 1, 3)), out_grad)


def solution(mesh):
    placed = (
        P("seq", ("head", "mp")),
        P("head", None),
        P("head", "seq", None, "mp"),
        P("head", "seq", "mp"),
        P("head", "seq", None),
        P(),
    )
    return jax.shard_map(
        per_device,
        mesh=mesh,
        in_specs=placed,
        out_specs=(P("seq", ("head", "mp")), P("head", "seq", None, "mp"), P("head", "seq", "mp")),
        check_vma=False,
    )
```

```python
import math

import jax
import jax.numpy as jnp
from jax import lax
from jax.experimental import pallas as pl
from jax.experimental.pallas import tpu as pltpu
from jax.sharding import PartitionSpec as P

HD = 64
EPS = 1e-05
MASKED = -1e30
MESH = pl.DeviceIdType.MESH
VMEM_LIMIT = 60 * 1024 * 1024
BF = jnp.bfloat16
F32 = jnp.float32


def places():
    head, seq, mp = (lax.axis_index(name) for name in ("head", "seq", "mp"))
    z, x = seq // 4, seq % 4
    odd = x % 2
    info = {
        "head": head,
        "mp": mp,
        "z": z,
        "x": x,
        "odd": odd,
        "pair": x // 2,
        "quarter": ((x + 1) // 2) % 2,
        "core": head % 2,
        "hi": head // 2,
        "e1": (head, seq + 1 - 2 * odd, mp),
        "e2": (head, z * 4 + 3 - x, mp),
        "zp": (head, ((z + 1) % 8) * 4 + x, mp),
        "zm": (head, ((z + 7) % 8) * 4 + x, mp),
        "near": (head, seq, 1 - mp),
        "far": ((head + 2) % 4, seq, 1 - mp),
        "twin": (head + 1 - 2 * (head % 2), seq, mp),
        "halo": (head, (seq + 31 + 2 * odd) % 32, mp),
    }
    return info


def greet(info):
    barrier = pltpu.get_barrier_semaphore()
    names = ("e1", "e2", "zp", "zm", "near", "far", "twin", "halo")
    for name in names:
        pl.semaphore_signal(barrier, inc=1, device_id=info[name], device_id_type=MESH)
    pl.semaphore_wait(barrier, len(names))


GROUPS = ("hidden", "weights", "cotangent", "grads", "trunk")


class Wires:
    def __init__(self, send, recv):
        self.send, self.recv, self.count = send, recv, 0
        self.sent = dict.fromkeys(GROUPS, 0)

    def slot(self):
        self.count += 1
        return self.count - 1

    def put(self, group, slot, src, dst, device):
        pltpu.make_async_remote_copy(
            src_ref=src,
            dst_ref=dst,
            send_sem=self.send.at[GROUPS.index(group)],
            recv_sem=self.recv.at[slot],
            device_id=device,
            device_id_type=MESH,
        ).start()
        self.sent[group] += math.prod(src.shape)

    def got(self, slot, dst):
        pltpu.make_async_copy(dst, dst, self.recv.at[slot]).wait()

    def settle(self, group, like):
        rows, rest = divmod(self.sent[group], like.shape[1])
        assert rest == 0 and rows <= like.shape[0]
        ref = like.at[0:rows]
        pltpu.make_async_copy(ref, ref, self.send.at[GROUPS.index(group)]).wait()


NT = (((1,), (1,)), ((), ()))
TN = (((0,), (0,)), ((), ()))
COT_PARTS = 6
COT_ROWS = 192 // COT_PARTS
SLOTS = 180
Q, K, V, O = 1, 3, 0, 2


def add(*terms):
    total = terms[0].astype(F32)
    for term in terms[1:]:
        total = total + term.astype(F32)
    return total.astype(BF)


def kernel(
    hid, qkv, wo, cot, gain, seg,
    t_res, qkv_res, wo_res,
    ws, hv, nv, wv, cv, inv, acc, q_s, k_s, v_s, g_s, segk, means, probs, dqkv, attn, grads,
    a_got, b_e2got, b_got, a_fin, a_e2got, w_pair, w_res,
    t_twin, t_far1, t_far2, t_near1, t_near2, t_mid1, t_mid2, t_fin, t_e1, t_halo, t_pass,
    send, recv, local,
):
    info = places()
    z, x, odd, p, q = (info[name] for name in ("z", "x", "odd", "pair", "quarter"))
    mp, core, hi = info["mp"], info["core"], info["hi"]
    seq = z * 4 + x
    wires = Wires(send, recv)
    ways = ("zp", "zm")
    mate = x + 1 - 2 * odd
    b = 1 + odd
    order = (b, 3 - b, 0)

    def cols(block, head_hi, head_core, part):
        start = pl.multiple_of(((head_hi * 2 + head_core) * 2 + part) * 256, 256)
        return hv.at[block, :, pl.ds(start, 256)]

    own_h = pltpu.make_async_copy(hid, cols(b, hi, core, mp), local.at[0])
    own_h.start()
    own_rows = pl.ds(pl.multiple_of(odd * 384, 384), 384)
    own_c = pltpu.make_async_copy(cot.at[0], cv.at[own_rows], local.at[1])
    own_c.start()
    for half in range(2):
        lanes = slice(half * 256, half * 256 + 256)
        for s in range(3):
            ws[half, (Q, K, V)[s]] = qkv[0, s, :, lanes]
        ws[half, O] = wo[0, :, lanes]
    wv[:, z, x] = ws[q]

    greet(info)

    def slots(count):
        return [wires.slot() for _ in range(count)]

    (w_e1,) = slots(1)
    h_e1, h_halo = slots(2)
    h_near, h_far, h_opp = slots(3), slots(3), slots(3)
    h_twin = [slots(2) for _ in range(3)]
    w_z = [[slots(4) for _ in range(2)] for _ in range(2)]
    x_z = [slots(4) for _ in range(2)]
    first_e2 = slots(2)
    b_e2in = [slots(5) for _ in range(2)]
    c_e1, c_near = slots(COT_PARTS), slots(COT_PARTS)

    def one(first, count, layer, place):
        return wv.at[pl.ds(first, count), layer, pl.ds(place, 1)]

    def other_pair(first, count, layer):
        return wv.at[pl.ds(first, count), layer, pl.ds(2 - 2 * p, 2)]

    def own_pair(first, count, layer):
        return wv.at[pl.ds(first, count), layer, pl.ds(2 * p, 2)]

    def span(way, hop, count):
        return (0, count) if hop < 4 else (way * count // 2, count // 2)

    def layer_from(way, hop):
        return (z + 8 - hop) % 8 if way == 0 else (z + hop) % 8

    mine = cols(b, hi, core, mp)
    halo_own = cols(0, hi, core, mp)
    wires.put("weights", w_e1, ws.at[1 - q], wv.at[:, z, x], info["e1"])
    wires.put("hidden", h_e1, hid, mine, info["e1"])
    own_rows_w = ws.at[q]
    own_place = wv.at[:, z, x]
    for way in range(2):
        wires.put("weights", w_z[0][way][0], own_rows_w, own_place, info[ways[way]])
    wires.put("weights", first_e2[0], own_rows_w, own_place, info["e2"])

    @pl.when(odd == 1)
    def _():
        pltpu.make_async_remote_copy(
            src_ref=hid,
            dst_ref=halo_own,
            send_sem=send.at[GROUPS.index("hidden")],
            recv_sem=recv.at[h_halo],
            device_id=info["halo"],
            device_id_type=MESH,
        ).start()

    def spread(r):
        dst = cols(order[r], hi, core, mp)
        if r == 1:
            wires.got(h_e1, dst)
        src = hid if r == 0 else dst
        wires.put("hidden", h_near[r], src, dst, info["near"])
        wires.put("hidden", h_far[r], src, dst, info["far"])

    spread(0)

    def half_cols(block, head_hi, head_core):
        start = pl.multiple_of((head_hi * 2 + head_core) * 512, 512)
        return hv.at[block, :, pl.ds(start, 512)]

    def halo_on():
        wires.got(h_halo, halo_own)

        @pl.when(odd == 0)
        def _():
            pltpu.make_async_remote_copy(
                src_ref=halo_own,
                dst_ref=halo_own,
                send_sem=send.at[GROUPS.index("hidden")],
                recv_sem=recv.at[h_halo],
                device_id=info["e1"],
                device_id_type=MESH,
            ).start()

        wires.sent["hidden"] += 384 * 256

    def from_near(r):
        got = cols(order[r], hi, core, 1 - mp)
        wires.got(h_near[r], got)
        wires.put("hidden", h_opp[r], got, got, info["far"])
        if r == 0:
            own_h.wait()
        both = half_cols(order[r], hi, core)
        wires.put("hidden", h_twin[r][0], both, both, info["twin"])

    def from_far(r):
        wires.got(h_far[r], cols(order[r], 1 - hi, core, 1 - mp))
        wires.got(h_opp[r], cols(order[r], 1 - hi, core, mp))
        both = half_cols(order[r], 1 - hi, core)
        wires.put("hidden", h_twin[r][1], both, both, info["twin"])

    def from_twin(r):
        wires.got(h_twin[r][0], half_cols(order[r], hi, 1 - core))
        wires.got(h_twin[r][1], half_cols(order[r], 1 - hi, 1 - core))
        block = order[r]

        def rows_step(i, carry):
            rows = pl.ds(pl.multiple_of(i * 32, 32), 32)
            states = hv[block, rows, :].astype(F32)
            inverse = lax.rsqrt(jnp.mean(states * states, axis=1, keepdims=True) + EPS)
            there = pl.ds(pl.multiple_of(block * 384 + i * 32, 32), 32)
            nv[there, :] = (states * inverse * gain[...].astype(F32)).astype(BF)
            inv[block, rows, :] = jnp.broadcast_to(inverse, (32, 128))
            return carry

        lax.fori_loop(0, 12, rows_step, 0)

    def c_rows(block, part, k):
        start = pl.multiple_of(block * 384 + part * 192 + k * COT_ROWS, COT_ROWS)
        return cv.at[pl.ds(start, COT_ROWS)]

    def c_send(k):
        start = pl.multiple_of(mp * 192 + k * COT_ROWS, COT_ROWS)
        wires.put("cotangent", c_e1[k], cot.at[0, pl.ds(start, COT_ROWS)], c_rows(odd, mp, k), info["e1"])

    c_send(0)

    def c_on(k):
        ref = c_rows(1 - odd, mp, k)
        wires.got(c_e1[k], ref)
        wires.put("cotangent", c_near[k], ref, ref, info["near"])

    def c_got(k):
        wires.got(c_near[k], c_rows(1 - odd, 1 - mp, k))

    def second():
        ref = wv.at[:, z, mate]
        wires.got(w_e1, ref)
        wires.put("weights", first_e2[1], ref, ref, info["e2"])
        for way in range(2):
            wires.put("weights", w_z[1][way][0], ref, ref, info[ways[way]])

    def w_hop(hop, way, member):
        place = (x, mate)[member]
        layer = layer_from(way, hop)
        lo, count = span(way, hop, 4)
        wires.got(w_z[member][way][hop - 1], one(lo, count, layer, place))
        if hop < 4:
            lo, count = span(way, hop + 1, 4)
            on = one(lo, count, layer, place)
            wires.put("weights", w_z[member][way][hop], on, on, info[ways[way]])
        if member == 1 and (hop < 4 or way == 1):
            ref = own_pair(2, 2, layer)
            wires.put("weights", b_e2in[way][hop], ref, ref, info["e2"])

    def x_hop(hop, way):
        if hop == 0:
            wires.got(first_e2[0], wv.at[:, z, 3 - x])
            wires.got(first_e2[1], wv.at[:, z, 3 - mate])
            ref = other_pair(0, 2, z)
            for each in range(2):
                wires.put("weights", x_z[each][0], ref, ref, info[ways[each]])
            return
        lo, count = span(way, hop, 2)
        layer = layer_from(way, hop)
        wires.got(x_z[way][hop - 1], other_pair(lo, count, layer))
        if hop < 4:
            lo, count = span(way, hop + 1, 2)
            on = other_pair(lo, count, layer)
            wires.put("weights", x_z[way][hop], on, on, info[ways[way]])

    def e2_got(hop, way):
        wires.got(b_e2in[way][hop], other_pair(2, 2, layer_from(way, hop)))

    def project(hop, r):
        here = pl.ds(pl.multiple_of(order[r] * 384, 384), 384)

        def step(way, carry):
            layer = (z + hop + way * (8 - 2 * hop)) % 8
            lanes = pl.ds(pl.multiple_of(layer * 256, 256), 256)
            rows = nv[here, lanes]
            for s in range(1 if r == 2 else 0, 3):
                weight = wv[(Q, K, V)[s], layer].reshape(256, 256)
                term = jnp.dot(rows, weight, preferred_element_type=F32)
                if hop == 0:
                    acc[s, here] = term
                else:
                    acc[s, here] += term
            return carry

        lax.fori_loop(0, 1 if hop in (0, 4) else 2, step, 0)

    def grad_block(block):
        rows = pl.ds(pl.multiple_of(block * 384, 384), 384)
        g_s[rows] = jnp.dot(
            cv[rows], wv[O].reshape(2048, 256), preferred_element_type=F32
        ).astype(BF)

    first_row = (seq - odd) * 3 - 3

    def seg_step(i, carry):
        row = first_row + i
        values = seg[pl.ds(jnp.maximum(row, 0), 1), :].astype(F32)
        values = jnp.where(row < 0, -1.0, values)
        segk[pl.ds(pl.multiple_of(i * 128, 128), 128), :] = jnp.broadcast_to(values, (128, 128)).T
        return carry

    lax.fori_loop(0, 9, seg_step, 0)

    def extract():
        lax.fori_loop(0, 9, extract_step, 0)
        dqkv[0:384, 0:256] = jnp.zeros((384, 256), BF)
        q_s[0:384] = jnp.zeros((384, 256), BF)

    def extract_step(i, carry):
        rows = pl.ds(pl.multiple_of(i * 128, 128), 128)
        q_s[rows] = (acc[0, rows] * HD**-0.5).astype(BF)
        k_s[rows] = acc[1, rows].astype(BF)
        v_s[rows] = acc[2, rows].astype(BF)
        acc[1, rows] = jnp.zeros((128, 256), F32)
        acc[2, rows] = jnp.zeros((128, 256), F32)
        return carry

    lane_head = lax.broadcasted_iota(jnp.int32, (128, 256), 1) // HD

    def by_head(rows):
        return jnp.concatenate(
            [jnp.where(lane_head == h, rows, jnp.zeros_like(rows)) for h in range(4)], axis=0
        )

    def gather_heads(rows, weights):
        parts = []
        for pair in range(2):
            wide = lax.dot_general(
                rows[:, pair * 128 : (pair + 1) * 128],
                weights[:, pair * 256 : (pair + 1) * 256],
                TN,
                preferred_element_type=F32,
            )
            parts += [wide[0:HD, 0:128], wide[HD : 2 * HD, 128:256]]
        return jnp.concatenate(parts, axis=0).T

    key_at = lax.broadcasted_iota(jnp.int32, (512, 128), 0)
    query_at = lax.broadcasted_iota(jnp.int32, (512, 128), 1) + 384
    causal = key_at <= query_at

    def tile_rows(t):
        start = pl.multiple_of(t * 128, 128)
        return (
            pl.ds(start, 128), pl.ds(start, 512), pl.ds(pl.multiple_of(start + 384, 128), 128)
        )

    def tile_front(t, carry):
        here, window, there = tile_rows(t)
        queries = by_head(q_s[there, :])
        keys, values = k_s[window, :], v_s[window, :]
        own_seg = seg[pl.ds(first_row + 3 + t, 1), :].astype(F32)
        allowed = causal & (segk[window, :] == own_seg)
        allowed = jnp.concatenate([allowed] * 4, axis=1)
        scores = lax.dot_general(keys, queries, NT, preferred_element_type=F32)
        scores = jnp.where(allowed, scores, MASKED)
        expo = jnp.exp(scores - jnp.max(scores, axis=0, keepdims=True))
        rows = expo * (1.0 / jnp.sum(expo, axis=0, keepdims=True))
        prob_rows = rows.astype(BF)
        probs[t] = prob_rows
        attn[here, :] = gather_heads(values, prob_rows).astype(BF)
        return carry

    def tiles_front(low_tile, high_tile):
        def pair(i, carry):
            tile_front(low_tile + 2 * i, 0)
            tile_front(low_tile + 2 * i + 1, 0)
            return carry

        lax.fori_loop(0, (high_tile - low_tile) // 2, pair, 0)

    def tiles_value():
        def value_step(t, carry):
            here, window, there = tile_rows(t)
            acc[2, window] += jnp.dot(
                probs[t], by_head(g_s[here, :]), preferred_element_type=F32
            )
            return carry

        def values_three(i, carry):
            for t in range(3):
                value_step(3 * i + t, carry)
            return carry

        lax.fori_loop(0, 2, values_three, 0)

        def pack_values(i, carry):
            rows = pl.ds(pl.multiple_of(i * 128, 128), 128)
            dqkv[rows, 512:768] = acc[2, rows].astype(BF)
            return carry

        lax.fori_loop(0, 9, pack_values, 0)

    def tile_step(t, carry):
        here, window, there = tile_rows(t)
        queries, out_grads = by_head(q_s[there, :]), by_head(g_s[here, :])
        keys, values = k_s[window, :], v_s[window, :]
        rows = probs[t].astype(F32)
        prob_grad = lax.dot_general(values, out_grads, NT, preferred_element_type=F32)
        delta = jnp.sum(rows * prob_grad, axis=0, keepdims=True)
        score_grad = (rows * (prob_grad - delta)).astype(BF)
        acc[1, window] += jnp.dot(score_grad, queries, preferred_element_type=F32)
        dqkv[there, 0:256] = (gather_heads(keys, score_grad) * HD**-0.5).astype(BF)
        return carry

    def tiles_back(low_tile, high_tile):
        def pair(i, carry):
            tile_step(low_tile + 2 * i, 0)
            tile_step(low_tile + 2 * i + 1, 0)
            return carry

        pairs = (high_tile - low_tile) // 2
        lax.fori_loop(0, pairs, pair, 0)
        if high_tile - low_tile > 2 * pairs:
            lax.fori_loop(high_tile - 1, high_tile, tile_step, 0)

    def pack():
        def step(i, carry):
            rows = pl.ds(pl.multiple_of(i * 128, 128), 128)
            dqkv[rows, 256:512] = acc[1, rows].astype(BF)
            products = (
                dqkv[rows, 0:256].astype(F32) * q_s[rows].astype(F32) * HD**0.5
                + dqkv[rows, 256:512].astype(F32) * k_s[rows].astype(F32)
                + dqkv[rows, 512:768].astype(F32) * v_s[rows].astype(F32)
            )
            mean = jnp.sum(products, axis=1, keepdims=True) * (1.0 / 2048)
            means[rows] = jnp.broadcast_to(mean, (128, 128))
            return carry

        lax.fori_loop(0, 9, step, 0)

    w_hop(1, 1, 0)
    w_hop(1, 0, 0)
    second()
    from_near(0)
    w_hop(2, 0, 0)
    w_hop(2, 1, 0)
    spread(1)
    w_hop(1, 0, 1)
    w_hop(1, 1, 1)
    x_hop(0, 0)
    halo_on()
    from_near(1)
    e2_got(1, 0)
    c_send(5)
    w_hop(2, 0, 1)
    w_hop(3, 1, 0)
    from_far(0)
    c_send(1)
    spread(2)
    c_send(3)
    c_send(2)
    c_on(0)
    w_hop(2, 1, 1)
    e2_got(1, 1)
    c_send(4)
    x_hop(1, 0)
    w_hop(3, 0, 0)
    x_hop(1, 1)
    from_twin(0)
    c_on(5)
    w_hop(3, 0, 1)
    e2_got(2, 0)
    w_hop(4, 1, 0)
    project(0, 0)
    from_far(1)
    w_hop(3, 1, 1)
    project(1, 0)
    x_hop(2, 0)
    e2_got(2, 1)
    from_near(2)
    from_twin(1)
    x_hop(2, 1)
    w_hop(4, 0, 0)
    project(0, 1)
    c_got(0)
    c_on(3)
    c_on(1)
    w_hop(4, 1, 1)
    project(2, 1)
    e2_got(3, 0)
    w_hop(4, 0, 1)
    project(2, 0)
    project(1, 1)
    c_got(5)
    c_on(2)
    x_hop(3, 0)
    from_far(2)
    e2_got(3, 1)
    x_hop(3, 1)
    project(3, 0)
    project(3, 1)
    e2_got(4, 1)
    c_got(3)
    c_on(4)
    from_twin(2)
    x_hop(4, 0)
    x_hop(4, 1)
    c_got(1)
    project(4, 0)
    project(4, 1)
    project(0, 2)
    project(2, 2)
    project(4, 2)
    project(3, 2)
    c_got(2)
    project(1, 2)
    extract()
    own_c.wait()
    grad_block(odd)
    tiles_front(0, 2)
    c_got(4)
    grad_block(1 - odd)
    tiles_front(2, 4)
    tiles_front(4, 6)
    tiles_value()

    a_slot, b_slot = ([[slots(4) for _ in range(2)] for _ in range(2)] for _ in range(2))
    b_e2 = [slots(2) for _ in range(8)]
    a_e2 = slots(2)
    r_e1 = [slots(2) for _ in range(2)]
    s_twin = [slots(2) for _ in range(3)]
    s_far1, s_far2, s_near1, s_near2, s_near3 = (slots(3) for _ in range(5))
    s_e1, s_half, s_halo = slots(3)
    blocks = (0, 2 - odd, 1 + odd)
    top, low = pl.ds(0, 192), pl.ds(192, 192)

    def to_layer(way, left):
        return (z + left) % 8 if way == 0 else (z + 8 - left) % 8

    def layers(left, body):
        def step(way, carry):
            layer = (z + left + way * (8 - 2 * left)) % 8
            body(layer, pl.ds(pl.multiple_of(layer * 256, 256), 256))
            return carry

        lax.fori_loop(0, 1 if left in (0, 4) else 2, step, 0)

    def store(s, layer, value):
        grads[s, layer] = value.astype(BF).reshape(4, 64, 256)

    def qk_grads(layer, lanes):
        pair = lax.dot_general(nv[:, lanes], dqkv[:, 0:512], TN, preferred_element_type=F32)
        store(Q, layer, pair[:, 0:256])
        store(K, layer, pair[:, 256:512])

    def vo_grads(layer, lanes):
        store(
            V,
            layer,
            lax.dot_general(nv[:, lanes], dqkv[:, 512:768], TN, preferred_element_type=F32),
        )
        store(O, layer, lax.dot_general(cv[:, lanes], attn[...], TN, preferred_element_type=F32))

    def part(m, left):
        layers(left, (vo_grads, qk_grads)[m])
        if left == 4:
            wires.put("grads",
                a_slot[m][m][0],
                grads.at[m, to_layer(m, 4)],
                a_got.at[m, 0, m],
                info[ways[m]],
            )
        for way in range(1 if left in (0, 4) else 2):
            k = 0 if left == 4 else 7 - 2 * left + way
            wires.put("grads",
                b_e2[k][m],
                grads.at[2 + m, to_layer(way, left), pl.ds(2 - 2 * p, 2)],
                b_e2got.at[k, m],
                info["e2"],
            )

    def early_part(left):
        part(0, left)

    def late_part(left):
        part(1, left)

    def hsettle():
        wires.settle("hidden", nv)

    def wsettle():
        wires.settle("weights", nv)
        wires.settle("cotangent", nv)

    def state_grads(r):
        block = blocks[r]
        start = pl.multiple_of(block * 384, 384)
        factor = inv[block, :, 0:1]

        mean = means[pl.ds(start, 384), 0:1]
        once = jnp.where(mp == 0, 1.0, 0.0)

        def final(c, carry):
            lanes = pl.ds(pl.multiple_of(c * 256, 256), 256)
            total = None
            for s in range(1 if r == 0 else 0, 3):
                term = lax.dot_general(
                    dqkv[pl.ds(start, 384), s * 256 : (s + 1) * 256],
                    wv[(Q, K, V)[s], c].reshape(256, 256),
                    NT,
                    preferred_element_type=F32,
                )
                total = term if total is None else total + term
            units = hv[block, :, lanes].astype(F32) * factor
            result = factor * (total * gain[:, lanes].astype(F32) - units * mean)
            if r == 2:
                result = result + cv[own_rows, lanes].astype(F32) * once
            hv[block, :, lanes] = result.astype(BF)
            return carry

        lax.fori_loop(0, 8, final, 0)
        for side in range(2):
            lanes = pl.ds(pl.multiple_of(side * 1024 + (1 - core) * 512, 512), 512)
            wires.put("trunk", s_twin[r][side], hv.at[block, :, lanes], t_twin.at[r, side], info["twin"])

    def fold_twin(r):
        for side in (0, 1):
            lanes = pl.ds(pl.multiple_of(side * 1024 + core * 512, 512), 512)
            wires.got(s_twin[r][side], t_twin.at[r, side])
            t_twin[r, side] = add(t_twin[r, side], hv[blocks[r], :, lanes])
        wires.put("trunk", s_far1[r], t_twin.at[r, 1 - hi, top], t_far1.at[r], info["far"])
        there = pl.ds(pl.multiple_of((1 - mp) * 256, 256), 256)
        wires.put("trunk", s_near1[r], t_twin.at[r, hi, low, there], t_near1.at[r, 0], info["near"])
        there = pl.ds(pl.multiple_of(mp * 256, 256), 256)
        wires.put("trunk", s_near3[r], t_twin.at[r, 1 - hi, low, there], t_near1.at[r, 1], info["near"])

    def fold_far(r):
        wires.got(s_far1[r], t_far1.at[r])
        for part in range(2):
            lanes = slice(part * 256, part * 256 + 256)
            t_mid1[r, part] = add(t_twin[r, hi, 0:192, lanes], t_far1[r, :, lanes])
        wires.put("trunk", s_near2[r], t_mid1.at[r, 1 - mp], t_near2.at[r], info["near"])

    def fold_near(r):
        wires.got(s_near3[r], t_near1.at[r, 1])
        there = pl.ds(pl.multiple_of((1 - mp) * 256, 256), 256)
        t_mid2[r, 1] = add(t_twin[r, 1 - hi, 192:384, there], t_near1[r, 1])
        wires.put("trunk", s_far2[r], t_mid2.at[r, 1], t_far2.at[r], info["far"])
        wires.got(s_near1[r], t_near1.at[r, 0])
        there = pl.ds(pl.multiple_of(mp * 256, 256), 256)
        t_mid2[r, 0] = add(t_twin[r, hi, 192:384, there], t_near1[r, 0])

    def fold_second(r):
        wires.got(s_near2[r], t_near2.at[r])
        t_fin[r, 0:192] = add(t_mid1[r, mp], t_near2[r])
        wires.got(s_far2[r], t_far2.at[r])
        t_fin[r, 192:384] = add(t_mid2[r, 0], t_far2[r])
        if r == 0:
            @pl.when(odd == 1)
            def _():
                pltpu.make_async_remote_copy(
                    src_ref=t_fin.at[0],
                    dst_ref=t_halo,
                    send_sem=send.at[len(GROUPS)],
                    recv_sem=recv.at[s_half],
                    device_id=info["e1"],
                    device_id_type=MESH,
                ).start()

        if r == 1:
            wires.put("trunk", s_e1, t_fin.at[1], t_e1, info["e1"])

    def halo_pass():
        @pl.when(odd == 0)
        def _():
            wires.got(s_half, t_halo)
            t_pass[...] = add(t_fin[0], t_halo[...])
            pltpu.make_async_remote_copy(
                src_ref=t_pass,
                dst_ref=t_halo,
                send_sem=send.at[len(GROUPS)],
                recv_sem=recv.at[s_halo],
                device_id=info["halo"],
                device_id_type=MESH,
            ).start()

    def a_step(way, step, m):
        layer = to_layer(way, 4 - step)
        on = a_got.at[way, step, m]
        if step == 1 and m != way:
            wires.put("grads", a_slot[m][way][1], grads.at[m, layer], on, info[ways[way]])
            return
        here = a_got.at[way, step - 1, m]
        wires.got(a_slot[m][way][step - 1], here)
        here[...] = add(grads[m, layer], here[...])
        wires.put("grads", a_slot[m][way][step], here, on, info[ways[way]])

    def b_start(way, left, k, m):
        wires.got(b_e2[k][m], b_e2got.at[k, m])
        return add(grads[2 + m, to_layer(way, left), pl.ds(2 * p, 2)], b_e2got[k, m])

    def b_begin(m):
        b_e2got[0, m] = b_start(m, 4, 0, m)
        wires.put("grads", b_slot[m][m][0], b_e2got.at[0, m], b_got.at[m, 0, m], info[ways[m]])

    def b_step(way, step, m):
        k = 2 * step - 1 + way
        added = b_start(way, 4 - step, k, m)
        here = b_got.at[way, step - 1, m]
        if step == 1 and m != way:
            here[...] = added
        else:
            wires.got(b_slot[m][way][step - 1], here)
            here[...] = add(added, here[...])
        wires.put("grads", b_slot[m][way][step], here, b_got.at[way, step, m], info[ways[way]])

    def a_finish(m):
        for way in range(2):
            wires.got(a_slot[m][way][3], a_got.at[way, 3, m])
        a_fin[m] = add(grads[m, z], a_got[0, 3, m], a_got[1, 3, m])
        wires.put("grads", a_e2[m], a_fin.at[m, pl.ds(2 - 2 * p, 2)], a_e2got.at[m], info["e2"])

    def swap(s, m, kind):
        wires.put("grads", r_e1[kind][m], w_pair.at[s, 1 - odd], w_res.at[q, s], info["e1"])
        w_res[q, s] = w_pair[s, odd]

    def b_finish(m):
        last = b_start(0, 0, 7, m)
        for way in range(2):
            wires.got(b_slot[m][way][3], b_got.at[way, 3, m])
        w_pair[2 + m] = add(last, b_got[0, 3, m], b_got[1, 3, m])
        swap(2 + m, m, 1)

    def a_end(m):
        wires.got(a_e2[m], a_e2got.at[m])
        w_pair[m] = add(a_fin[m, pl.ds(2 * p, 2)], a_e2got[m])
        swap(m, m, 0)

    def w_end():
        for kind in range(2):
            for m in range(2):
                wires.got(r_e1[kind][m], w_res.at[1 - q, 2 * kind + m])
        for half in range(2):
            lanes = slice(half * 256, half * 256 + 256)
            for s in range(3):
                qkv_res[0, s, :, lanes] = w_res[half, (Q, K, V)[s]]
            wo_res[0, :, lanes] = w_res[half, O]

    def t_end():
        wires.got(s_e1, t_e1)

        @pl.when(odd == 0)
        def _():
            t_res[...] = add(t_fin[2], t_e1[...])
            pltpu.make_async_copy(t_pass, t_pass, send.at[len(GROUPS)]).wait()

        @pl.when(odd == 1)
        def _():
            wires.got(s_halo, t_halo)
            t_res[...] = add(t_fin[2], t_e1[...], t_halo[...])
            pltpu.make_async_copy(t_halo, t_halo, send.at[len(GROUPS)]).wait()

    early_part(4)
    tiles_back(0, 1)
    early_part(3)
    a_step(1, 1, 0)
    tiles_back(1, 4)
    b_begin(0)
    tiles_back(4, 6)
    b_step(1, 1, 0)
    a_step(0, 1, 0)
    pack()
    late_part(4)
    b_step(0, 1, 0)
    hsettle()
    state_grads(0)
    b_begin(1)
    late_part(3)
    a_step(0, 1, 1)
    state_grads(1)
    a_step(1, 1, 1)
    fold_twin(0)
    b_step(0, 1, 1)
    early_part(2)
    a_step(0, 2, 0)
    a_step(1, 2, 0)
    fold_twin(1)
    late_part(2)
    a_step(0, 2, 1)
    a_step(1, 2, 1)
    state_grads(2)
    fold_far(0)
    b_step(1, 2, 0)
    fold_near(0)
    early_part(1)
    a_step(1, 3, 0)
    b_step(0, 2, 1)
    a_step(0, 3, 0)
    b_step(1, 1, 1)
    fold_far(1)
    late_part(1)
    fold_near(1)
    a_step(1, 3, 1)
    fold_second(0)
    a_step(0, 3, 1)
    b_step(0, 2, 0)
    late_part(0)
    fold_twin(2)
    b_step(1, 2, 1)
    early_part(0)
    b_step(0, 3, 1)
    b_step(1, 3, 0)
    fold_second(1)
    a_finish(0)
    a_finish(1)
    b_step(1, 3, 1)
    b_step(0, 3, 0)
    halo_pass()
    a_end(0)
    fold_near(2)
    fold_far(2)
    a_end(1)
    b_finish(1)
    b_finish(0)
    wsettle()
    fold_second(2)
    w_end()
    t_end()
    wires.settle("grads", nv)
    wires.settle("trunk", nv)


def hand_over(a_ref, b_ref, c_ref, a_out, b_out, c_out):
    a_out[...] = a_ref[...]
    b_out[...] = b_ref[...]
    c_out[...] = c_ref[...]


def per_device(hidden_states, norm_gain, qkv_weight, out_weight, cotangent, segment_ids):
    anywhere = pl.BlockSpec(memory_space=pl.ANY)
    in_vmem = pl.BlockSpec(memory_space=pltpu.VMEM)
    first = [
        (2, 4, 64, 256), (3, 384, 2048), (1152, 2048), (4, 8, 4, 64, 256), (768, 2048),
    ]
    wide = [(3, 384, 128), (3, 1152, 256)]
    heads = [(1152, 256), (1152, 256), (1152, 256), (768, 256)]
    later = [
        (1152, 768), (768, 256), (4, 8, 4, 64, 256),
        (2, 4, 2, 4, 64, 256), (8, 2, 2, 64, 256), (2, 4, 2, 2, 64, 256),
        (2, 4, 64, 256), (2, 2, 64, 256), (4, 2, 64, 256), (2, 4, 64, 256),
        (3, 2, 384, 512), (3, 192, 512), (3, 192, 256), (3, 2, 192, 256), (3, 192, 256),
        (3, 2, 192, 256), (3, 2, 192, 256),
        (3, 384, 256), (384, 256), (384, 256), (384, 256),
    ]

    def vmem(shapes, dtype):
        return [pltpu.VMEM(shape, dtype) for shape in shapes]

    results = pl.pallas_call(
        kernel,
        out_shape=(
            jax.ShapeDtypeStruct((384, 256), BF),
            jax.ShapeDtypeStruct((1, 3, 64, 512), BF),
            jax.ShapeDtypeStruct((1, 64, 512), BF),
        ),
        in_specs=[anywhere, in_vmem, in_vmem, anywhere, in_vmem, in_vmem],
        out_specs=(in_vmem,) * 3,
        scratch_shapes=vmem(first, BF)
        + vmem(wide, F32)
        + vmem(heads, BF)
        + vmem([(1152, 128), (1152, 128)], F32)
        + vmem([(6, 512, 512)] + later, BF)
        + [
            pltpu.SemaphoreType.DMA((len(GROUPS) + 1,)),
            pltpu.SemaphoreType.DMA((SLOTS,)),
            pltpu.SemaphoreType.DMA((2,)),
        ],
        compiler_params=pltpu.CompilerParams(
            collective_id=0, has_side_effects=True, vmem_limit_bytes=VMEM_LIMIT
        ),
        name="whole",
    )(
        hidden_states,
        jnp.transpose(qkv_weight, (0, 2, 1, 3)),
        out_weight,
        cotangent,
        norm_gain,
        segment_ids.reshape(96, 128),
    )
    trunk_grad, qkv_grad, out_grad = pl.pallas_call(
        hand_over,
        out_shape=tuple(jax.ShapeDtypeStruct(result.shape, BF) for result in results),
        in_specs=[in_vmem] * 3,
        out_specs=(in_vmem,) * 3,
        name="hand_over",
    )(*results)
    return (trunk_grad, jnp.transpose(qkv_grad, (0, 2, 1, 3)), out_grad)


def solution(mesh):
    placed = (
        P("seq", ("head", "mp")),
        P("head", None),
        P("head", "seq", None, "mp"),
        P("head", "seq", "mp"),
        P("head", "seq", None),
        P(),
    )
    return jax.shard_map(
        per_device,
        mesh=mesh,
        in_specs=placed,
        out_specs=(P("seq", ("head", "mp")), P("head", "seq", None, "mp"), P("head", "seq", "mp")),
        check_vma=False,
    )
```
